32 devices in a mesh: photo: 4 (over y, x), tile: 8 (over z, core).
Axes of the slice: x: 2, y: 2, z: 4, core: 2. Of those that a mesh axis runs over, the one named last changes fastest.
Arguments:
- photos: bfloat16 [64, 128, 4096], P('photo', 'tile'), may hold values from 0.25 to 64, as said below
- camera_id: int32 [64], P('photo'), may hold values from 0 to 31, never falling along the last dimension, each value on 1 to 4 neighbouring positions
Outputs:
- fingerprints: float32 [32, 128, 4096], P(None, 'tile', 'photo')
- correlation: float32 [32, 32], replicated
The draws below stay inside these ranges and needn't reach their ends.
Inputs may be any that keep to these rules, and one draw needn't show every extreme that they name: `photos`: values are positive intensities. `camera_id`: photos are ordered by camera: ids never fall, every camera has 1 to 4 photos, and one has exactly 4.
All inputs are finite; a program needn't handle non-finite values.
Results may differ from the reference program's by a relative error of at most 0.0026.
Values may be sent and summed in bfloat16 or wider, within the bound.
No kernel may reach another device: no remote copies, remote signals or barrier semaphores. Data moves between devices by JAX's collectives and lax.ppermute only.
A program may use at most 192 MiB of HBM per device.

```python
import math
import jax
import jax.numpy as jnp
import numpy as np
from jax import lax

W = 4096
CAMS = 32
H = 128
PHOTOS = 64
MOST_PHOTOS = 4


def draw_photos(key, part):
    keys = jax.random.split(key, 4)
    positions = jnp.arange(H, dtype=jnp.float32) / float(max(H - 1, 1))
    ramp = jnp.exp(jnp.log(1.5) * positions)[None, :, None]
    row_texture = jnp.exp(jax.random.uniform(keys[0], (PHOTOS, H, 1), jnp.float32) * jnp.log(4.0))
    col_texture = jnp.exp(jax.random.uniform(keys[1], (PHOTOS, 1, W), jnp.float32) * jnp.log(4.0))
    shared = jax.random.uniform(keys[2], (1, H, W), jnp.float32, 0.5, 1.5)
    own_part = jax.random.uniform(keys[3], (PHOTOS, H, W), jnp.float32)
    content = shared + own_part
    values = ramp * row_texture * col_texture * content
    return values.astype(jnp.bfloat16)


def split_up(number_of, total, limit, lean):
    loads = [(1 << 20) // math.isqrt(grade ** lean) + 1 for grade in range(2, number_of + 1)]
    surplus, holding = total - limit - (number_of - 1), [1] * (number_of - 1)
    while surplus > 0:
        free = [i for i in range(number_of - 1) if holding[i] < limit]
        mass, left = sum([loads[i] for i in free]), surplus
        for i in free:
            addition = min(limit - holding[i], max(1, left * loads[i] // mass), surplus)
            holding[i] = holding[i] + addition
            surplus = surplus - addition
    return np.array([limit] + holding)


def uneven_parts(own_key, amount, total, most, slope):
    if amount == 2:
        one = jax.random.randint(own_key, (), max(1, total - most), min(most, total - 1) + 1)
        return jnp.stack([one, total - one])
    sizes = jnp.asarray(split_up(amount, total, most, slope), jnp.int32)
    couples = (amount - 1) // 2
    donor, taker = sizes[1:1 + 2 * couples:2], sizes[2:2 + 2 * couples:2]
    room = jnp.minimum(donor - 1, most - taker)
    moved = jax.random.randint(jax.random.fold_in(own_key, 1), (couples,), 0, 1 << 20) % (room + 1)
    sizes = sizes.at[1:1 + 2 * couples:2].set(donor - moved).at[2:2 + 2 * couples:2].set(taker + moved)
    return sizes[jax.random.permutation(jax.random.fold_in(own_key, 2), amount)]


def setup_inputs(seed: int = 0) -> dict:
    streams_of = jax.random.split(jax.random.key(seed), 3)
    return {
        "photos": draw_photos(jax.random.fold_in(streams_of[2], 71), 0),
        "camera_id": jnp.searchsorted(jnp.cumsum(uneven_parts(streams_of[1], CAMS, PHOTOS, MOST_PHOTOS, 2)), jnp.arange(PHOTOS), side="right").astype(jnp.int32),
    }


noise_power = 1.0
var_eps = 1e-06

def forward_haar(field):
    top_left = field[..., 0::2, 0::2]
    top_right = field[..., 0::2, 1::2]
    low_left = field[..., 1::2, 0::2]
    low_right = field[..., 1::2, 1::2]
    horiz = (top_left + top_right - low_left - low_right) * 0.5
    vertic = (top_left - top_right + low_left - low_right) * 0.5
    diagon = (top_left - top_right - low_left + low_right) * 0.5
    return jnp.stack([horiz, vertic, diagon])

def inverse_haar(bands):
    horiz, vertic, diagon = (bands[0], bands[1], bands[2])
    top_left = (horiz + vertic + diagon) * 0.5
    top_right = (horiz - vertic - diagon) * 0.5
    low_left = (vertic - horiz - diagon) * 0.5
    low_right = (diagon - horiz - vertic) * 0.5
    upper = jnp.stack([top_left, top_right], -1).reshape(top_left.shape[:-1] + (-1,))
    lower = jnp.stack([low_left, low_right], -1).reshape(low_left.shape[:-1] + (-1,))
    joined = jnp.stack([upper, lower], -2)
    return joined.reshape(upper.shape[:-2] + (-1, upper.shape[-1]))

def local_variance(padded, rows, cols):
    squares = padded * padded
    column_box = squares[..., :, 4:4 + cols]
    lowest = None
    for radius in range(1, 5):
        column_box = column_box + squares[..., :, 4 - radius:4 - radius + cols] + squares[..., :, 4 + radius:4 + radius + cols]
        row_box = column_box[..., 4:4 + rows, :]
        for offset in range(1, radius + 1):
            row_box = row_box + column_box[..., 4 - offset:4 - offset + rows, :] + column_box[..., 4 + offset:4 + offset + rows, :]
        mean_square = row_box / float((2 * radius + 1) ** 2)
        lowest = mean_square if lowest is None else jnp.minimum(lowest, mean_square)
    return lowest

def residual_of(image):
    field = image.astype(jnp.float32)
    bands = forward_haar(field)
    half_rows, half_cols = (bands.shape[1], bands.shape[2])
    padded = jnp.pad(bands, ((0, 0), (4, 4), (4, 4)))
    variance = local_variance(padded, half_rows, half_cols)
    gain = noise_power / jnp.maximum(variance, noise_power)
    return inverse_haar(bands * gain).astype(jnp.bfloat16)

def correlate(gram, totals, pixel_count):
    average = totals / pixel_count
    covar = gram / pixel_count - average[:, None] * average[None, :]
    spread = jnp.diagonal(covar) + var_eps
    return covar / jnp.sqrt(spread[:, None] * spread[None, :])

def reference(photos, camera_id):
    rows_all, width_all = (photos.shape[1], photos.shape[2])

    def accumulate(carry, item):
        weighted, energy = carry
        image, camera = item
        noise_map = residual_of(image)
        field = image.astype(jnp.float32)
        weighted = weighted.at[camera].add(noise_map.astype(jnp.float32) * field)
        energy = energy.at[camera].add(field * field)
        return ((weighted, energy), None)
    empty = jnp.zeros((CAMS, rows_all, width_all), jnp.float32)
    (weighted, energy), unused = lax.scan(accumulate, (empty, empty), (photos, camera_id))
    fingerprints = weighted / energy
    flat = fingerprints.reshape(CAMS, -1)
    gram = jnp.dot(flat, flat.T, precision=lax.Precision.HIGHEST, preferred_element_type=jnp.float32)
    totals = lax.optimization_barrier(jnp.sum(flat, axis=1))
    correlation = correlate(gram, totals, float(rows_all * width_all))
    return (fingerprints, correlation)
```

```python
import functools

import jax
import jax.numpy as jnp
import numpy as np
from jax import lax
from jax.experimental import pallas as pl
from jax.experimental.pallas import tpu as pltpu
from jax.sharding import PartitionSpec as P

CAMS = 32
RADII = 4
LANES = 128

noise_power = 1.0
var_eps = 1e-06

f32 = jnp.float32
bf16 = jnp.bfloat16


def log2(value):
    return value.bit_length() - 1


def row_permutation(photos, rows):
    size = photos * rows
    matrix = np.zeros((size, size), np.float32)
    for photo in range(photos):
        for row in range(rows):
            matrix[row * photos + photo, photo * rows + row] = 1.0
    return jnp.asarray(matrix, bf16)


def column_split():
    matrix = np.zeros((2 * LANES, 2 * LANES), np.float32)
    for cell in range(LANES):
        matrix[2 * cell, cell] = 1.0
        matrix[2 * cell + 1, LANES + cell] = 1.0
    return matrix


def box_matrices():
    source = np.arange(4 * LANES)[:, None] - LANES
    target = np.arange(2 * LANES)[None, :]
    distance = np.abs(source - target)
    return jnp.asarray(
        np.stack([(distance <= radius).astype(np.float32) for radius in range(1, RADII + 1)]), bf16
    )


def haar_rows(even0, odd0, even1, odd1):
    low0, low1 = even0 + odd0, even1 + odd1
    high0, high1 = even0 - odd0, even1 - odd1
    return (low0 - low1, high0 + high1, high0 - high1)


def halves(value):
    upper = value.astype(bf16)
    lower = (value - upper.astype(f32)).astype(bf16)
    return upper, lower


def prepare_kernel(ids, photos, perm, split, sorted_out, up_out, down_out, first_out, last_out):
    count, rows, width = photos.shape
    cells = rows // 2
    flat = photos[...].reshape(count * rows, width)
    by_row = jnp.dot(perm[...], flat, preferred_element_type=f32).astype(bf16)

    lane = lax.broadcasted_iota(jnp.int32, (2 * rows, count * rows), 1)
    sub = lax.broadcasted_iota(jnp.int32, (2 * rows, count * rows), 0)
    lane_photo = lane & (count - 1)
    lane_id = jnp.zeros_like(lane)
    for photo in range(count):
        lane_id = jnp.where(lane_photo == photo, ids[photo], lane_id)
    wanted = jnp.where(sub < rows, ids[0], ids[count - 1])
    chosen = (lane_id == wanted) & ((sub & (rows - 1)) == (lane >> log2(count)))
    edge_select = jnp.where(chosen, 1.0, 0.0).astype(bf16)

    for block in range(width // (2 * LANES)):
        cols = slice(block * 2 * LANES, (block + 1) * 2 * LANES)
        cell_cols = slice(block * LANES, (block + 1) * LANES)
        parted = jnp.dot(by_row[:, cols], split[...], preferred_element_type=f32)
        sorted_out[:, cols] = parted.astype(bf16)
        upper, lower = halves(parted * parted)
        edge = jnp.dot(edge_select, upper, preferred_element_type=f32) + jnp.dot(
            edge_select, lower, preferred_element_type=f32
        )
        first_out[:rows, cols] = edge[:rows]
        last_out[:rows, cols] = edge[rows:]
        for i in range(cells):
            if RADII <= i < cells - RADII:
                continue
            top = parted[2 * i * count : (2 * i + 1) * count]
            low = parted[(2 * i + 1) * count : (2 * i + 2) * count]
            bands = haar_rows(top[:, :LANES], top[:, LANES:], low[:, :LANES], low[:, LANES:])
            for band in range(3):
                square = (bands[band] * bands[band]).astype(bf16)
                if i < RADII:
                    start = (band * RADII + i) * count
                    up_out[start : start + count, cell_cols] = square
                if i >= cells - RADII:
                    start = (band * RADII + i - (cells - RADII)) * count
                    down_out[start : start + count, cell_cols] = square
    first_out[rows:, :] = jnp.full((8, width), ids[0].astype(f32))
    last_out[rows:, :] = jnp.full((8, width), ids[count - 1].astype(f32))


def prepare(ids, photos):
    count, rows, width = photos.shape
    step = min(width, 1024)
    size = count * rows
    halo = 3 * RADII * count
    whole = lambda i, ids: (0, 0)
    along = lambda i, ids: (0, i)
    return pl.pallas_call(
        prepare_kernel,
        grid_spec=pltpu.PrefetchScalarGridSpec(
            num_scalar_prefetch=1,
            grid=(width // step,),
            in_specs=[
                pl.BlockSpec((count, rows, step), lambda i, ids: (0, 0, i)),
                pl.BlockSpec((size, size), whole),
                pl.BlockSpec((2 * LANES, 2 * LANES), whole),
            ],
            out_specs=[
                pl.BlockSpec((size, step), along),
                pl.BlockSpec((halo, step // 2), along),
                pl.BlockSpec((halo, step // 2), along),
                pl.BlockSpec((rows + 8, step), along),
                pl.BlockSpec((rows + 8, step), along),
            ],
        ),
        out_shape=[
            jax.ShapeDtypeStruct((size, width), bf16),
            jax.ShapeDtypeStruct((halo, width // 2), bf16),
            jax.ShapeDtypeStruct((halo, width // 2), bf16),
            jax.ShapeDtypeStruct((rows + 8, width), f32),
            jax.ShapeDtypeStruct((rows + 8, width), f32),
        ],
        compiler_params=pltpu.CompilerParams(vmem_limit_bytes=24 * 2**20),
        cost_estimate=pl.CostEstimate(flops=10**9, bytes_accessed=8 * 2**20, transcendentals=0),
        name="prepare",
    )(ids, photos, row_permutation(count, rows), jnp.asarray(column_split(), bf16))


def main_kernel(
    count, rows, blocks_all,
    where, ids,
    own, own_l, own_r, above, above_l, above_r, below, below_l, below_r,
    before, after, box, merge,
    out,
    sums, least, product, square, energy,
):
    cells = rows // 2
    size = count * rows
    width = own.shape[1]
    blocks = width // (2 * LANES)
    chunk = where[0]
    left_ok = jnp.where(chunk > 0, 1.0, 0.0).astype(f32)
    right_ok = jnp.where((chunk + 1) * blocks < blocks_all, 1.0, 0.0).astype(f32)

    for block in range(-1, blocks + 1):
        if block < 0:
            mine, over, under, factor, at = own_l, above_l, below_l, left_ok, 0
        elif block == blocks:
            mine, over, under, factor, at = own_r, above_r, below_r, right_ok, 0
        else:
            mine, over, under, factor, at = own, above, below, None, block
        even = slice(2 * at * LANES, (2 * at + 1) * LANES)
        odd = slice((2 * at + 1) * LANES, (2 * at + 2) * LANES)
        cols = slice(at * LANES, (at + 1) * LANES)
        place = slice((block + 1) * LANES, (block + 2) * LANES)
        squares = [[], [], []]
        for i in range(cells):
            top = slice(2 * i * count, (2 * i + 1) * count)
            low = slice((2 * i + 1) * count, (2 * i + 2) * count)
            bands = haar_rows(
                mine[top, even].astype(f32),
                mine[top, odd].astype(f32),
                mine[low, even].astype(f32),
                mine[low, odd].astype(f32),
            )
            for band in range(3):
                squares[band].append(bands[band] * bands[band])
        for band in range(3):
            start = band * RADII * count
            outer = [
                over[start + i * count : start + (i + 1) * count, cols].astype(f32)
                for i in range(RADII)
            ]
            inner = [
                under[start + i * count : start + (i + 1) * count, cols].astype(f32)
                for i in range(RADII)
            ]
            column = outer + squares[band] + inner
            if factor is not None:
                column = [value * factor for value in column]
            for i in range(cells):
                total = column[i + RADII]
                at_row = (band * cells + i) * count
                for radius in range(1, RADII + 1):
                    total = total + (column[i + RADII - radius] + column[i + RADII + radius])
                    sums[radius - 1, at_row : at_row + count, place] = total.astype(bf16)

    for group in range(blocks // 2):
        window = slice(2 * group * LANES, (2 * group + 4) * LANES)
        for radius in range(1, RADII + 1):
            wide = jnp.dot(sums[radius - 1, :, window], box[radius - 1], preferred_element_type=f32)
            mean = wide * (1.0 / float((2 * radius + 1) ** 2))
            least[...] = mean if radius == 1 else jnp.minimum(least[...], mean)
        for half in range(2):
            block = 2 * group + half
            even = slice(2 * block * LANES, (2 * block + 1) * LANES)
            odd = slice((2 * block + 1) * LANES, (2 * block + 2) * LANES)
            lanes = slice(half * LANES, (half + 1) * LANES)
            for i in range(cells):
                top = slice(2 * i * count, (2 * i + 1) * count)
                low = slice((2 * i + 1) * count, (2 * i + 2) * count)
                pixels = (
                    own[top, even].astype(f32),
                    own[top, odd].astype(f32),
                    own[low, even].astype(f32),
                    own[low, odd].astype(f32),
                )
                bands = haar_rows(*pixels)
                shrunk = []
                for band in range(3):
                    at_row = (band * cells + i) * count
                    variance = least[at_row : at_row + count, lanes]
                    gain = 1.0 / jnp.maximum(variance, 4.0 * noise_power)
                    shrunk.append(bands[band] * (gain * noise_power))
                horiz, vertic, diagon = shrunk
                both, cross = vertic + diagon, vertic - diagon
                noise = (horiz + both, horiz - both, cross - horiz, -horiz - cross)
                for (rows_at, cols_at), pixel, part in zip(
                    ((top, even), (top, odd), (low, even), (low, odd)), pixels, noise
                ):
                    start, stop = rows_at.start, rows_at.stop
                    upper, lower = halves(part.astype(bf16).astype(f32) * pixel)
                    product[start:stop, cols_at] = upper
                    product[size + start : size + stop, cols_at] = lower
                    upper, lower = halves(pixel * pixel)
                    square[start:stop, cols_at] = upper
                    square[size + start : size + stop, cols_at] = lower

    lane = lax.broadcasted_iota(jnp.int32, (size, size), 1)
    sub = lax.broadcasted_iota(jnp.int32, (size, size), 0)
    lane_photo = lane & (count - 1)
    lane_rank = jnp.zeros_like(lane)
    slot_lane = lax.broadcasted_iota(jnp.int32, (rows, size), 1) >> log2(rows)
    slot_id = jnp.full((rows, size), -1, jnp.int32)
    rank = jnp.int32(0)
    for photo in range(count):
        if photo:
            rank = rank + jnp.where(ids[photo] != ids[photo - 1], 1, 0)
        lane_rank = jnp.where(lane_photo == photo, rank, lane_rank)
        slot_id = jnp.where(slot_lane == rank, ids[photo], slot_id)
    chosen = (lane_rank == (sub >> log2(rows))) & ((sub & (rows - 1)) == (lane >> log2(count)))
    select = jnp.where(chosen, 1.0, 0.0).astype(bf16)
    select = jnp.concatenate([select, select], axis=1)
    out[size:, :] = jnp.zeros((rows, width), bf16)
    out[size:, :size] = slot_id.astype(f32).astype(bf16)
    first_id = ids[0].astype(f32)
    last_id = ids[count - 1].astype(f32)
    for block in range(blocks):
        cols = slice(2 * block * LANES, (2 * block + 2) * LANES)
        weighted = jnp.dot(select, product[:, cols], preferred_element_type=f32)
        energy[...] = jnp.dot(select, square[:, cols], preferred_element_type=f32)
        shared = jnp.where(before[rows : rows + 1, cols] == first_id, before[:rows, cols], 0.0)
        energy[:rows, :] += shared
        shared = jnp.where(after[rows : rows + 1, cols] == last_id, after[:rows, cols], 0.0)
        tail = pl.ds(pl.multiple_of(rank * rows, rows), rows)
        energy[tail, :] += shared
        part = (weighted / jnp.maximum(energy[...], 2.0**-20)).astype(bf16)
        out[:size, cols] = jnp.dot(part, merge[...], preferred_element_type=f32).astype(bf16)


def main_part(chunk, ids, own, above, below, before, after, rows, pieces):
    size, width_all = own.shape
    count = size // rows
    width = width_all // pieces
    halo = above.shape[0]
    blocks_all = width_all // (2 * LANES)
    blocks = width // (2 * LANES)
    here = lambda i, where, ids: (0, where[0])
    left = lambda i, where, ids: (0, jnp.maximum(where[0] * blocks - 1, 0))
    right = lambda i, where, ids: (0, jnp.minimum((where[0] + 1) * blocks, blocks_all - 1))
    cell_rows = 3 * (rows // 2) * count
    halo_specs = [
        pl.BlockSpec((halo, width // 2), here),
        pl.BlockSpec((halo, LANES), left),
        pl.BlockSpec((halo, LANES), right),
    ]
    return pl.pallas_call(
        functools.partial(main_kernel, count, rows, blocks_all),
        grid_spec=pltpu.PrefetchScalarGridSpec(
            num_scalar_prefetch=2,
            grid=(1,),
            in_specs=[
                pl.BlockSpec((size, width), here),
                pl.BlockSpec((size, 2 * LANES), left),
                pl.BlockSpec((size, 2 * LANES), right),
                *halo_specs,
                *halo_specs,
                pl.BlockSpec((rows + 8, width), here),
                pl.BlockSpec((rows + 8, width), here),
                pl.BlockSpec((RADII, 4 * LANES, 2 * LANES), lambda i, where, ids: (0, 0, 0)),
                pl.BlockSpec((2 * LANES, 2 * LANES), lambda i, where, ids: (0, 0)),
            ],
            out_specs=pl.BlockSpec((size + rows, width), lambda i, where, ids: (0, 0)),
            scratch_shapes=[
                pltpu.VMEM((RADII, cell_rows, width // 2 + 2 * LANES), bf16),
                pltpu.VMEM((cell_rows, 2 * LANES), f32),
                pltpu.VMEM((2 * size, width), bf16),
                pltpu.VMEM((2 * size, width), bf16),
                pltpu.VMEM((size, 2 * LANES), f32),
            ],
        ),
        out_shape=jax.ShapeDtypeStruct((size + rows, width), bf16),
        compiler_params=pltpu.CompilerParams(vmem_limit_bytes=32 * 2**20),
        cost_estimate=pl.CostEstimate(
            flops=2 * 10**9, bytes_accessed=4 * 2**20, transcendentals=0
        ),
        name="residual",
    )(
        chunk, ids, own, own, own, above, above, above, below, below, below, before, after,
        box_matrices(), jnp.asarray(column_split().T, bf16),
    )


def assemble_kernel(rows, *refs):
    pieces = len(refs) - 3
    parts, (prints, partial, flat) = refs[:pieces], refs[pieces:]
    size = parts[0].shape[0] - rows
    width = parts[0].shape[1]
    tall = CAMS * rows
    sub = lax.broadcasted_iota(jnp.int32, (tall, size), 0)
    lane = lax.broadcasted_iota(jnp.int32, (tall, size), 1)
    same_row = (sub & (rows - 1)) == (lane & (rows - 1))
    camera = (sub >> log2(rows)).astype(f32)
    selects = []
    for part in parts:
        slot_id = part[size : size + rows, :size].astype(f32)[:1]
        selects.append(jnp.where((camera == slot_id) & same_row, 1.0, 0.0).astype(bf16))
    total = jnp.zeros((tall, 1), f32)
    for block in range(width // (2 * LANES)):
        cols = slice(block * 2 * LANES, (block + 1) * 2 * LANES)
        joined = jnp.zeros((tall, 2 * LANES), f32)
        for select, part in zip(selects, parts):
            joined = joined + jnp.dot(select, part[:size, cols], preferred_element_type=f32)
        prints[:, :, cols] = joined.reshape(CAMS, rows, 2 * LANES)
        flat[:, cols] = joined.astype(bf16)
        total = total + jnp.sum(joined, axis=1, keepdims=True)
    gram = lax.dot_general(
        flat[...], flat[...], (((1,), (1,)), ((), ())), preferred_element_type=f32
    )
    sub = lax.broadcasted_iota(jnp.int32, (tall, tall), 0)
    lane = lax.broadcasted_iota(jnp.int32, (tall, tall), 1)
    gram = jnp.where((sub & (rows - 1)) == (lane & (rows - 1)), gram, 0.0)
    gram = jnp.sum(gram.reshape(CAMS, rows, tall), axis=1)
    sub = lax.broadcasted_iota(jnp.int32, (tall, LANES), 0)
    lane = lax.broadcasted_iota(jnp.int32, (tall, LANES), 1)
    gather = jnp.where((sub >> log2(rows)) == lane, 1.0, 0.0).astype(f32)
    gram = jnp.dot(gram, gather, precision=lax.Precision.HIGHEST, preferred_element_type=f32)
    total = jnp.sum(total.reshape(CAMS, rows, 1), axis=1)
    lane = lax.broadcasted_iota(jnp.int32, (CAMS, LANES), 1)
    partial[...] = jnp.where(lane == CAMS, total, gram)


def assemble(parts, rows):
    width = parts[0].shape[1]
    return pl.pallas_call(
        functools.partial(assemble_kernel, rows),
        out_shape=[
            jax.ShapeDtypeStruct((CAMS, rows, width), f32),
            jax.ShapeDtypeStruct((CAMS, LANES), f32),
        ],
        scratch_shapes=[pltpu.VMEM((CAMS * rows, width), bf16)],
        compiler_params=pltpu.CompilerParams(vmem_limit_bytes=32 * 2**20),
        cost_estimate=pl.CostEstimate(
            flops=2 * 10**9, bytes_accessed=4 * 2**20, transcendentals=0
        ),
        name="assemble",
    )(*parts)


def correlate_kernel(pixels, *refs):
    parts, out = refs[:-1], refs[-1]
    whole = parts[0][...]
    for part in parts[1:]:
        whole = whole + part[...]
    gram = whole[:, :CAMS]
    mean = whole[:, CAMS : CAMS + 1] / pixels
    sub = lax.broadcasted_iota(jnp.int32, (CAMS, CAMS), 0)
    lane = lax.broadcasted_iota(jnp.int32, (CAMS, CAMS), 1)
    diagonal = sub == lane
    mean_row = jnp.sum(jnp.where(diagonal, mean, 0.0), axis=0, keepdims=True)
    covar = gram / pixels - mean * mean_row
    only = jnp.where(diagonal, covar, 0.0)
    spread = jnp.sum(only, axis=1, keepdims=True) + var_eps
    spread_row = jnp.sum(only, axis=0, keepdims=True) + var_eps
    out[...] = covar / jnp.sqrt(spread * spread_row)


def correlate(parts, pixels):
    return pl.pallas_call(
        functools.partial(correlate_kernel, pixels),
        out_shape=jax.ShapeDtypeStruct((CAMS, CAMS), f32),
        name="correlate",
    )(*parts)


def exchange(array, axis, distance):
    size = lax.axis_size(axis)
    return lax.ppermute(array, axis, [(i, i ^ distance) for i in range(size)])


def on_device(photos, camera_id):
    rows, width = photos.shape[1:]
    pieces, tiles = lax.axis_size("photo"), lax.axis_size("tile")
    own, up, down, first, last = prepare(camera_id, photos)
    above = lax.ppermute(down, "tile", [(i, i + 1) for i in range(tiles - 1)])
    below = lax.ppermute(up, "tile", [(i + 1, i) for i in range(tiles - 1)])
    before = lax.ppermute(last, "photo", [(i, i + 1) for i in range(pieces - 1)])
    after = lax.ppermute(first, "photo", [(i + 1, i) for i in range(pieces - 1)])
    me = lax.axis_index("photo").astype(jnp.int32)
    parts = []
    for distance in reversed(range(pieces)):
        chunk = (me ^ distance).reshape(1)
        part = main_part(chunk, camera_id, own, above, below, before, after, rows, pieces)
        parts.append(exchange(part, "photo", distance) if distance else part)
    prints, partial = assemble(parts, rows)
    total = partial
    for distance in range(1, pieces):
        total = total + exchange(partial, "photo", distance)
    sums = [total] + [exchange(total, "tile", distance) for distance in range(1, tiles)]
    return prints, correlate(sums, float(rows * tiles * width))


def solution(mesh):
    return jax.shard_map(
        on_device,
        mesh=mesh,
        in_specs=(P("photo", "tile", None), P("photo")),
        out_specs=(P(None, "tile", "photo"), P()),
        check_vma=False,
    )
```

```python
import functools

import jax
import jax.numpy as jnp
from jax import lax
from jax.experimental import pallas as pl
from jax.experimental.pallas import tpu as pltpu
from jax.sharding import PartitionSpec as P

CAMS = 32
RADII = 4
FINE = 2
LANES = 128

noise_power = 1.0
var_eps = 1e-06

f32 = jnp.float32
bf16 = jnp.bfloat16


def log2(value):
    return value.bit_length() - 1


def indicator(condition):
    return jnp.where(condition, 1.0, 0.0).astype(bf16)


def iotas(shape):
    return (
        lax.broadcasted_iota(jnp.int32, shape, len(shape) - 2),
        lax.broadcasted_iota(jnp.int32, shape, len(shape) - 1),
    )


def row_permutation(photos, rows):
    sub, lane = iotas((photos * rows, photos * rows))
    same_row = (sub >> log2(photos)) == (lane & (rows - 1))
    same_photo = (sub & (photos - 1)) == (lane >> log2(rows))
    return indicator(same_row & same_photo)


def column_split():
    sub, lane = iotas((2 * LANES, 2 * LANES))
    return indicator(sub == 2 * (lane & (LANES - 1)) + (lane >> log2(LANES)))


def column_merge():
    sub, lane = iotas((2 * LANES, 2 * LANES))
    return indicator(lane == 2 * (sub & (LANES - 1)) + (sub >> log2(LANES)))


def box_matrix(radius):
    sub, lane = iotas((4 * LANES, 2 * LANES))
    return indicator(jnp.abs(sub - LANES - lane) <= radius)


def haar_rows(even0, odd0, even1, odd1):
    low0, low1 = even0 + odd0, even1 + odd1
    high0, high1 = even0 - odd0, even1 - odd1
    return (low0 - low1, high0 + high1, high0 - high1)


def halves(value):
    upper = value.astype(bf16)
    lower = (value - upper.astype(f32)).astype(bf16)
    return upper, lower


def prepare_kernel(photos, sorted_out, up_out, down_out, buffer, arrived):
    count, rows, width = photos.shape
    cells = rows // 2
    step = width // arrived.shape[0]
    copies = []
    for part in range(width // step):
        cols = pl.ds(part * step, step)
        copies.append(
            pltpu.make_async_copy(photos.at[:, :, cols], buffer.at[:, :, cols], arrived.at[part])
        )
        copies[-1].start()
    perm = row_permutation(count, rows)
    split = column_split()
    for part in range(width // step):
        copies[part].wait()
        flat = buffer[:, :, part * step : (part + 1) * step].reshape(count * rows, step)
        by_row = jnp.dot(perm, flat, preferred_element_type=f32).astype(bf16)
        for inner in range(step // (2 * LANES)):
            block = part * (step // (2 * LANES)) + inner
            cols = slice(block * 2 * LANES, (block + 1) * 2 * LANES)
            cell_cols = slice(block * LANES, (block + 1) * LANES)
            pixels = by_row[:, inner * 2 * LANES : (inner + 1) * 2 * LANES]
            parted = jnp.dot(pixels, split, preferred_element_type=f32)
            sorted_out[:, cols] = parted.astype(bf16)
            for i in range(cells):
                if RADII <= i < cells - RADII:
                    continue
                top = parted[2 * i * count : (2 * i + 1) * count]
                low = parted[(2 * i + 1) * count : (2 * i + 2) * count]
                bands = haar_rows(top[:, :LANES], top[:, LANES:], low[:, :LANES], low[:, LANES:])
                for band in range(3):
                    square = (bands[band] * bands[band]).astype(bf16)
                    if i < RADII:
                        start = (band * RADII + i) * count
                        up_out[start : start + count, cell_cols] = square
                    if i >= cells - RADII:
                        start = (band * RADII + i - (cells - RADII)) * count
                        down_out[start : start + count, cell_cols] = square


def prepare(photos):
    count, rows, width = photos.shape
    step = min(width, 1024)
    size = count * rows
    halo = 3 * RADII * count
    vmem = pl.BlockSpec(memory_space=pltpu.VMEM)
    return pl.pallas_call(
        prepare_kernel,
        in_specs=[pl.BlockSpec(memory_space=pltpu.HBM)],
        out_specs=[vmem] * 3,
        out_shape=[
            jax.ShapeDtypeStruct((size, width), bf16),
            jax.ShapeDtypeStruct((halo, width // 2), bf16),
            jax.ShapeDtypeStruct((halo, width // 2), bf16),
        ],
        scratch_shapes=[
            pltpu.VMEM((count, rows, width), bf16),
            pltpu.SemaphoreType.DMA((width // step,)),
        ],
        compiler_params=pltpu.CompilerParams(vmem_limit_bytes=24 * 2**20),
        cost_estimate=pl.CostEstimate(flops=10**9, bytes_accessed=8 * 2**20, transcendentals=0),
        name="prepare",
    )(photos)


def energy_kernel(count, rows, me, ids, own, inverse, select_out, box_out, merge_out, *extras):
    size, width_all = own.shape
    width = width_all // len(extras)
    ranks = [jnp.int32(0)]
    for photo in range(1, count):
        ranks.append(ranks[-1] + jnp.where(ids[photo] != ids[photo - 1], 1, 0))
    last = ranks[-1]
    slots = [jnp.where(rank == 0, 0, jnp.where(rank == last, 1, rank + 1)) for rank in ranks]

    sub, lane = iotas((size, size))
    lane_photo = lane & (count - 1)
    lane_slot = jnp.zeros_like(lane)
    for photo in range(count):
        lane_slot = jnp.where(lane_photo == photo, slots[photo], lane_slot)
    in_slot = lane_slot == (sub >> log2(rows))
    same_row = (sub & (rows - 1)) == (lane >> log2(count))
    select = indicator(in_slot & same_row)
    select = jnp.concatenate([select, select], axis=1)
    select_out[...] = select
    for radius in range(1, RADII + 1):
        box_out[radius - 1] = box_matrix(radius)
    merge = column_merge()
    merge_out[...] = merge

    sub, lane = iotas((rows, width))
    slot_id = jnp.full((rows, width), -1, jnp.int32)
    for photo in range(count):
        slot_id = jnp.where((lane >> log2(rows)) == slots[photo], ids[photo], slot_id)
    notes = jnp.where(sub == 0, ids[0], jnp.where(sub == 1, ids[count - 1], slot_id))
    notes = jnp.where(sub == 3, last + 1, notes).astype(f32).astype(bf16)

    for distance, extra in enumerate(extras):
        base = (me[0] ^ distance) * width
        extra[2 * rows :, :] = notes
        for block in range(width // (2 * LANES)):
            cols = pl.ds(pl.multiple_of(base + block * 2 * LANES, 2 * LANES), 2 * LANES)
            pixel = own[:, cols].astype(f32)
            pair = jnp.concatenate(halves(pixel * pixel), axis=0)
            energy = jnp.dot(select, pair, preferred_element_type=f32)
            inverse[:, cols] = 1.0 / jnp.maximum(energy, 2.0**-20)
            edges = jnp.dot(
                energy[: 2 * rows].astype(bf16), merge, preferred_element_type=f32
            )
            extra[: 2 * rows, block * 2 * LANES : (block + 1) * 2 * LANES] = edges.astype(bf16)


def energies(me, ids, own, rows, pieces):
    size, width = own.shape
    vmem = pl.BlockSpec(memory_space=pltpu.VMEM)
    smem = pl.BlockSpec(memory_space=pltpu.SMEM)
    return pl.pallas_call(
        functools.partial(energy_kernel, size // rows, rows),
        in_specs=[smem, smem, vmem],
        out_specs=[vmem] * (4 + pieces),
        out_shape=[
            jax.ShapeDtypeStruct((size, width), f32),
            jax.ShapeDtypeStruct((size, 2 * size), bf16),
            jax.ShapeDtypeStruct((RADII, 4 * LANES, 2 * LANES), bf16),
            jax.ShapeDtypeStruct((2 * LANES, 2 * LANES), bf16),
        ]
        + [jax.ShapeDtypeStruct((3 * rows, width // pieces), bf16)] * pieces,
        compiler_params=pltpu.CompilerParams(vmem_limit_bytes=24 * 2**20),
        cost_estimate=pl.CostEstimate(flops=10**9, bytes_accessed=8 * 2**20, transcendentals=0),
        name="energies",
    )(me, ids, own)


def blend_kernel(rows, me, *refs):
    pieces = (len(refs) - 4) // 1
    extras, (select, share, most, held) = refs[:pieces], refs[pieces:]
    size = select.shape[2]
    tall = CAMS * rows
    sub, lane = iotas((tall, size))
    same_row = (sub & (rows - 1)) == (lane & (rows - 1))
    camera = (sub >> log2(rows)).astype(f32)
    highest = jnp.float32(0)
    for distance, extra in enumerate(extras):
        notes = extra[2 * rows :, :].astype(f32)
        select[distance] = indicator((camera == notes[2:3, :size]) & same_row)
        highest = jnp.maximum(highest, jnp.max(notes[3:4, :LANES]))
        held[me[0] ^ distance] = extra[...].astype(f32)
    most[0, 0] = highest.astype(jnp.int32)
    ones = jnp.ones((rows, share.shape[3]), f32)
    for device in range(pieces):
        if device == 0:
            share[me[0] ^ device, 0] = ones
        if device == pieces - 1:
            share[me[0] ^ device, 1] = ones
            continue
        late = held[device, rows : 2 * rows]
        early = held[device + 1, :rows]
        crosses = held[device, 2 * rows + 1 : 2 * rows + 2] == held[device + 1, 2 * rows : 2 * rows + 1]
        joint = 1.0 / (late + early)
        share[me[0] ^ device, 1] = jnp.where(crosses, late * joint, 1.0)
        share[me[0] ^ (device + 1), 0] = jnp.where(crosses, early * joint, 1.0)


def blend(me, extras, rows, size):
    pieces, width = len(extras), extras[0].shape[1]
    vmem = pl.BlockSpec(memory_space=pltpu.VMEM)
    smem = pl.BlockSpec(memory_space=pltpu.SMEM)
    return pl.pallas_call(
        functools.partial(blend_kernel, rows),
        in_specs=[smem] + [vmem] * pieces,
        out_specs=[vmem, vmem, smem],
        out_shape=[
            jax.ShapeDtypeStruct((pieces, CAMS * rows, size), bf16),
            jax.ShapeDtypeStruct((pieces, 2, rows, width), f32),
            jax.ShapeDtypeStruct((1, 1), jnp.int32),
        ],
        scratch_shapes=[pltpu.VMEM((pieces, 3 * rows, width), f32)],
        compiler_params=pltpu.CompilerParams(vmem_limit_bytes=24 * 2**20),
        name="blend",
    )(me, *extras)


def main_kernel(
    count, rows, blocks_all,
    where,
    own, own_l, own_r, above, above_l, above_r, below, below_l, below_r,
    inverse, select, box, merge,
    out,
    sums, rest, least, product,
):
    cells = rows // 2
    size = count * rows
    width = own.shape[1]
    blocks = width // (2 * LANES)
    chunk = where[0]
    left_ok = jnp.where(chunk > 0, 1.0, 0.0).astype(f32)
    right_ok = jnp.where((chunk + 1) * blocks < blocks_all, 1.0, 0.0).astype(f32)

    for block in range(-1, blocks + 1):
        if block < 0:
            mine, over, under, factor, at = own_l, above_l, below_l, left_ok, 0
        elif block == blocks:
            mine, over, under, factor, at = own_r, above_r, below_r, right_ok, 0
        else:
            mine, over, under, factor, at = own, above, below, None, block
        even = slice(2 * at * LANES, (2 * at + 1) * LANES)
        odd = slice((2 * at + 1) * LANES, (2 * at + 2) * LANES)
        cols = slice(at * LANES, (at + 1) * LANES)
        place = slice((block + 1) * LANES, (block + 2) * LANES)
        squares = [[], [], []]
        for i in range(cells):
            top = slice(2 * i * count, (2 * i + 1) * count)
            low = slice((2 * i + 1) * count, (2 * i + 2) * count)
            bands = haar_rows(
                mine[top, even].astype(f32),
                mine[top, odd].astype(f32),
                mine[low, even].astype(f32),
                mine[low, odd].astype(f32),
            )
            for band in range(3):
                squares[band].append(bands[band] * bands[band])
        for band in range(3):
            start = band * RADII * count
            outer = [
                over[start + i * count : start + (i + 1) * count, cols].astype(f32)
                for i in range(RADII)
            ]
            inner = [
                under[start + i * count : start + (i + 1) * count, cols].astype(f32)
                for i in range(RADII)
            ]
            column = outer + squares[band] + inner
            if factor is not None:
                column = [value * factor for value in column]
            for i in range(cells):
                total = column[i + RADII]
                at_row = (band * cells + i) * count
                for radius in range(1, RADII + 1):
                    total = total + (column[i + RADII - radius] + column[i + RADII + radius])
                    upper = total.astype(bf16)
                    sums[radius - 1, at_row : at_row + count, place] = upper
                    if radius <= FINE and factor is None:
                        lower = (total - upper.astype(f32)).astype(bf16)
                        rest[radius - 1, at_row : at_row + count, cols] = lower

    for group in range(blocks // 2):
        window = slice(2 * group * LANES, (2 * group + 4) * LANES)
        for radius in range(1, RADII + 1):
            narrow, weights = sums[radius - 1, :, window], box[radius - 1]
            if radius <= FINE:
                middle = slice(2 * group * LANES, (2 * group + 2) * LANES)
                narrow = jnp.concatenate([narrow, rest[radius - 1, :, middle]], axis=1)
                weights = jnp.concatenate([weights, weights[LANES : 3 * LANES]], axis=0)
            wide = jnp.dot(narrow, weights, preferred_element_type=f32)
            mean = wide * (1.0 / float((2 * radius + 1) ** 2))
            least[...] = mean if radius == 1 else jnp.minimum(least[...], mean)
        for half in range(2):
            block = 2 * group + half
            even = slice(2 * block * LANES, (2 * block + 1) * LANES)
            odd = slice((2 * block + 1) * LANES, (2 * block + 2) * LANES)
            lanes = slice(half * LANES, (half + 1) * LANES)
            for i in range(cells):
                top = slice(2 * i * count, (2 * i + 1) * count)
                low = slice((2 * i + 1) * count, (2 * i + 2) * count)
                pixels = (
                    own[top, even].astype(f32),
                    own[top, odd].astype(f32),
                    own[low, even].astype(f32),
                    own[low, odd].astype(f32),
                )
                bands = haar_rows(*pixels)
                shrunk = []
                for band in range(3):
                    at_row = (band * cells + i) * count
                    variance = least[at_row : at_row + count, lanes]
                    gain = 1.0 / jnp.maximum(variance, 4.0 * noise_power)
                    shrunk.append(bands[band] * (gain * noise_power))
                horiz, vertic, diagon = shrunk
                both, cross = vertic + diagon, vertic - diagon
                noise = (horiz + both, horiz - both, cross - horiz, -horiz - cross)
                for (rows_at, cols_at), pixel, part in zip(
                    ((top, even), (top, odd), (low, even), (low, odd)), pixels, noise
                ):
                    start, stop = rows_at.start, rows_at.stop
                    upper, lower = halves(part.astype(bf16).astype(f32) * pixel)
                    product[start:stop, cols_at] = upper
                    product[size + start : size + stop, cols_at] = lower

    for block in range(blocks):
        cols = slice(2 * block * LANES, (2 * block + 2) * LANES)
        weighted = jnp.dot(select[...], product[:, cols], preferred_element_type=f32)
        part = (weighted * inverse[:, cols]).astype(bf16)
        out[:, cols] = jnp.dot(part, merge[...], preferred_element_type=f32).astype(bf16)


def main_part(chunk, own, above, below, inverse, select, box, merge, rows, pieces, slots):
    size, width_all = own.shape
    count = size // rows
    width = width_all // pieces
    halo = above.shape[0]
    blocks_all = width_all // (2 * LANES)
    blocks = width // (2 * LANES)
    here = lambda i, where: (0, where[0])
    left = lambda i, where: (0, jnp.maximum(where[0] * blocks - 1, 0))
    right = lambda i, where: (0, jnp.minimum((where[0] + 1) * blocks, blocks_all - 1))
    cell_rows = 3 * (rows // 2) * count
    halo_specs = [
        pl.BlockSpec((halo, width // 2), here),
        pl.BlockSpec((halo, LANES), left),
        pl.BlockSpec((halo, LANES), right),
    ]
    return pl.pallas_call(
        functools.partial(main_kernel, count, rows, blocks_all),
        grid_spec=pltpu.PrefetchScalarGridSpec(
            num_scalar_prefetch=1,
            grid=(1,),
            in_specs=[
                pl.BlockSpec((size, width), here),
                pl.BlockSpec((size, 2 * LANES), left),
                pl.BlockSpec((size, 2 * LANES), right),
                *halo_specs,
                *halo_specs,
                pl.BlockSpec((slots * rows, width), here),
                pl.BlockSpec((slots * rows, 2 * size), lambda i, where: (0, 0)),
                pl.BlockSpec((RADII, 4 * LANES, 2 * LANES), lambda i, where: (0, 0, 0)),
                pl.BlockSpec((2 * LANES, 2 * LANES), lambda i, where: (0, 0)),
            ],
            out_specs=pl.BlockSpec((slots * rows, width), lambda i, where: (0, 0)),
            scratch_shapes=[
                pltpu.VMEM((RADII, cell_rows, width // 2 + 2 * LANES), bf16),
                pltpu.VMEM((FINE, cell_rows, width // 2), bf16),
                pltpu.VMEM((cell_rows, 2 * LANES), f32),
                pltpu.VMEM((2 * size, width), bf16),
            ],
        ),
        out_shape=jax.ShapeDtypeStruct((slots * rows, width), bf16),
        compiler_params=pltpu.CompilerParams(vmem_limit_bytes=32 * 2**20),
        cost_estimate=pl.CostEstimate(
            flops=2 * 10**9, bytes_accessed=4 * 2**20, transcendentals=0
        ),
        name="residual",
    )(
        chunk, own, own, own, above, above, above, below, below, below, inverse, select, box, merge,
    )


def assemble_kernel(rows, select, share, *refs):
    pieces = len(refs) - 4
    parts, (prints, partial, flat, scaled) = refs[:pieces], refs[pieces:]
    size, width = parts[0].shape
    tall = CAMS * rows
    for place, part in enumerate(parts):
        edges = part[: 2 * rows, :].astype(f32) * share[place].reshape(2 * rows, width)
        scaled[place, : 2 * rows, :] = edges.astype(bf16)
    total = jnp.zeros((tall, 1), f32)
    for block in range(width // (2 * LANES)):
        cols = slice(block * 2 * LANES, (block + 1) * 2 * LANES)
        joined = jnp.zeros((tall, 2 * LANES), f32)
        for place, part in enumerate(parts):
            source = jnp.concatenate([scaled[place, :, cols], part[2 * rows :, cols]], axis=0)
            joined = joined + jnp.dot(
                select[place, :, :size], source, preferred_element_type=f32
            )
        prints[:, :, cols] = joined.reshape(CAMS, rows, 2 * LANES)
        flat[:, cols] = joined.astype(bf16)
        total = total + jnp.sum(joined, axis=1, keepdims=True)
    gram = lax.dot_general(
        flat[...], flat[...], (((1,), (1,)), ((), ())), preferred_element_type=f32
    )
    sub = lax.broadcasted_iota(jnp.int32, (tall, tall), 0)
    lane = lax.broadcasted_iota(jnp.int32, (tall, tall), 1)
    gram = jnp.where((sub & (rows - 1)) == (lane & (rows - 1)), gram, 0.0)
    gram = jnp.sum(gram.reshape(CAMS, rows, tall), axis=1)
    sub = lax.broadcasted_iota(jnp.int32, (tall, LANES), 0)
    lane = lax.broadcasted_iota(jnp.int32, (tall, LANES), 1)
    gather = jnp.where((sub >> log2(rows)) == lane, 1.0, 0.0).astype(f32)
    gram = jnp.dot(gram, gather, precision=lax.Precision.HIGHEST, preferred_element_type=f32)
    total = jnp.sum(total.reshape(CAMS, rows, 1), axis=1)
    lane = lax.broadcasted_iota(jnp.int32, (CAMS, LANES), 1)
    partial[...] = jnp.where(lane == CAMS, total, gram)


def assemble(select, share, parts, rows):
    width = parts[0].shape[1]
    return pl.pallas_call(
        functools.partial(assemble_kernel, rows),
        out_shape=[
            jax.ShapeDtypeStruct((CAMS, rows, width), f32),
            jax.ShapeDtypeStruct((CAMS, LANES), f32),
        ],
        scratch_shapes=[
            pltpu.VMEM((CAMS * rows, width), bf16),
            pltpu.VMEM((len(parts), 2 * rows, width), bf16),
        ],
        compiler_params=pltpu.CompilerParams(vmem_limit_bytes=32 * 2**20),
        cost_estimate=pl.CostEstimate(
            flops=2 * 10**9, bytes_accessed=4 * 2**20, transcendentals=0
        ),
        name="assemble",
    )(select, share, *parts)


def correlate_kernel(pixels, *refs):
    parts, out = refs[:-1], refs[-1]
    whole = parts[0][...]
    for part in parts[1:]:
        whole = whole + part[...]
    gram = whole[:, :CAMS]
    mean = whole[:, CAMS : CAMS + 1] / pixels
    sub = lax.broadcasted_iota(jnp.int32, (CAMS, CAMS), 0)
    lane = lax.broadcasted_iota(jnp.int32, (CAMS, CAMS), 1)
    diagonal = sub == lane
    mean_row = jnp.sum(jnp.where(diagonal, mean, 0.0), axis=0, keepdims=True)
    covar = gram / pixels - mean * mean_row
    only = jnp.where(diagonal, covar, 0.0)
    spread = jnp.sum(only, axis=1, keepdims=True) + var_eps
    spread_row = jnp.sum(only, axis=0, keepdims=True) + var_eps
    out[...] = covar / jnp.sqrt(spread * spread_row)


def correlate(parts, pixels):
    return pl.pallas_call(
        functools.partial(correlate_kernel, pixels),
        out_shape=jax.ShapeDtypeStruct((CAMS, CAMS), f32),
        name="correlate",
    )(*parts)


def exchange(array, axis, distance):
    size = lax.axis_size(axis)
    return lax.ppermute(array, axis, [(i, i ^ distance) for i in range(size)])


def gathered(array, axis):
    size = lax.axis_size(axis)
    return lax.all_to_all(
        jnp.broadcast_to(array, (size,) + array.shape), axis, split_axis=0, concat_axis=0
    )


def on_device(photos, camera_id):
    count, rows, width = photos.shape
    pieces, tiles = lax.axis_size("photo"), lax.axis_size("tile")
    me = lax.axis_index("photo").astype(jnp.int32)
    own, up, down = prepare(photos)
    above = lax.ppermute(down, "tile", [(i, i + 1) for i in range(tiles - 1)])
    below = lax.ppermute(up, "tile", [(i + 1, i) for i in range(tiles - 1)])
    inverse, select, box, merge, *extras = energies(
        me.reshape(1), camera_id, own, rows, pieces
    )
    extras = [
        exchange(extra, "photo", distance) if distance else extra
        for distance, extra in enumerate(extras)
    ]
    place, share, most = blend(me.reshape(1), extras, rows, count * rows)

    def finish(slots):
        parts = [None] * pieces
        for distance in reversed(range(pieces)):
            part = main_part(
                (me ^ distance).reshape(1), own, above, below, inverse, select, box, merge,
                rows, pieces, slots,
            )
            parts[distance] = exchange(part, "photo", distance) if distance else part
        return assemble(place, share, parts, rows)

    few = max(2, 3 * count // 4)
    prints, partial = lax.cond(
        most[0, 0] > few, lambda: finish(count), lambda: finish(few)
    )
    total = jnp.sum(gathered(partial, "photo"), axis=0)
    sums = gathered(total, "tile")
    return prints, correlate([sums[i] for i in range(tiles)], float(rows * tiles * width))


def solution(mesh):
    return jax.shard_map(
        on_device,
        mesh=mesh,
        in_specs=(P("photo", "tile", None), P("photo")),
        out_specs=(P(None, "tile", "photo"), P()),
        check_vma=False,
    )
```

```python
import functools

import jax
import jax.numpy as jnp
from jax import lax
from jax.experimental import pallas as pl
from jax.experimental.pallas import tpu as pltpu
from jax.sharding import PartitionSpec as P

CAMS = 32
RADII = 4
FINE = 2
LANES = 128

noise_power = 1.0
var_eps = 1e-06

f32 = jnp.float32
bf16 = jnp.bfloat16


def log2(value):
    return value.bit_length() - 1


def indicator(condition):
    return jnp.where(condition, 1.0, 0.0).astype(bf16)


def iotas(shape):
    return (
        lax.broadcasted_iota(jnp.int32, shape, len(shape) - 2),
        lax.broadcasted_iota(jnp.int32, shape, len(shape) - 1),
    )


def row_permutation(photos, rows):
    sub, lane = iotas((photos * rows, photos * rows))
    same_row = (sub >> log2(photos)) == (lane & (rows - 1))
    same_photo = (sub & (photos - 1)) == (lane >> log2(rows))
    return indicator(same_row & same_photo)


def column_split():
    sub, lane = iotas((2 * LANES, 2 * LANES))
    return indicator(sub == 2 * (lane & (LANES - 1)) + (lane >> log2(LANES)))


def column_merge():
    sub, lane = iotas((2 * LANES, 2 * LANES))
    return indicator(lane == 2 * (sub & (LANES - 1)) + (sub >> log2(LANES)))


def box_matrix(radius):
    sub, lane = iotas((4 * LANES, 2 * LANES))
    return indicator(jnp.abs(sub - LANES - lane) <= radius)


def haar_rows(even0, odd0, even1, odd1):
    low0, low1 = even0 + odd0, even1 + odd1
    high0, high1 = even0 - odd0, even1 - odd1
    return (low0 - low1, high0 + high1, high0 - high1)


def halves(value):
    upper = value.astype(bf16)
    lower = (value - upper.astype(f32)).astype(bf16)
    return upper, lower


def slot_numbers(ids, count):
    ranks = [jnp.int32(0)]
    for photo in range(1, count):
        ranks.append(ranks[-1] + jnp.where(ids[photo] != ids[photo - 1], 1, 0))
    last = ranks[-1]
    slots = [jnp.where(rank == 0, 0, jnp.where(rank == last, 1, rank + 1)) for rank in ranks]
    return slots, last + 1


def prepare_kernel(me, ids, photos, sorted_out, up_out, down_out, *refs):
    extras, (buffer, arrived) = refs[:-2], refs[-2:]
    count, rows, width = photos.shape
    cells = rows // 2
    pieces = len(extras)
    step = width // pieces
    bases = [pl.multiple_of((me[0] ^ distance) * step, step) for distance in range(pieces)]
    copies = []
    for distance in range(pieces):
        cols = pl.ds(bases[distance], step)
        copies.append(
            pltpu.make_async_copy(
                photos.at[:, :, cols], buffer.at[distance], arrived.at[distance]
            )
        )
        copies[-1].start()
    perm = row_permutation(count, rows)
    split = column_split()

    slots, cameras = slot_numbers(ids, count)
    sub, lane = iotas((rows, step))
    slot_id = jnp.full((rows, step), -1, jnp.int32)
    in_first, in_last = jnp.int32(0), jnp.int32(0)
    for photo in range(count):
        slot_id = jnp.where((lane >> log2(rows)) == slots[photo], ids[photo], slot_id)
        in_first = in_first + jnp.where(ids[photo] == ids[0], 1, 0)
        in_last = in_last + jnp.where(ids[photo] == ids[count - 1], 1, 0)
    notes = jnp.where(sub == 0, ids[0], jnp.where(sub == 1, ids[count - 1], slot_id))
    notes = jnp.where(sub == 3, cameras, notes).astype(f32).astype(bf16)

    for distance in range(pieces):
        copies[distance].wait()
        flat = buffer[distance].reshape(count * rows, step)
        by_row = jnp.dot(perm, flat, preferred_element_type=f32).astype(bf16)
        for inner in range(step // (2 * LANES)):
            at = inner * 2 * LANES
            cols = pl.ds(pl.multiple_of(bases[distance] + at, 2 * LANES), 2 * LANES)
            cell_cols = pl.ds(
                pl.multiple_of((me[0] ^ distance) * (step // 2) + at // 2, LANES), LANES
            )
            parted = jnp.dot(by_row[:, at : at + 2 * LANES], split, preferred_element_type=f32)
            sorted_out[:, cols] = parted.astype(bf16)
            for i in range(cells):
                if RADII <= i < cells - RADII:
                    continue
                top = parted[2 * i * count : (2 * i + 1) * count]
                low = parted[(2 * i + 1) * count : (2 * i + 2) * count]
                bands = haar_rows(top[:, :LANES], top[:, LANES:], low[:, :LANES], low[:, LANES:])
                for band in range(3):
                    square = (bands[band] * bands[band]).astype(bf16)
                    if i < RADII:
                        start = (band * RADII + i) * count
                        up_out[start : start + count, cell_cols] = square
                    if i >= cells - RADII:
                        start = (band * RADII + i - (cells - RADII)) * count
                        down_out[start : start + count, cell_cols] = square

        def add(photo, total):
            pixel = buffer[distance, photo].astype(f32)
            return total + pixel * pixel

        none = jnp.zeros((rows, step), f32)
        extra = extras[distance]
        extra[:rows, :] = lax.fori_loop(0, in_first, add, none).astype(bf16)
        extra[rows : 2 * rows, :] = lax.fori_loop(count - in_last, count, add, none).astype(bf16)
        extra[2 * rows :, :] = notes


def prepare(me, ids, photos, pieces):
    count, rows, width = photos.shape
    step = width // pieces
    size = count * rows
    halo = 3 * RADII * count
    vmem = pl.BlockSpec(memory_space=pltpu.VMEM)
    smem = pl.BlockSpec(memory_space=pltpu.SMEM)
    return pl.pallas_call(
        prepare_kernel,
        in_specs=[smem, smem, pl.BlockSpec(memory_space=pltpu.HBM)],
        out_specs=[vmem] * (3 + pieces),
        out_shape=[
            jax.ShapeDtypeStruct((size, width), bf16),
            jax.ShapeDtypeStruct((halo, width // 2), bf16),
            jax.ShapeDtypeStruct((halo, width // 2), bf16),
        ]
        + [jax.ShapeDtypeStruct((3 * rows, step), bf16)] * pieces,
        scratch_shapes=[
            pltpu.VMEM((pieces, count, rows, step), bf16),
            pltpu.SemaphoreType.DMA((pieces,)),
        ],
        compiler_params=pltpu.CompilerParams(vmem_limit_bytes=20 * 2**20),
        cost_estimate=pl.CostEstimate(flops=10**9, bytes_accessed=8 * 2**20, transcendentals=0),
        name="prepare",
    )(me, ids, photos)


def energy_kernel(count, rows, ids, own, inverse, select_out, box_out, merge_out):
    size, width = own.shape
    slots, _ = slot_numbers(ids, count)
    sub, lane = iotas((size, size))
    lane_photo = lane & (count - 1)
    lane_slot = jnp.zeros_like(lane)
    for photo in range(count):
        lane_slot = jnp.where(lane_photo == photo, slots[photo], lane_slot)
    in_slot = lane_slot == (sub >> log2(rows))
    same_row = (sub & (rows - 1)) == (lane >> log2(count))
    select = indicator(in_slot & same_row)
    select = jnp.concatenate([select, select], axis=1)
    select_out[...] = select
    for radius in range(1, RADII + 1):
        box_out[radius - 1] = box_matrix(radius)
    merge_out[...] = column_merge()
    for block in range(width // (2 * LANES)):
        cols = slice(block * 2 * LANES, (block + 1) * 2 * LANES)
        pixel = own[:, cols].astype(f32)
        pair = jnp.concatenate(halves(pixel * pixel), axis=0)
        energy = jnp.dot(select, pair, preferred_element_type=f32)
        inverse[:, cols] = 1.0 / jnp.maximum(energy, 2.0**-20)


def energies(ids, own, rows):
    size, width = own.shape
    vmem = pl.BlockSpec(memory_space=pltpu.VMEM)
    smem = pl.BlockSpec(memory_space=pltpu.SMEM)
    return pl.pallas_call(
        functools.partial(energy_kernel, size // rows, rows),
        in_specs=[smem, vmem],
        out_specs=[vmem] * 4,
        out_shape=[
            jax.ShapeDtypeStruct((size, width), f32),
            jax.ShapeDtypeStruct((size, 2 * size), bf16),
            jax.ShapeDtypeStruct((RADII, 4 * LANES, 2 * LANES), bf16),
            jax.ShapeDtypeStruct((2 * LANES, 2 * LANES), bf16),
        ],
        compiler_params=pltpu.CompilerParams(vmem_limit_bytes=20 * 2**20),
        cost_estimate=pl.CostEstimate(flops=10**9, bytes_accessed=8 * 2**20, transcendentals=0),
        name="energies",
    )(ids, own)


def blend_kernel(rows, me, *refs):
    pieces = len(refs) - 4
    extras, (select, share, most, held) = refs[:pieces], refs[pieces:]
    size = select.shape[2]
    tall = CAMS * rows
    sub, lane = iotas((tall, size))
    same_row = (sub & (rows - 1)) == (lane & (rows - 1))
    camera = (sub >> log2(rows)).astype(f32)
    highest = jnp.float32(0)
    for distance, extra in enumerate(extras):
        notes = extra[2 * rows :, :].astype(f32)
        select[distance] = indicator((camera == notes[2:3, :size]) & same_row)
        highest = jnp.maximum(highest, jnp.max(notes[3:4, :LANES]))
        held[me[0] ^ distance] = extra[...].astype(f32)
    most[0, 0] = highest.astype(jnp.int32)
    ones = jnp.ones((rows, share.shape[3]), f32)
    for device in range(pieces):
        if device == 0:
            share[me[0] ^ device, 0] = ones
        if device == pieces - 1:
            share[me[0] ^ device, 1] = ones
            continue
        late = held[device, rows : 2 * rows]
        early = held[device + 1, :rows]
        crosses = held[device, 2 * rows + 1 : 2 * rows + 2] == held[device + 1, 2 * rows : 2 * rows + 1]
        joint = 1.0 / (late + early)
        share[me[0] ^ device, 1] = jnp.where(crosses, late * joint, 1.0)
        share[me[0] ^ (device + 1), 0] = jnp.where(crosses, early * joint, 1.0)


def blend(me, extras, rows, size):
    pieces, width = len(extras), extras[0].shape[1]
    vmem = pl.BlockSpec(memory_space=pltpu.VMEM)
    smem = pl.BlockSpec(memory_space=pltpu.SMEM)
    return pl.pallas_call(
        functools.partial(blend_kernel, rows),
        in_specs=[smem] + [vmem] * pieces,
        out_specs=[vmem, vmem, smem],
        out_shape=[
            jax.ShapeDtypeStruct((pieces, CAMS * rows, size), bf16),
            jax.ShapeDtypeStruct((pieces, 2, rows, width), f32),
            jax.ShapeDtypeStruct((1, 1), jnp.int32),
        ],
        scratch_shapes=[pltpu.VMEM((pieces, 3 * rows, width), f32)],
        compiler_params=pltpu.CompilerParams(vmem_limit_bytes=20 * 2**20),
        name="blend",
    )(me, *extras)


def main_kernel(
    count, rows, width, where, own, above, below, inverse, select, box, merge, out,
    sums, rest, least, product,
):
    cells = rows // 2
    size = count * rows
    width_all = own.shape[1]
    blocks = width // (2 * LANES)
    slot_rows = out.shape[0]
    base = where[0] * width
    left_ok = jnp.where(base > 0, 1.0, 0.0).astype(f32)
    right_ok = jnp.where(base + width < width_all, 1.0, 0.0).astype(f32)

    def pixels_of(i, start):
        top = slice(2 * i * count, (2 * i + 1) * count)
        low = slice((2 * i + 1) * count, (2 * i + 2) * count)
        even = pl.ds(pl.multiple_of(start, 2 * LANES), LANES)
        odd = pl.ds(pl.multiple_of(start + LANES, LANES), LANES)
        return tuple(
            own[at, cols].astype(f32)
            for at, cols in ((top, even), (top, odd), (low, even), (low, odd))
        )

    for block in range(-1, blocks + 1):
        start = base + block * 2 * LANES
        factor = None
        if block < 0:
            start, factor = jnp.maximum(start, 0), left_ok
        elif block == blocks:
            start, factor = jnp.minimum(start, width_all - 2 * LANES), right_ok
        place = slice((block + 1) * LANES, (block + 2) * LANES)
        cols = slice(block * LANES, (block + 1) * LANES)
        cell_cols = pl.ds(pl.multiple_of(lax.shift_right_arithmetic(start, 1), LANES), LANES)
        squares = [[], [], []]
        for i in range(cells):
            bands = haar_rows(*pixels_of(i, start))
            for band in range(3):
                squares[band].append(bands[band] * bands[band])
        for band in range(3):
            first = band * RADII * count
            outer, inner = (
                [
                    halo[first + i * count : first + (i + 1) * count, cell_cols].astype(f32)
                    for i in range(RADII)
                ]
                for halo in (above, below)
            )
            column = outer + squares[band] + inner
            if factor is not None:
                column = [value * factor for value in column]
            for i in range(cells):
                total = column[i + RADII]
                at_row = (band * cells + i) * count
                for radius in range(1, RADII + 1):
                    total = total + (column[i + RADII - radius] + column[i + RADII + radius])
                    upper = total.astype(bf16)
                    sums[radius - 1, at_row : at_row + count, place] = upper
                    if radius <= FINE and factor is None:
                        lower = (total - upper.astype(f32)).astype(bf16)
                        rest[radius - 1, at_row : at_row + count, cols] = lower

    for group in range(blocks // 2):
        window = slice(2 * group * LANES, (2 * group + 4) * LANES)
        for radius in range(1, RADII + 1):
            narrow, weights = sums[radius - 1, :, window], box[radius - 1]
            if radius <= FINE:
                middle = slice(2 * group * LANES, (2 * group + 2) * LANES)
                narrow = jnp.concatenate([narrow, rest[radius - 1, :, middle]], axis=1)
                weights = jnp.concatenate([weights, weights[LANES : 3 * LANES]], axis=0)
            wide = jnp.dot(narrow, weights, preferred_element_type=f32)
            mean = wide * (1.0 / float((2 * radius + 1) ** 2))
            least[...] = mean if radius == 1 else jnp.minimum(least[...], mean)
        for half in range(2):
            block = 2 * group + half
            even = slice(2 * block * LANES, (2 * block + 1) * LANES)
            odd = slice((2 * block + 1) * LANES, (2 * block + 2) * LANES)
            lanes = slice(half * LANES, (half + 1) * LANES)
            for i in range(cells):
                top = slice(2 * i * count, (2 * i + 1) * count)
                low = slice((2 * i + 1) * count, (2 * i + 2) * count)
                pixels = pixels_of(i, base + block * 2 * LANES)
                bands = haar_rows(*pixels)
                shrunk = []
                for band in range(3):
                    at_row = (band * cells + i) * count
                    variance = least[at_row : at_row + count, lanes]
                    gain = 1.0 / jnp.maximum(variance, 4.0 * noise_power)
                    shrunk.append(bands[band] * (gain * noise_power))
                horiz, vertic, diagon = shrunk
                both, cross = vertic + diagon, vertic - diagon
                noise = (horiz + both, horiz - both, cross - horiz, -horiz - cross)
                for (rows_at, cols_at), pixel, part in zip(
                    ((top, even), (top, odd), (low, even), (low, odd)), pixels, noise
                ):
                    start, stop = rows_at.start, rows_at.stop
                    upper, lower = halves(part.astype(bf16).astype(f32) * pixel)
                    product[start:stop, cols_at] = upper
                    product[size + start : size + stop, cols_at] = lower

    for block in range(blocks):
        cols = slice(2 * block * LANES, (2 * block + 2) * LANES)
        there = pl.ds(pl.multiple_of(base + block * 2 * LANES, 2 * LANES), 2 * LANES)
        weighted = jnp.dot(
            select[:slot_rows, :], product[:, cols], preferred_element_type=f32
        )
        part = (weighted * inverse[:slot_rows, there]).astype(bf16)
        out[:, cols] = jnp.dot(part, merge[...], preferred_element_type=f32).astype(bf16)


def main_part(chunk, own, above, below, inverse, select, box, merge, rows, pieces, slots):
    size, width_all = own.shape
    count = size // rows
    width = width_all // pieces
    cell_rows = 3 * (rows // 2) * count
    vmem = pl.BlockSpec(memory_space=pltpu.VMEM)
    smem = pl.BlockSpec(memory_space=pltpu.SMEM)
    return pl.pallas_call(
        functools.partial(main_kernel, count, rows, width),
        in_specs=[smem] + [vmem] * 7,
        out_specs=vmem,
        scratch_shapes=[
            pltpu.VMEM((RADII, cell_rows, width // 2 + 2 * LANES), bf16),
            pltpu.VMEM((FINE, cell_rows, width // 2), bf16),
            pltpu.VMEM((cell_rows, 2 * LANES), f32),
            pltpu.VMEM((2 * size, width), bf16),
        ],
        out_shape=jax.ShapeDtypeStruct((slots * rows, width), bf16),
        compiler_params=pltpu.CompilerParams(vmem_limit_bytes=20 * 2**20),
        cost_estimate=pl.CostEstimate(
            flops=2 * 10**9, bytes_accessed=4 * 2**20, transcendentals=0
        ),
        name="residual",
    )(chunk, own, above, below, inverse, select, box, merge)


def assemble_kernel(rows, select, share, *refs):
    pieces = len(refs) - 4
    parts, (prints, partial, flat, scaled) = refs[:pieces], refs[pieces:]
    size, width = parts[0].shape
    tall = CAMS * rows
    for place, part in enumerate(parts):
        edges = part[: 2 * rows, :].astype(f32) * share[place].reshape(2 * rows, width)
        scaled[place, : 2 * rows, :] = edges.astype(bf16)
    total = jnp.zeros((tall, 1), f32)
    for block in range(width // (2 * LANES)):
        cols = slice(block * 2 * LANES, (block + 1) * 2 * LANES)
        joined = jnp.zeros((tall, 2 * LANES), f32)
        for place, part in enumerate(parts):
            source = jnp.concatenate([scaled[place, :, cols], part[2 * rows :, cols]], axis=0)
            joined = joined + jnp.dot(
                select[place, :, :size], source, preferred_element_type=f32
            )
        prints[:, :, cols] = joined.reshape(CAMS, rows, 2 * LANES)
        flat[:, cols] = joined.astype(bf16)
        total = total + jnp.sum(joined, axis=1, keepdims=True)
    gram = lax.dot_general(
        flat[...], flat[...], (((1,), (1,)), ((), ())), preferred_element_type=f32
    )
    sub = lax.broadcasted_iota(jnp.int32, (tall, tall), 0)
    lane = lax.broadcasted_iota(jnp.int32, (tall, tall), 1)
    gram = jnp.where((sub & (rows - 1)) == (lane & (rows - 1)), gram, 0.0)
    gram = jnp.sum(gram.reshape(CAMS, rows, tall), axis=1)
    sub = lax.broadcasted_iota(jnp.int32, (tall, LANES), 0)
    lane = lax.broadcasted_iota(jnp.int32, (tall, LANES), 1)
    gather = jnp.where((sub >> log2(rows)) == lane, 1.0, 0.0).astype(f32)
    gram = jnp.dot(gram, gather, precision=lax.Precision.HIGHEST, preferred_element_type=f32)
    total = jnp.sum(total.reshape(CAMS, rows, 1), axis=1)
    lane = lax.broadcasted_iota(jnp.int32, (CAMS, LANES), 1)
    partial[...] = jnp.where(lane == CAMS, total, gram)


def assemble(select, share, parts, rows):
    width = parts[0].shape[1]
    return pl.pallas_call(
        functools.partial(assemble_kernel, rows),
        out_shape=[
            jax.ShapeDtypeStruct((CAMS, rows, width), f32),
            jax.ShapeDtypeStruct((CAMS, LANES), f32),
        ],
        scratch_shapes=[
            pltpu.VMEM((CAMS * rows, width), bf16),
            pltpu.VMEM((len(parts), 2 * rows, width), bf16),
        ],
        compiler_params=pltpu.CompilerParams(vmem_limit_bytes=20 * 2**20),
        cost_estimate=pl.CostEstimate(
            flops=2 * 10**9, bytes_accessed=4 * 2**20, transcendentals=0
        ),
        name="assemble",
    )(select, share, *parts)


def correlate_kernel(pixels, *refs):
    parts, out = refs[:-1], refs[-1]
    whole = parts[0][...]
    for part in parts[1:]:
        whole = whole + part[...]
    gram = whole[:, :CAMS]
    mean = whole[:, CAMS : CAMS + 1] / pixels
    sub = lax.broadcasted_iota(jnp.int32, (CAMS, CAMS), 0)
    lane = lax.broadcasted_iota(jnp.int32, (CAMS, CAMS), 1)
    diagonal = sub == lane
    mean_row = jnp.sum(jnp.where(diagonal, mean, 0.0), axis=0, keepdims=True)
    covar = gram / pixels - mean * mean_row
    only = jnp.where(diagonal, covar, 0.0)
    spread = jnp.sum(only, axis=1, keepdims=True) + var_eps
    spread_row = jnp.sum(only, axis=0, keepdims=True) + var_eps
    out[...] = covar / jnp.sqrt(spread * spread_row)


def correlate(parts, pixels):
    return pl.pallas_call(
        functools.partial(correlate_kernel, pixels),
        out_shape=jax.ShapeDtypeStruct((CAMS, CAMS), f32),
        name="correlate",
    )(*parts)


def exchange(array, axis, distance):
    size = lax.axis_size(axis)
    return lax.ppermute(array, axis, [(i, i ^ distance) for i in range(size)])


def on_device(photos, camera_id):
    count, rows, width = photos.shape
    pieces, tiles = lax.axis_size("photo"), lax.axis_size("tile")
    me = lax.axis_index("photo").astype(jnp.int32)
    own, up, down, *extras = prepare(me.reshape(1), camera_id, photos, pieces)
    above = lax.ppermute(down, "tile", [(i, i + 1) for i in range(tiles - 1)])
    below = lax.ppermute(up, "tile", [(i + 1, i) for i in range(tiles - 1)])
    extras = [
        exchange(extra, "photo", distance) if distance else extra
        for distance, extra in enumerate(extras)
    ]
    inverse, select, box, merge = energies(camera_id, own, rows)
    place, share, most = blend(me.reshape(1), extras, rows, count * rows)

    def finish(slots):
        parts = [None] * pieces
        for distance in reversed(range(pieces)):
            part = main_part(
                (me ^ distance).reshape(1), own, above, below, inverse, select, box, merge,
                rows, pieces, slots,
            )
            parts[distance] = exchange(part, "photo", distance) if distance else part
        return assemble(place, share, parts, rows)

    few = max(2, 3 * count // 4)
    prints, partial = lax.cond(
        most[0, 0] > few, lambda: finish(count), lambda: finish(few)
    )
    terms = [partial] + [exchange(partial, "photo", i) for i in range(1, pieces)]
    while len(terms) > 1:
        terms = [terms[i] + terms[i + 1] for i in range(0, len(terms), 2)]
    total = terms[0]
    distance = 1
    while 2 * distance < tiles:
        total = total + exchange(total, "tile", distance)
        distance *= 2
    sums = [total, exchange(total, "tile", distance)]
    return prints, correlate(sums, float(rows * tiles * width))


def solution(mesh):
    return jax.shard_map(
        on_device,
        mesh=mesh,
        in_specs=(P("photo", "tile", None), P("photo")),
        out_specs=(P(None, "tile", "photo"), P()),
        check_vma=False,
    )
```

```python
import functools

import jax
import jax.numpy as jnp
from jax import lax
from jax.experimental import pallas as pl
from jax.experimental.pallas import tpu as pltpu
from jax.sharding import PartitionSpec as P

CAMS = 32
RADII = 4
FINE = 2
LANES = 128

noise_power = 1.0
var_eps = 1e-06

f32 = jnp.float32
bf16 = jnp.bfloat16


def log2(value):
    return value.bit_length() - 1


def indicator(condition):
    return jnp.where(condition, 1.0, 0.0).astype(bf16)


def iotas(shape):
    return (
        lax.broadcasted_iota(jnp.int32, shape, len(shape) - 2),
        lax.broadcasted_iota(jnp.int32, shape, len(shape) - 1),
    )


def row_permutation(photos, rows):
    sub, lane = iotas((photos * rows, photos * rows))
    same_row = (sub >> log2(photos)) == (lane & (rows - 1))
    same_photo = (sub & (photos - 1)) == (lane >> log2(rows))
    return indicator(same_row & same_photo)


def column_split():
    sub, lane = iotas((2 * LANES, 2 * LANES))
    return indicator(sub == 2 * (lane & (LANES - 1)) + (lane >> log2(LANES)))


def column_merge():
    sub, lane = iotas((2 * LANES, 2 * LANES))
    return indicator(lane == 2 * (sub & (LANES - 1)) + (sub >> log2(LANES)))


def box_matrix(radius):
    sub, lane = iotas((4 * LANES, 2 * LANES))
    return indicator(jnp.abs(sub - LANES - lane) <= radius)


def haar_rows(even0, odd0, even1, odd1):
    low0, low1 = even0 + odd0, even1 + odd1
    high0, high1 = even0 - odd0, even1 - odd1
    return (low0 - low1, high0 + high1, high0 - high1)


def halves(value):
    upper = value.astype(bf16)
    lower = (value - upper.astype(f32)).astype(bf16)
    return upper, lower


def slot_numbers(ids, count):
    ranks = [jnp.int32(0)]
    for photo in range(1, count):
        ranks.append(ranks[-1] + jnp.where(ids[photo] != ids[photo - 1], 1, 0))
    last = ranks[-1]
    slots = [jnp.where(rank == 0, 0, jnp.where(rank == last, 1, rank + 1)) for rank in ranks]
    return slots, last + 1


def prepare_kernel(me, ids, photos, sorted_out, up_out, down_out, *refs):
    extras, (buffer, arrived) = refs[:-2], refs[-2:]
    count, rows, width = photos.shape
    cells = rows // 2
    pieces = len(extras)
    step = width // pieces
    bases = [pl.multiple_of((me[0] ^ distance) * step, step) for distance in range(pieces)]
    copies = []
    for distance in range(pieces):
        cols = pl.ds(bases[distance], step)
        copies.append(
            pltpu.make_async_copy(
                photos.at[:, :, cols], buffer.at[distance], arrived.at[distance]
            )
        )
        copies[-1].start()
    perm = row_permutation(count, rows)
    split = column_split()

    slots, cameras = slot_numbers(ids, count)
    sub, lane = iotas((rows, step))
    slot_id = jnp.full((rows, step), -1, jnp.int32)
    in_first, in_last = jnp.int32(0), jnp.int32(0)
    for photo in range(count):
        slot_id = jnp.where((lane >> log2(rows)) == slots[photo], ids[photo], slot_id)
        in_first = in_first + jnp.where(ids[photo] == ids[0], 1, 0)
        in_last = in_last + jnp.where(ids[photo] == ids[count - 1], 1, 0)
    notes = jnp.where(sub == 0, ids[0], jnp.where(sub == 1, ids[count - 1], slot_id))
    notes = jnp.where(sub == 3, cameras, notes).astype(f32).astype(bf16)

    for distance in range(pieces):
        copies[distance].wait()
        flat = buffer[distance].reshape(count * rows, step)
        by_row = jnp.dot(perm, flat, preferred_element_type=f32).astype(bf16)
        for inner in range(step // (2 * LANES)):
            at = inner * 2 * LANES
            cols = pl.ds(pl.multiple_of(bases[distance] + at, 2 * LANES), 2 * LANES)
            cell_cols = pl.ds(
                pl.multiple_of((me[0] ^ distance) * (step // 2) + at // 2, LANES), LANES
            )
            parted = jnp.dot(by_row[:, at : at + 2 * LANES], split, preferred_element_type=f32)
            sorted_out[:, cols] = parted.astype(bf16)
            for i in range(cells):
                if RADII <= i < cells - RADII:
                    continue
                top = parted[2 * i * count : (2 * i + 1) * count]
                low = parted[(2 * i + 1) * count : (2 * i + 2) * count]
                bands = haar_rows(top[:, :LANES], top[:, LANES:], low[:, :LANES], low[:, LANES:])
                for band in range(3):
                    square = (bands[band] * bands[band]).astype(bf16)
                    if i < RADII:
                        start = (band * RADII + i) * count
                        up_out[start : start + count, cell_cols] = square
                    if i >= cells - RADII:
                        start = (band * RADII + i - (cells - RADII)) * count
                        down_out[start : start + count, cell_cols] = square

        def add(photo, total):
            pixel = buffer[distance, photo].astype(f32)
            return total + pixel * pixel

        none = jnp.zeros((rows, step), f32)
        extra = extras[distance]
        extra[:rows, :] = lax.fori_loop(0, in_first, add, none).astype(bf16)
        extra[rows : 2 * rows, :] = lax.fori_loop(count - in_last, count, add, none).astype(bf16)
        extra[2 * rows :, :] = notes


def prepare(me, ids, photos, pieces):
    count, rows, width = photos.shape
    step = width // pieces
    size = count * rows
    halo = 3 * RADII * count
    vmem = pl.BlockSpec(memory_space=pltpu.VMEM)
    smem = pl.BlockSpec(memory_space=pltpu.SMEM)
    return pl.pallas_call(
        prepare_kernel,
        in_specs=[smem, smem, pl.BlockSpec(memory_space=pltpu.HBM)],
        out_specs=[vmem] * (3 + pieces),
        out_shape=[
            jax.ShapeDtypeStruct((size, width), bf16),
            jax.ShapeDtypeStruct((halo, width // 2), bf16),
            jax.ShapeDtypeStruct((halo, width // 2), bf16),
        ]
        + [jax.ShapeDtypeStruct((3 * rows, step), bf16)] * pieces,
        scratch_shapes=[
            pltpu.VMEM((pieces, count, rows, step), bf16),
            pltpu.SemaphoreType.DMA((pieces,)),
        ],
        compiler_params=pltpu.CompilerParams(vmem_limit_bytes=20 * 2**20),
        cost_estimate=pl.CostEstimate(flops=10**9, bytes_accessed=8 * 2**20, transcendentals=0),
        name="prepare",
    )(me, ids, photos)


def energy_kernel(count, rows, ids, own, inverse, select_out, box_out, merge_out):
    size, width = own.shape
    slots, _ = slot_numbers(ids, count)
    sub, lane = iotas((size, size))
    lane_photo = lane & (count - 1)
    lane_slot = jnp.zeros_like(lane)
    for photo in range(count):
        lane_slot = jnp.where(lane_photo == photo, slots[photo], lane_slot)
    in_slot = lane_slot == (sub >> log2(rows))
    same_row = (sub & (rows - 1)) == (lane >> log2(count))
    select = indicator(in_slot & same_row)
    select = jnp.concatenate([select, select], axis=1)
    select_out[...] = select
    for radius in range(1, RADII + 1):
        box_out[radius - 1] = box_matrix(radius)
    merge_out[...] = column_merge()
    for block in range(width // (2 * LANES)):
        cols = slice(block * 2 * LANES, (block + 1) * 2 * LANES)
        pixel = own[:, cols].astype(f32)
        pair = jnp.concatenate(halves(pixel * pixel), axis=0)
        energy = jnp.dot(select, pair, preferred_element_type=f32)
        inverse[:, cols] = 1.0 / jnp.maximum(energy, 2.0**-20)


def energies(ids, own, rows):
    size, width = own.shape
    vmem = pl.BlockSpec(memory_space=pltpu.VMEM)
    smem = pl.BlockSpec(memory_space=pltpu.SMEM)
    return pl.pallas_call(
        functools.partial(energy_kernel, size // rows, rows),
        in_specs=[smem, vmem],
        out_specs=[vmem] * 4,
        out_shape=[
            jax.ShapeDtypeStruct((size, width), f32),
            jax.ShapeDtypeStruct((size, 2 * size), bf16),
            jax.ShapeDtypeStruct((RADII, 4 * LANES, 2 * LANES), bf16),
            jax.ShapeDtypeStruct((2 * LANES, 2 * LANES), bf16),
        ],
        compiler_params=pltpu.CompilerParams(vmem_limit_bytes=20 * 2**20),
        cost_estimate=pl.CostEstimate(flops=10**9, bytes_accessed=8 * 2**20, transcendentals=0),
        name="energies",
    )(ids, own)


def blend_kernel(rows, me, *refs):
    pieces = len(refs) - 3
    extras, (select, share, held) = refs[:pieces], refs[pieces:]
    size = select.shape[2]
    tall = CAMS * rows
    sub, lane = iotas((tall, size))
    same_row = (sub & (rows - 1)) == (lane & (rows - 1))
    camera = (sub >> log2(rows)).astype(f32)
    for distance, extra in enumerate(extras):
        notes = extra[2 * rows :, :].astype(f32)
        select[distance] = indicator((camera == notes[2:3, :size]) & same_row)
        held[me[0] ^ distance] = extra[...].astype(f32)
    ones = jnp.ones((rows, share.shape[3]), f32)
    for device in range(pieces):
        if device == 0:
            share[me[0] ^ device, 0] = ones
        if device == pieces - 1:
            share[me[0] ^ device, 1] = ones
            continue
        late = held[device, rows : 2 * rows]
        early = held[device + 1, :rows]
        crosses = held[device, 2 * rows + 1 : 2 * rows + 2] == held[device + 1, 2 * rows : 2 * rows + 1]
        joint = 1.0 / (late + early)
        share[me[0] ^ device, 1] = jnp.where(crosses, late * joint, 1.0)
        share[me[0] ^ (device + 1), 0] = jnp.where(crosses, early * joint, 1.0)


def blend(me, extras, rows, size):
    pieces, width = len(extras), extras[0].shape[1]
    vmem = pl.BlockSpec(memory_space=pltpu.VMEM)
    smem = pl.BlockSpec(memory_space=pltpu.SMEM)
    return pl.pallas_call(
        functools.partial(blend_kernel, rows),
        in_specs=[smem] + [vmem] * pieces,
        out_specs=[vmem, vmem],
        out_shape=[
            jax.ShapeDtypeStruct((pieces, CAMS * rows, size), bf16),
            jax.ShapeDtypeStruct((pieces, 2, rows, width), f32),
        ],
        scratch_shapes=[pltpu.VMEM((pieces, 3 * rows, width), f32)],
        compiler_params=pltpu.CompilerParams(vmem_limit_bytes=20 * 2**20),
        name="blend",
    )(me, *extras)


def main_kernel(
    count, rows, blocks_all,
    where,
    own, own_l, own_r, above, above_l, above_r, below, below_l, below_r,
    inverse, select, box, merge,
    out,
    sums, rest, least, product, scale, arrived,
):
    cells = rows // 2
    size = count * rows
    width = own.shape[1]
    blocks = width // (2 * LANES)
    chunk = where[0]
    left_ok = jnp.where(chunk > 0, 1.0, 0.0).astype(f32)
    right_ok = jnp.where((chunk + 1) * blocks < blocks_all, 1.0, 0.0).astype(f32)

    slot_rows = out.shape[0]
    copy = pltpu.make_async_copy(
        inverse.at[pl.ds(0, slot_rows), pl.ds(pl.multiple_of(chunk * width, width), width)],
        scale,
        arrived,
    )
    copy.start()

    for block in range(-1, blocks + 1):
        if block < 0:
            mine, over, under, factor, at = own_l, above_l, below_l, left_ok, 0
        elif block == blocks:
            mine, over, under, factor, at = own_r, above_r, below_r, right_ok, 0
        else:
            mine, over, under, factor, at = own, above, below, None, block
        even = slice(2 * at * LANES, (2 * at + 1) * LANES)
        odd = slice((2 * at + 1) * LANES, (2 * at + 2) * LANES)
        cols = slice(at * LANES, (at + 1) * LANES)
        place = slice((block + 1) * LANES, (block + 2) * LANES)
        squares = [[], [], []]
        for i in range(cells):
            top = slice(2 * i * count, (2 * i + 1) * count)
            low = slice((2 * i + 1) * count, (2 * i + 2) * count)
            bands = haar_rows(
                mine[top, even].astype(f32),
                mine[top, odd].astype(f32),
                mine[low, even].astype(f32),
                mine[low, odd].astype(f32),
            )
            for band in range(3):
                squares[band].append(bands[band] * bands[band])
        for band in range(3):
            start = band * RADII * count
            outer = [
                over[start + i * count : start + (i + 1) * count, cols].astype(f32)
                for i in range(RADII)
            ]
            inner = [
                under[start + i * count : start + (i + 1) * count, cols].astype(f32)
                for i in range(RADII)
            ]
            column = outer + squares[band] + inner
            if factor is not None:
                column = [value * factor for value in column]
            for i in range(cells):
                total = column[i + RADII]
                at_row = (band * cells + i) * count
                for radius in range(1, RADII + 1):
                    total = total + (column[i + RADII - radius] + column[i + RADII + radius])
                    upper = total.astype(bf16)
                    sums[radius - 1, at_row : at_row + count, place] = upper
                    if radius <= FINE and factor is None:
                        lower = (total - upper.astype(f32)).astype(bf16)
                        rest[radius - 1, at_row : at_row + count, cols] = lower

    for group in range(blocks // 2):
        window = slice(2 * group * LANES, (2 * group + 4) * LANES)
        for radius in range(1, RADII + 1):
            narrow, weights = sums[radius - 1, :, window], box[radius - 1]
            if radius <= FINE:
                middle = slice(2 * group * LANES, (2 * group + 2) * LANES)
                narrow = jnp.concatenate([narrow, rest[radius - 1, :, middle]], axis=1)
                weights = jnp.concatenate([weights, weights[LANES : 3 * LANES]], axis=0)
            wide = jnp.dot(narrow, weights, preferred_element_type=f32)
            mean = wide * (1.0 / float((2 * radius + 1) ** 2))
            least[...] = mean if radius == 1 else jnp.minimum(least[...], mean)
        for half in range(2):
            block = 2 * group + half
            even = slice(2 * block * LANES, (2 * block + 1) * LANES)
            odd = slice((2 * block + 1) * LANES, (2 * block + 2) * LANES)
            lanes = slice(half * LANES, (half + 1) * LANES)
            for i in range(cells):
                top = slice(2 * i * count, (2 * i + 1) * count)
                low = slice((2 * i + 1) * count, (2 * i + 2) * count)
                pixels = (
                    own[top, even].astype(f32),
                    own[top, odd].astype(f32),
                    own[low, even].astype(f32),
                    own[low, odd].astype(f32),
                )
                bands = haar_rows(*pixels)
                shrunk = []
                for band in range(3):
                    at_row = (band * cells + i) * count
                    variance = least[at_row : at_row + count, lanes]
                    gain = 1.0 / jnp.maximum(variance, 4.0 * noise_power)
                    shrunk.append(bands[band] * (gain * noise_power))
                horiz, vertic, diagon = shrunk
                both, cross = vertic + diagon, vertic - diagon
                noise = (horiz + both, horiz - both, cross - horiz, -horiz - cross)
                for (rows_at, cols_at), pixel, part in zip(
                    ((top, even), (top, odd), (low, even), (low, odd)), pixels, noise
                ):
                    start, stop = rows_at.start, rows_at.stop
                    upper, lower = halves(part.astype(bf16).astype(f32) * pixel)
                    product[start:stop, cols_at] = upper
                    product[size + start : size + stop, cols_at] = lower

    copy.wait()
    for block in range(blocks):
        cols = slice(2 * block * LANES, (2 * block + 2) * LANES)
        weighted = jnp.dot(select[...], product[:, cols], preferred_element_type=f32)
        part = (weighted * scale[:, cols]).astype(bf16)
        out[:, cols] = jnp.dot(part, merge[...], preferred_element_type=f32).astype(bf16)


def main_part(chunk, own, above, below, inverse, select, box, merge, rows, pieces, slots):
    size, width_all = own.shape
    count = size // rows
    width = width_all // pieces
    halo = above.shape[0]
    blocks_all = width_all // (2 * LANES)
    blocks = width // (2 * LANES)
    here = lambda i, where: (0, where[0])
    left = lambda i, where: (0, jnp.maximum(where[0] * blocks - 1, 0))
    right = lambda i, where: (0, jnp.minimum((where[0] + 1) * blocks, blocks_all - 1))
    cell_rows = 3 * (rows // 2) * count
    halo_specs = [
        pl.BlockSpec((halo, width // 2), here),
        pl.BlockSpec((halo, LANES), left),
        pl.BlockSpec((halo, LANES), right),
    ]
    return pl.pallas_call(
        functools.partial(main_kernel, count, rows, blocks_all),
        grid_spec=pltpu.PrefetchScalarGridSpec(
            num_scalar_prefetch=1,
            grid=(1,),
            in_specs=[
                pl.BlockSpec((size, width), here),
                pl.BlockSpec((size, 2 * LANES), left),
                pl.BlockSpec((size, 2 * LANES), right),
                *halo_specs,
                *halo_specs,
                pl.BlockSpec(memory_space=pl.ANY),
                pl.BlockSpec((slots * rows, 2 * size), lambda i, where: (0, 0)),
                pl.BlockSpec((RADII, 4 * LANES, 2 * LANES), lambda i, where: (0, 0, 0)),
                pl.BlockSpec((2 * LANES, 2 * LANES), lambda i, where: (0, 0)),
            ],
            out_specs=pl.BlockSpec((slots * rows, width), lambda i, where: (0, 0)),
            scratch_shapes=[
                pltpu.VMEM((RADII, cell_rows, width // 2 + 2 * LANES), bf16),
                pltpu.VMEM((FINE, cell_rows, width // 2), bf16),
                pltpu.VMEM((cell_rows, 2 * LANES), f32),
                pltpu.VMEM((2 * size, width), bf16),
                pltpu.VMEM((slots * rows, width), f32),
                pltpu.SemaphoreType.DMA(()),
            ],
        ),
        out_shape=jax.ShapeDtypeStruct((slots * rows, width), bf16),
        compiler_params=pltpu.CompilerParams(vmem_limit_bytes=20 * 2**20),
        cost_estimate=pl.CostEstimate(
            flops=2 * 10**9, bytes_accessed=4 * 2**20, transcendentals=0
        ),
        name="residual",
    )(
        chunk, own, own, own, above, above, above, below, below, below, inverse, select, box, merge,
    )


def assemble_kernel(rows, select, share, *refs):
    pieces = len(refs) - 3
    parts, (flat, partial, scaled) = refs[:pieces], refs[pieces:]
    size, width = parts[0].shape
    tall = CAMS * rows
    for place, part in enumerate(parts):
        edges = part[: 2 * rows, :].astype(f32) * share[place].reshape(2 * rows, width)
        scaled[place, : 2 * rows, :] = edges.astype(bf16)
    total = jnp.zeros((tall, 1), f32)
    for block in range(width // (2 * LANES)):
        cols = slice(block * 2 * LANES, (block + 1) * 2 * LANES)
        joined = jnp.zeros((tall, 2 * LANES), f32)
        for place, part in enumerate(parts):
            source = jnp.concatenate([scaled[place, :, cols], part[2 * rows :, cols]], axis=0)
            joined = joined + jnp.dot(
                select[place, :, :size], source, preferred_element_type=f32
            )
        flat[:, cols] = joined.astype(bf16)
        total = total + jnp.sum(joined, axis=1, keepdims=True)
    gram = lax.dot_general(
        flat[...], flat[...], (((1,), (1,)), ((), ())), preferred_element_type=f32
    )
    sub = lax.broadcasted_iota(jnp.int32, (tall, tall), 0)
    lane = lax.broadcasted_iota(jnp.int32, (tall, tall), 1)
    gram = jnp.where((sub & (rows - 1)) == (lane & (rows - 1)), gram, 0.0)
    gram = jnp.sum(gram.reshape(CAMS, rows, tall), axis=1)
    sub = lax.broadcasted_iota(jnp.int32, (tall, LANES), 0)
    lane = lax.broadcasted_iota(jnp.int32, (tall, LANES), 1)
    gather = jnp.where((sub >> log2(rows)) == lane, 1.0, 0.0).astype(f32)
    gram = jnp.dot(gram, gather, precision=lax.Precision.HIGHEST, preferred_element_type=f32)
    total = jnp.sum(total.reshape(CAMS, rows, 1), axis=1)
    lane = lax.broadcasted_iota(jnp.int32, (CAMS, LANES), 1)
    partial[...] = jnp.where(lane == CAMS, total, gram)


def assemble(select, share, parts, rows):
    width = parts[0].shape[1]
    return pl.pallas_call(
        functools.partial(assemble_kernel, rows),
        out_shape=[
            jax.ShapeDtypeStruct((CAMS * rows, width), bf16),
            jax.ShapeDtypeStruct((CAMS, LANES), f32),
        ],
        scratch_shapes=[
            pltpu.VMEM((len(parts), 2 * rows, width), bf16),
        ],
        compiler_params=pltpu.CompilerParams(vmem_limit_bytes=20 * 2**20),
        cost_estimate=pl.CostEstimate(
            flops=2 * 10**9, bytes_accessed=4 * 2**20, transcendentals=0
        ),
        name="assemble",
    )(select, share, *parts)


def correlate_kernel(pixels, *refs):
    parts, out = refs[:-1], refs[-1]
    whole = parts[0][...]
    for part in parts[1:]:
        whole = whole + part[...]
    gram = whole[:, :CAMS]
    mean = whole[:, CAMS : CAMS + 1] / pixels
    sub = lax.broadcasted_iota(jnp.int32, (CAMS, CAMS), 0)
    lane = lax.broadcasted_iota(jnp.int32, (CAMS, CAMS), 1)
    diagonal = sub == lane
    mean_row = jnp.sum(jnp.where(diagonal, mean, 0.0), axis=0, keepdims=True)
    covar = gram / pixels - mean * mean_row
    only = jnp.where(diagonal, covar, 0.0)
    spread = jnp.sum(only, axis=1, keepdims=True) + var_eps
    spread_row = jnp.sum(only, axis=0, keepdims=True) + var_eps
    out[...] = covar / jnp.sqrt(spread * spread_row)


def correlate(parts, pixels):
    return pl.pallas_call(
        functools.partial(correlate_kernel, pixels),
        out_shape=jax.ShapeDtypeStruct((CAMS, CAMS), f32),
        compiler_params=pltpu.CompilerParams(vmem_limit_bytes=4 * 2**20),
        name="correlate",
    )(*parts)


def exchange(array, axis, distance):
    size = lax.axis_size(axis)
    return lax.ppermute(array, axis, [(i, i ^ distance) for i in range(size)])


def summed(array, axis, distances):
    terms = [array] + [exchange(array, axis, distance) for distance in distances]
    while len(terms) > 1:
        terms = [terms[i] + terms[i + 1] for i in range(0, len(terms), 2)]
    return terms[0]


def on_device(photos, camera_id):
    count, rows, width = photos.shape
    pieces, tiles = lax.axis_size("photo"), lax.axis_size("tile")
    me = lax.axis_index("photo").astype(jnp.int32)
    own, up, down, *extras = prepare(me.reshape(1), camera_id, photos, pieces)
    above = lax.ppermute(down, "tile", [(i, i + 1) for i in range(tiles - 1)])
    below = lax.ppermute(up, "tile", [(i + 1, i) for i in range(tiles - 1)])
    extras = [
        exchange(extra, "photo", distance) if distance else extra
        for distance, extra in enumerate(extras)
    ]
    inverse, select, box, merge = energies(camera_id, own, rows)

    def finish(slots):
        parts = [None] * pieces
        for distance in reversed(range(pieces)):
            part = main_part(
                (me ^ distance).reshape(1), own, above, below, inverse, select, box, merge,
                rows, pieces, slots,
            )
            parts[distance] = exchange(part, "photo", distance) if distance else part
        place, share = blend(me.reshape(1), extras, rows, count * rows)
        return assemble(place, share, parts, rows)

    most = functools.reduce(jnp.maximum, [extra[2 * rows + 3, 0] for extra in extras])
    sizes = sorted({max(2, count * part // 16) for part in (9, 10, 12, 16)})
    branch = sum((most > size).astype(jnp.int32) for size in sizes[:-1])
    flat, partial = lax.switch(branch, [functools.partial(finish, size) for size in sizes])
    prints = flat.reshape(CAMS, rows, width // pieces).astype(f32)

    total = summed(partial, "tile", (1,))
    total = summed(total, "photo", range(1, pieces))
    total = summed(total, "tile", range(2, tiles, 2))
    return prints, correlate([total], float(rows * tiles * width))


def solution(mesh):
    return jax.shard_map(
        on_device,
        mesh=mesh,
        in_specs=(P("photo", "tile", None), P("photo")),
        out_specs=(P(None, "tile", "photo"), P()),
        check_vma=False,
    )
```

```python
import functools

import jax
import jax.numpy as jnp
from jax import lax
from jax.experimental import pallas as pl
from jax.experimental.pallas import tpu as pltpu
from jax.sharding import PartitionSpec as P

CAMS = 32
RADII = 4
FINE = 2
LANES = 128

noise_power = 1.0
var_eps = 1e-06

f32 = jnp.float32
bf16 = jnp.bfloat16


def log2(value):
    return value.bit_length() - 1


def indicator(condition):
    return jnp.where(condition, 1.0, 0.0).astype(bf16)


def iotas(shape):
    return (
        lax.broadcasted_iota(jnp.int32, shape, len(shape) - 2),
        lax.broadcasted_iota(jnp.int32, shape, len(shape) - 1),
    )


def row_permutation(photos, rows):
    sub, lane = iotas((photos * rows, photos * rows))
    same_row = (sub >> log2(photos)) == (lane & (rows - 1))
    same_photo = (sub & (photos - 1)) == (lane >> log2(rows))
    return indicator(same_row & same_photo)


def column_split():
    sub, lane = iotas((2 * LANES, 2 * LANES))
    return indicator(sub == 2 * (lane & (LANES - 1)) + (lane >> log2(LANES)))


def column_merge():
    sub, lane = iotas((2 * LANES, 2 * LANES))
    return indicator(lane == 2 * (sub & (LANES - 1)) + (sub >> log2(LANES)))


def box_matrix(radius):
    sub, lane = iotas((4 * LANES, 2 * LANES))
    return indicator(jnp.abs(sub - LANES - lane) <= radius)


def haar_rows(even0, odd0, even1, odd1):
    low0, low1 = even0 + odd0, even1 + odd1
    high0, high1 = even0 - odd0, even1 - odd1
    return (low0 - low1, high0 + high1, high0 - high1)


def halves(value):
    upper = value.astype(bf16)
    lower = (value - upper.astype(f32)).astype(bf16)
    return upper, lower


def slot_numbers(ids, count):
    ranks = [jnp.int32(0)]
    for photo in range(1, count):
        ranks.append(ranks[-1] + jnp.where(ids[photo] != ids[photo - 1], 1, 0))
    last = ranks[-1]
    slots = [jnp.where(rank == 0, 0, jnp.where(rank == last, 1, rank + 1)) for rank in ranks]
    return slots, last + 1


def prepare_kernel(me, ids, photos, sorted_out, up_out, down_out, *refs):
    extras, (buffer, arrived) = refs[:-2], refs[-2:]
    count, rows, width = photos.shape
    cells = rows // 2
    pieces = len(extras)
    step = width // pieces
    bases = [pl.multiple_of((me[0] ^ distance) * step, step) for distance in range(pieces)]
    copies = []
    for distance in range(pieces):
        cols = pl.ds(bases[distance], step)
        copies.append(
            pltpu.make_async_copy(
                photos.at[:, :, cols], buffer.at[distance], arrived.at[distance]
            )
        )
        copies[-1].start()
    perm = row_permutation(count, rows)
    split = column_split()

    slots, cameras = slot_numbers(ids, count)
    sub, lane = iotas((rows, step))
    slot_id = jnp.full((rows, step), -1, jnp.int32)
    in_first, in_last = jnp.int32(0), jnp.int32(0)
    for photo in range(count):
        slot_id = jnp.where((lane >> log2(rows)) == slots[photo], ids[photo], slot_id)
        in_first = in_first + jnp.where(ids[photo] == ids[0], 1, 0)
        in_last = in_last + jnp.where(ids[photo] == ids[count - 1], 1, 0)
    notes = jnp.where(sub == 0, ids[0], jnp.where(sub == 1, ids[count - 1], slot_id))
    notes = jnp.where(sub == 3, cameras, notes).astype(f32).astype(bf16)

    for distance in range(pieces):
        copies[distance].wait()
        flat = buffer[distance].reshape(count * rows, step)
        by_row = jnp.dot(perm, flat, preferred_element_type=f32).astype(bf16)
        for inner in range(step // (2 * LANES)):
            at = inner * 2 * LANES
            cols = pl.ds(pl.multiple_of(bases[distance] + at, 2 * LANES), 2 * LANES)
            cell_cols = pl.ds(
                pl.multiple_of((me[0] ^ distance) * (step // 2) + at // 2, LANES), LANES
            )
            parted = jnp.dot(by_row[:, at : at + 2 * LANES], split, preferred_element_type=f32)
            sorted_out[:, cols] = parted.astype(bf16)
            for i in range(cells):
                if RADII <= i < cells - RADII:
                    continue
                top = parted[2 * i * count : (2 * i + 1) * count]
                low = parted[(2 * i + 1) * count : (2 * i + 2) * count]
                bands = haar_rows(top[:, :LANES], top[:, LANES:], low[:, :LANES], low[:, LANES:])
                for band in range(3):
                    square = (bands[band] * bands[band]).astype(bf16)
                    if i < RADII:
                        start = (band * RADII + i) * count
                        up_out[start : start + count, cell_cols] = square
                    if i >= cells - RADII:
                        start = (band * RADII + i - (cells - RADII)) * count
                        down_out[start : start + count, cell_cols] = square

        def add(photo, total):
            pixel = buffer[distance, photo].astype(f32)
            return total + pixel * pixel

        none = jnp.zeros((rows, step), f32)
        extra = extras[distance]
        extra[:rows, :] = lax.fori_loop(0, in_first, add, none).astype(bf16)
        extra[rows : 2 * rows, :] = lax.fori_loop(count - in_last, count, add, none).astype(bf16)
        extra[2 * rows :, :] = notes


def prepare(me, ids, photos, pieces):
    count, rows, width = photos.shape
    step = width // pieces
    size = count * rows
    halo = 3 * RADII * count
    vmem = pl.BlockSpec(memory_space=pltpu.VMEM)
    smem = pl.BlockSpec(memory_space=pltpu.SMEM)
    return pl.pallas_call(
        prepare_kernel,
        in_specs=[smem, smem, pl.BlockSpec(memory_space=pltpu.HBM)],
        out_specs=[vmem] * (3 + pieces),
        out_shape=[
            jax.ShapeDtypeStruct((size, width), bf16),
            jax.ShapeDtypeStruct((halo, width // 2), bf16),
            jax.ShapeDtypeStruct((halo, width // 2), bf16),
        ]
        + [jax.ShapeDtypeStruct((3 * rows, step), bf16)] * pieces,
        scratch_shapes=[
            pltpu.VMEM((pieces, count, rows, step), bf16),
            pltpu.SemaphoreType.DMA((pieces,)),
        ],
        compiler_params=pltpu.CompilerParams(vmem_limit_bytes=20 * 2**20),
        cost_estimate=pl.CostEstimate(flops=10**9, bytes_accessed=8 * 2**20, transcendentals=0),
        name="prepare",
    )(me, ids, photos)


def energy_kernel(count, rows, ids, own, inverse, select_out, box_out, merge_out):
    size, width = own.shape
    slots, _ = slot_numbers(ids, count)
    sub, lane = iotas((size, size))
    lane_photo = lane & (count - 1)
    lane_slot = jnp.zeros_like(lane)
    for photo in range(count):
        lane_slot = jnp.where(lane_photo == photo, slots[photo], lane_slot)
    in_slot = lane_slot == (sub >> log2(rows))
    same_row = (sub & (rows - 1)) == (lane >> log2(count))
    select = indicator(in_slot & same_row)
    select = jnp.concatenate([select, select], axis=1)
    select_out[...] = select
    for radius in range(1, RADII + 1):
        box_out[radius - 1] = box_matrix(radius)
    merge_out[...] = column_merge()
    for block in range(width // (2 * LANES)):
        cols = slice(block * 2 * LANES, (block + 1) * 2 * LANES)
        pixel = own[:, cols].astype(f32)
        pair = jnp.concatenate(halves(pixel * pixel), axis=0)
        energy = jnp.dot(select, pair, preferred_element_type=f32)
        inverse[:, cols] = 1.0 / jnp.maximum(energy, 2.0**-20)


def energies(ids, own, rows):
    size, width = own.shape
    vmem = pl.BlockSpec(memory_space=pltpu.VMEM)
    smem = pl.BlockSpec(memory_space=pltpu.SMEM)
    return pl.pallas_call(
        functools.partial(energy_kernel, size // rows, rows),
        in_specs=[smem, vmem],
        out_specs=[vmem] * 4,
        out_shape=[
            jax.ShapeDtypeStruct((size, width), f32),
            jax.ShapeDtypeStruct((size, 2 * size), bf16),
            jax.ShapeDtypeStruct((RADII, 4 * LANES, 2 * LANES), bf16),
            jax.ShapeDtypeStruct((2 * LANES, 2 * LANES), bf16),
        ],
        compiler_params=pltpu.CompilerParams(vmem_limit_bytes=20 * 2**20),
        cost_estimate=pl.CostEstimate(flops=10**9, bytes_accessed=8 * 2**20, transcendentals=0),
        name="energies",
    )(ids, own)


def blend_kernel(rows, me, *refs):
    pieces = len(refs) - 3
    extras, (select, share, held) = refs[:pieces], refs[pieces:]
    size = select.shape[2]
    tall = CAMS * rows
    sub, lane = iotas((tall, size))
    same_row = (sub & (rows - 1)) == (lane & (rows - 1))
    camera = (sub >> log2(rows)).astype(f32)
    for distance, extra in enumerate(extras):
        notes = extra[2 * rows :, :].astype(f32)
        select[distance] = indicator((camera == notes[2:3, :size]) & same_row)
        held[me[0] ^ distance] = extra[...].astype(f32)
    ones = jnp.ones((rows, share.shape[3]), f32)
    for device in range(pieces):
        if device == 0:
            share[me[0] ^ device, 0] = ones
        if device == pieces - 1:
            share[me[0] ^ device, 1] = ones
            continue
        late = held[device, rows : 2 * rows]
        early = held[device + 1, :rows]
        crosses = held[device, 2 * rows + 1 : 2 * rows + 2] == held[device + 1, 2 * rows : 2 * rows + 1]
        joint = 1.0 / (late + early)
        share[me[0] ^ device, 1] = jnp.where(crosses, late * joint, 1.0)
        share[me[0] ^ (device + 1), 0] = jnp.where(crosses, early * joint, 1.0)


def blend(me, extras, rows, size):
    pieces, width = len(extras), extras[0].shape[1]
    vmem = pl.BlockSpec(memory_space=pltpu.VMEM)
    smem = pl.BlockSpec(memory_space=pltpu.SMEM)
    return pl.pallas_call(
        functools.partial(blend_kernel, rows),
        in_specs=[smem] + [vmem] * pieces,
        out_specs=[vmem, vmem],
        out_shape=[
            jax.ShapeDtypeStruct((pieces, CAMS * rows, size), bf16),
            jax.ShapeDtypeStruct((pieces, 2, rows, width), f32),
        ],
        scratch_shapes=[pltpu.VMEM((pieces, 3 * rows, width), f32)],
        compiler_params=pltpu.CompilerParams(vmem_limit_bytes=20 * 2**20),
        name="blend",
    )(me, *extras)


def main_kernel(
    count, rows, pairs,
    where,
    own, own_l, own_r, above, above_l, above_r, below, below_l, below_r,
    inverse, select, box, merge,
    far, near,
    sums, rest, least, product, scale, select_in, box_in, merge_in, joined, arrived,
):
    cells = rows // 2
    size = count * rows
    span = own.shape[1]
    width = span // 2
    blocks = span // (2 * LANES)
    pair = where[0]
    slot_rows = far.shape[0]
    late = [
        pltpu.make_async_copy(box, box_in, arrived.at[0]),
        pltpu.make_async_copy(select.at[pl.ds(0, slot_rows)], select_in, arrived.at[1]),
        pltpu.make_async_copy(
            inverse.at[pl.ds(0, slot_rows), pl.ds(pl.multiple_of(pair * span, span), span)],
            scale,
            arrived.at[2],
        ),
        pltpu.make_async_copy(merge, merge_in, arrived.at[3]),
    ]
    for copy in late:
        copy.start()

    def add_up(mine, over, under, at, block):
        even = slice(2 * at * LANES, (2 * at + 1) * LANES)
        odd = slice((2 * at + 1) * LANES, (2 * at + 2) * LANES)
        cols = slice(at * LANES, (at + 1) * LANES)
        place = slice((block + 1) * LANES, (block + 2) * LANES)
        inside = 0 <= block < blocks
        squares = [[], [], []]
        for i in range(cells):
            top = slice(2 * i * count, (2 * i + 1) * count)
            low = slice((2 * i + 1) * count, (2 * i + 2) * count)
            bands = haar_rows(
                mine[top, even].astype(f32),
                mine[top, odd].astype(f32),
                mine[low, even].astype(f32),
                mine[low, odd].astype(f32),
            )
            for band in range(3):
                squares[band].append(bands[band] * bands[band])
        for band in range(3):
            first = band * RADII * count
            outer, inner = (
                [
                    halo[first + i * count : first + (i + 1) * count, cols].astype(f32)
                    for i in range(RADII)
                ]
                for halo in (over, under)
            )
            column = outer + squares[band] + inner
            for i in range(cells):
                total = column[i + RADII]
                at_row = (band * cells + i) * count
                for radius in range(1, RADII + 1):
                    total = total + (column[i + RADII - radius] + column[i + RADII + radius])
                    upper = total.astype(bf16)
                    sums[radius - 1, at_row : at_row + count, place] = upper
                    if radius <= FINE and inside:
                        lower = (total - upper.astype(f32)).astype(bf16)
                        rest[radius - 1, at_row : at_row + count, cols] = lower

    for valid, mine, over, under, block in (
        (pair > 0, own_l, above_l, below_l, -1),
        (pair < pairs - 1, own_r, above_r, below_r, blocks),
    ):
        place = slice((block + 1) * LANES, (block + 2) * LANES)

        @pl.when(valid)
        def _():
            add_up(mine, over, under, 0, block)

        @pl.when(jnp.logical_not(valid))
        def _():
            sums[:, :, place] = jnp.zeros(sums.shape[:2] + (LANES,), bf16)

    for block in range(blocks):
        add_up(own, above, below, block, block)

    late[0].wait()
    for group in range(blocks // 2):
        window = slice(2 * group * LANES, (2 * group + 4) * LANES)
        for radius in range(1, RADII + 1):
            narrow, weights = sums[radius - 1, :, window], box_in[radius - 1]
            if radius <= FINE:
                middle = slice(2 * group * LANES, (2 * group + 2) * LANES)
                narrow = jnp.concatenate([narrow, rest[radius - 1, :, middle]], axis=1)
                weights = jnp.concatenate([weights, weights[LANES : 3 * LANES]], axis=0)
            wide = jnp.dot(narrow, weights, preferred_element_type=f32)
            mean = wide * (1.0 / float((2 * radius + 1) ** 2))
            least[...] = mean if radius == 1 else jnp.minimum(least[...], mean)
        for half in range(2):
            block = 2 * group + half
            even = slice(2 * block * LANES, (2 * block + 1) * LANES)
            odd = slice((2 * block + 1) * LANES, (2 * block + 2) * LANES)
            lanes = slice(half * LANES, (half + 1) * LANES)
            for i in range(cells):
                top = slice(2 * i * count, (2 * i + 1) * count)
                low = slice((2 * i + 1) * count, (2 * i + 2) * count)
                pixels = (
                    own[top, even].astype(f32),
                    own[top, odd].astype(f32),
                    own[low, even].astype(f32),
                    own[low, odd].astype(f32),
                )
                bands = haar_rows(*pixels)
                shrunk = []
                for band in range(3):
                    at_row = (band * cells + i) * count
                    variance = least[at_row : at_row + count, lanes]
                    bound = jnp.maximum(variance, 4.0 * noise_power)
                    guess = pl.reciprocal(bound, approx=True)
                    gain = guess * (2.0 * noise_power - noise_power * (bound * guess))
                    shrunk.append(bands[band] * gain)
                horiz, vertic, diagon = shrunk
                both, cross = vertic + diagon, vertic - diagon
                noise = (horiz + both, horiz - both, cross - horiz, -horiz - cross)
                for (rows_at, cols_at), pixel, part in zip(
                    ((top, even), (top, odd), (low, even), (low, odd)), pixels, noise
                ):
                    start, stop = rows_at.start, rows_at.stop
                    upper, lower = halves(part.astype(bf16).astype(f32) * pixel)
                    product[start:stop, cols_at] = upper
                    product[size + start : size + stop, cols_at] = lower

    for copy in late[1:]:
        copy.wait()
    for block in range(blocks):
        cols = slice(2 * block * LANES, (2 * block + 2) * LANES)
        weighted = jnp.dot(select_in[...], product[:, cols], preferred_element_type=f32)
        part = (weighted * scale[:, cols]).astype(bf16)
        joined[:, cols] = jnp.dot(part, merge_in[...], preferred_element_type=f32).astype(bf16)
    place = where[1]
    far[...] = joined[:, pl.ds(pl.multiple_of((1 - place) * width, width), width)]
    near[...] = joined[:, pl.ds(pl.multiple_of(place * width, width), width)]


def main_part(where, own, above, below, inverse, select, box, merge, rows, pieces, slots):
    size, width_all = own.shape
    count = size // rows
    width = width_all // pieces
    span = 2 * width
    halo = above.shape[0]
    blocks_all = width_all // (2 * LANES)
    blocks = span // (2 * LANES)
    here = lambda i, where: (0, where[0])
    left = lambda i, where: (0, jnp.maximum(where[0] * blocks - 1, 0))
    right = lambda i, where: (0, jnp.minimum((where[0] + 1) * blocks, blocks_all - 1))
    cell_rows = 3 * (rows // 2) * count
    halo_specs = [
        pl.BlockSpec((halo, span // 2), here),
        pl.BlockSpec((halo, LANES), left),
        pl.BlockSpec((halo, LANES), right),
    ]
    out = jax.ShapeDtypeStruct((slots * rows, width), bf16)
    return pl.pallas_call(
        functools.partial(main_kernel, count, rows, pieces // 2),
        grid_spec=pltpu.PrefetchScalarGridSpec(
            num_scalar_prefetch=1,
            grid=(1,),
            in_specs=[
                pl.BlockSpec((size, span), here),
                pl.BlockSpec((size, 2 * LANES), left),
                pl.BlockSpec((size, 2 * LANES), right),
                *halo_specs,
                *halo_specs,
                *[pl.BlockSpec(memory_space=pl.ANY)] * 4,
            ],
            out_specs=[pl.BlockSpec((slots * rows, width), lambda i, where: (0, 0))] * 2,
            scratch_shapes=[
                pltpu.VMEM((RADII, cell_rows, span // 2 + 2 * LANES), bf16),
                pltpu.VMEM((FINE, cell_rows, span // 2), bf16),
                pltpu.VMEM((cell_rows, 2 * LANES), f32),
                pltpu.VMEM((2 * size, span), bf16),
                pltpu.VMEM((slots * rows, span), f32),
                pltpu.VMEM((slots * rows, 2 * size), bf16),
                pltpu.VMEM((RADII, 4 * LANES, 2 * LANES), bf16),
                pltpu.VMEM((2 * LANES, 2 * LANES), bf16),
                pltpu.VMEM((slots * rows, span), bf16),
                pltpu.SemaphoreType.DMA((4,)),
            ],
        ),
        out_shape=[out, out],
        compiler_params=pltpu.CompilerParams(vmem_limit_bytes=32 * 2**20),
        cost_estimate=pl.CostEstimate(
            flops=4 * 10**9, bytes_accessed=8 * 2**20, transcendentals=0
        ),
        name="residual",
    )(
        where, own, own, own, above, above, above, below, below, below, inverse, select, box, merge,
    )


def most_kernel(*refs):
    notes, most = refs[:-1], refs[-1]
    highest = notes[0][...].astype(f32)
    for note in notes[1:]:
        highest = jnp.maximum(highest, note[...].astype(f32))
    most[0, 0] = jnp.max(highest[3:4]).astype(jnp.int32)


def most_cameras(extras, rows):
    return pl.pallas_call(
        most_kernel,
        grid=(1,),
        in_specs=[pl.BlockSpec((rows, LANES), lambda i: (2, 0))] * len(extras),
        out_specs=pl.BlockSpec(memory_space=pltpu.SMEM),
        out_shape=jax.ShapeDtypeStruct((1, 1), jnp.int32),
        compiler_params=pltpu.CompilerParams(vmem_limit_bytes=4 * 2**20),
        name="most_cameras",
    )(*extras)[0, 0]


def assemble_kernel(rows, select, share, *refs):
    pieces = len(refs) - 3
    parts, (flat, partial, scaled) = refs[:pieces], refs[pieces:]
    size, width = parts[0].shape
    tall = CAMS * rows
    for place, part in enumerate(parts):
        edges = part[: 2 * rows, :].astype(f32) * share[place].reshape(2 * rows, width)
        scaled[place, : 2 * rows, :] = edges.astype(bf16)
    total = jnp.zeros((tall, 1), f32)
    for block in range(width // (2 * LANES)):
        cols = slice(block * 2 * LANES, (block + 1) * 2 * LANES)
        joined = jnp.zeros((tall, 2 * LANES), f32)
        for place, part in enumerate(parts):
            source = jnp.concatenate([scaled[place, :, cols], part[2 * rows :, cols]], axis=0)
            joined = joined + jnp.dot(
                select[place, :, :size], source, preferred_element_type=f32
            )
        flat[:, cols] = joined.astype(bf16)
        total = total + jnp.sum(joined, axis=1, keepdims=True)
    gram = lax.dot_general(
        flat[...], flat[...], (((1,), (1,)), ((), ())), preferred_element_type=f32
    )
    sub = lax.broadcasted_iota(jnp.int32, (tall, tall), 0)
    lane = lax.broadcasted_iota(jnp.int32, (tall, tall), 1)
    gram = jnp.where((sub & (rows - 1)) == (lane & (rows - 1)), gram, 0.0)
    gram = jnp.sum(gram.reshape(CAMS, rows, tall), axis=1)
    sub = lax.broadcasted_iota(jnp.int32, (tall, LANES), 0)
    lane = lax.broadcasted_iota(jnp.int32, (tall, LANES), 1)
    gather = jnp.where((sub >> log2(rows)) == lane, 1.0, 0.0).astype(f32)
    gram = jnp.dot(gram, gather, precision=lax.Precision.HIGHEST, preferred_element_type=f32)
    total = jnp.sum(total.reshape(CAMS, rows, 1), axis=1)
    lane = lax.broadcasted_iota(jnp.int32, (CAMS, LANES), 1)
    partial[...] = jnp.where(lane == CAMS, total, gram)


def assemble(select, share, parts, rows):
    width = parts[0].shape[1]
    return pl.pallas_call(
        functools.partial(assemble_kernel, rows),
        out_shape=[
            jax.ShapeDtypeStruct((CAMS * rows, width), bf16),
            jax.ShapeDtypeStruct((CAMS, LANES), f32),
        ],
        scratch_shapes=[
            pltpu.VMEM((len(parts), 2 * rows, width), bf16),
        ],
        compiler_params=pltpu.CompilerParams(vmem_limit_bytes=20 * 2**20),
        cost_estimate=pl.CostEstimate(
            flops=2 * 10**9, bytes_accessed=4 * 2**20, transcendentals=0
        ),
        name="assemble",
    )(select, share, *parts)


def correlate_kernel(pixels, *refs):
    parts, out = refs[:-1], refs[-1]
    whole = parts[0][...]
    for part in parts[1:]:
        whole = whole + part[...]
    gram = whole[:, :CAMS]
    mean = whole[:, CAMS : CAMS + 1] / pixels
    sub = lax.broadcasted_iota(jnp.int32, (CAMS, CAMS), 0)
    lane = lax.broadcasted_iota(jnp.int32, (CAMS, CAMS), 1)
    diagonal = sub == lane
    mean_row = jnp.sum(jnp.where(diagonal, mean, 0.0), axis=0, keepdims=True)
    covar = gram / pixels - mean * mean_row
    only = jnp.where(diagonal, covar, 0.0)
    spread = jnp.sum(only, axis=1, keepdims=True) + var_eps
    spread_row = jnp.sum(only, axis=0, keepdims=True) + var_eps
    out[...] = covar / jnp.sqrt(spread * spread_row)


def correlate(parts, pixels):
    return pl.pallas_call(
        functools.partial(correlate_kernel, pixels),
        out_shape=jax.ShapeDtypeStruct((CAMS, CAMS), f32),
        compiler_params=pltpu.CompilerParams(vmem_limit_bytes=4 * 2**20),
        name="correlate",
    )(*parts)


def exchange(array, axis, distance):
    size = lax.axis_size(axis)
    return lax.ppermute(array, axis, [(i, i ^ distance) for i in range(size)])


def summed(array, axis, distances):
    terms = [array] + [exchange(array, axis, distance) for distance in distances]
    while len(terms) > 1:
        terms = [terms[i] + terms[i + 1] for i in range(0, len(terms), 2)]
    return terms[0]


def on_device(photos, camera_id):
    count, rows, width = photos.shape
    pieces, tiles = lax.axis_size("photo"), lax.axis_size("tile")
    me = lax.axis_index("photo").astype(jnp.int32)
    own, up, down, *extras = prepare(me.reshape(1), camera_id, photos, pieces)
    above = lax.ppermute(down, "tile", [(i, i + 1) for i in range(tiles - 1)])
    below = lax.ppermute(up, "tile", [(i + 1, i) for i in range(tiles - 1)])
    extras = [
        exchange(extra, "photo", distance) if distance else extra
        for distance, extra in enumerate(extras)
    ]
    inverse, select, box, merge = energies(camera_id, own, rows)

    def finish(slots):
        parts = [None] * pieces
        for distance in reversed(range(0, pieces, 2)):
            where = jnp.stack([(me ^ distance) >> 1, me & 1])
            pair = main_part(
                where, own, above, below, inverse, select, box, merge, rows, pieces, slots
            )
            for part, apart in zip(pair, (distance + 1, distance)):
                parts[apart] = exchange(part, "photo", apart) if apart else part
        place, share = blend(me.reshape(1), extras, rows, count * rows)
        return assemble(place, share, parts, rows)

    most = most_cameras(extras, rows)
    sizes = sorted({max(2, count * part // 16) for part in (9, 10, 12, 16)})
    branch = sum((most > size).astype(jnp.int32) for size in sizes[:-1])
    flat, partial = lax.switch(branch, [functools.partial(finish, size) for size in sizes])
    flat, partial = lax.optimization_barrier((flat, partial))
    prints = flat.reshape(CAMS, rows, width // pieces).astype(f32)

    total = summed(partial, "tile", (1,))
    total = summed(total, "photo", range(1, pieces))
    total = summed(total, "tile", range(2, tiles, 2))
    return prints, correlate([total], float(rows * tiles * width))


def solution(mesh):
    return jax.shard_map(
        on_device,
        mesh=mesh,
        in_specs=(P("photo", "tile", None), P("photo")),
        out_specs=(P(None, "tile", "photo"), P()),
        check_vma=False,
    )
```

```python
import functools

import jax
import jax.numpy as jnp
from jax import lax
from jax.experimental import pallas as pl
from jax.experimental.pallas import tpu as pltpu
from jax.sharding import PartitionSpec as P

CAMS = 32
RADII = 4
FINE = 2
LANES = 128

noise_power = 1.0
var_eps = 1e-06

f32 = jnp.float32
bf16 = jnp.bfloat16


def log2(value):
    return value.bit_length() - 1


def indicator(condition):
    return jnp.where(condition, 1.0, 0.0).astype(bf16)


def iotas(shape):
    return (
        lax.broadcasted_iota(jnp.int32, shape, len(shape) - 2),
        lax.broadcasted_iota(jnp.int32, shape, len(shape) - 1),
    )


def row_permutation(photos, rows):
    sub, lane = iotas((photos * rows, photos * rows))
    same_row = (sub >> log2(photos)) == (lane & (rows - 1))
    same_photo = (sub & (photos - 1)) == (lane >> log2(rows))
    return indicator(same_row & same_photo)


def column_split():
    sub, lane = iotas((2 * LANES, 2 * LANES))
    return indicator(sub == 2 * (lane & (LANES - 1)) + (lane >> log2(LANES)))


def column_merge():
    sub, lane = iotas((2 * LANES, 2 * LANES))
    return indicator(lane == 2 * (sub & (LANES - 1)) + (sub >> log2(LANES)))


def box_matrix(radius):
    sub, lane = iotas((4 * LANES, 2 * LANES))
    return indicator(jnp.abs(sub - LANES - lane) <= radius)


def haar_rows(even0, odd0, even1, odd1):
    low0, low1 = even0 + odd0, even1 + odd1
    high0, high1 = even0 - odd0, even1 - odd1
    return (low0 - low1, high0 + high1, high0 - high1)


def halves(value):
    upper = value.astype(bf16)
    lower = (value - upper.astype(f32)).astype(bf16)
    return upper, lower


def inverted(value):
    guess = pl.reciprocal(value, approx=True)
    return guess * (2.0 - value * guess)


def slot_numbers(ids, count):
    ranks = [jnp.int32(0)]
    for photo in range(1, count):
        ranks.append(ranks[-1] + jnp.where(ids[photo] != ids[photo - 1], 1, 0))
    last = ranks[-1]
    slots = [jnp.where(rank == 0, 0, jnp.where(rank == last, 1, rank + 1)) for rank in ranks]
    return slots, last + 1


def prepare_kernel(me, ids, photos, sorted_out, up_out, down_out, *refs):
    extras, (buffer, by_row, arrived) = refs[:-3], refs[-3:]
    count, rows, width = photos.shape
    cells = rows // 2
    pieces = len(extras)
    step = width // pieces
    for distance in range(pieces):
        cols = pl.ds(pl.multiple_of((me[0] ^ distance) * step, step), step)
        pltpu.make_async_copy(
            photos.at[:, :, cols], buffer.at[distance], arrived.at[distance]
        ).start()
    perm = row_permutation(count, rows)
    split = column_split()

    slots, cameras = slot_numbers(ids, count)
    sub, lane = iotas((rows, step))
    slot_id = jnp.full((rows, step), -1, jnp.int32)
    in_first, in_last = jnp.int32(0), jnp.int32(0)
    for photo in range(count):
        slot_id = jnp.where((lane >> log2(rows)) == slots[photo], ids[photo], slot_id)
        in_first = in_first + jnp.where(ids[photo] == ids[0], 1, 0)
        in_last = in_last + jnp.where(ids[photo] == ids[count - 1], 1, 0)
    notes = jnp.where(sub == 0, ids[0], jnp.where(sub == 1, ids[count - 1], slot_id))
    notes = jnp.where(sub == 3, cameras, notes).astype(f32).astype(bf16)

    @pl.loop(0, pieces)
    def _(distance):
        piece = me[0] ^ distance
        cols = pl.ds(pl.multiple_of(piece * step, step), step)
        pltpu.make_async_copy(
            photos.at[:, :, cols], buffer.at[distance], arrived.at[distance]
        ).wait()
        flat = buffer[distance].reshape(count * rows, step)
        by_row[...] = jnp.dot(perm, flat, preferred_element_type=f32).astype(bf16)

        @pl.loop(0, step // (2 * LANES))
        def _(inner):
            block = piece * (step // (2 * LANES)) + inner
            cols = pl.ds(pl.multiple_of(block * 2 * LANES, 2 * LANES), 2 * LANES)
            cell_cols = pl.ds(pl.multiple_of(block * LANES, LANES), LANES)
            local = pl.ds(pl.multiple_of(inner * 2 * LANES, 2 * LANES), 2 * LANES)
            parted = jnp.dot(by_row[:, local], split, preferred_element_type=f32)
            sorted_out[:, cols] = parted.astype(bf16)
            for i in range(cells):
                if RADII <= i < cells - RADII:
                    continue
                top = parted[2 * i * count : (2 * i + 1) * count]
                low = parted[(2 * i + 1) * count : (2 * i + 2) * count]
                bands = haar_rows(top[:, :LANES], top[:, LANES:], low[:, :LANES], low[:, LANES:])
                for band in range(3):
                    square = (bands[band] * bands[band]).astype(bf16)
                    if i < RADII:
                        start = (band * RADII + i) * count
                        up_out[start : start + count, cell_cols] = square
                    if i >= cells - RADII:
                        start = (band * RADII + i - (cells - RADII)) * count
                        down_out[start : start + count, cell_cols] = square

    none = jnp.zeros((rows, step), f32)
    for distance, extra in enumerate(extras):

        def add(photo, total):
            pixel = buffer[distance, photo].astype(f32)
            return total + pixel * pixel

        extra[:rows, :] = lax.fori_loop(0, in_first, add, none).astype(bf16)
        extra[rows : 2 * rows, :] = lax.fori_loop(count - in_last, count, add, none).astype(bf16)
        extra[2 * rows :, :] = notes


def prepare(me, ids, photos, pieces):
    count, rows, width = photos.shape
    step = width // pieces
    size = count * rows
    halo = 3 * RADII * count
    vmem = pl.BlockSpec(memory_space=pltpu.VMEM)
    smem = pl.BlockSpec(memory_space=pltpu.SMEM)
    return pl.pallas_call(
        prepare_kernel,
        in_specs=[smem, smem, pl.BlockSpec(memory_space=pltpu.HBM)],
        out_specs=[vmem] * (3 + pieces),
        out_shape=[
            jax.ShapeDtypeStruct((size, width), bf16),
            jax.ShapeDtypeStruct((halo, width // 2), bf16),
            jax.ShapeDtypeStruct((halo, width // 2), bf16),
        ]
        + [jax.ShapeDtypeStruct((3 * rows, step), bf16)] * pieces,
        scratch_shapes=[
            pltpu.VMEM((pieces, count, rows, step), bf16),
            pltpu.VMEM((size, step), bf16),
            pltpu.SemaphoreType.DMA((pieces,)),
        ],
        compiler_params=pltpu.CompilerParams(vmem_limit_bytes=20 * 2**20),
        cost_estimate=pl.CostEstimate(flops=10**9, bytes_accessed=8 * 2**20, transcendentals=0),
        name="prepare",
    )(me, ids, photos)


def energy_kernel(count, rows, ids, own, inverse, select_out, box_out, merge_out):
    size, width = own.shape
    slots, _ = slot_numbers(ids, count)
    sub, lane = iotas((size, size))
    lane_photo = lane & (count - 1)
    lane_slot = jnp.zeros_like(lane)
    for photo in range(count):
        lane_slot = jnp.where(lane_photo == photo, slots[photo], lane_slot)
    in_slot = lane_slot == (sub >> log2(rows))
    same_row = (sub & (rows - 1)) == (lane >> log2(count))
    select = indicator(in_slot & same_row)
    select = jnp.concatenate([select, select], axis=1)
    select_out[...] = select
    for radius in range(1, RADII + 1):
        box_out[radius - 1] = box_matrix(radius)
    merge_out[...] = column_merge()

    @pl.loop(0, width // (2 * LANES))
    def _(block):
        cols = pl.ds(pl.multiple_of(block * 2 * LANES, 2 * LANES), 2 * LANES)
        pixel = own[:, cols].astype(f32)
        pair = jnp.concatenate(halves(pixel * pixel), axis=0)
        energy = jnp.dot(select, pair, preferred_element_type=f32)
        inverse[:, cols] = inverted(jnp.maximum(energy, 2.0**-20))


def energies(ids, own, rows):
    size, width = own.shape
    vmem = pl.BlockSpec(memory_space=pltpu.VMEM)
    smem = pl.BlockSpec(memory_space=pltpu.SMEM)
    return pl.pallas_call(
        functools.partial(energy_kernel, size // rows, rows),
        in_specs=[smem, vmem],
        out_specs=[vmem] * 4,
        out_shape=[
            jax.ShapeDtypeStruct((size, width), f32),
            jax.ShapeDtypeStruct((size, 2 * size), bf16),
            jax.ShapeDtypeStruct((RADII, 4 * LANES, 2 * LANES), bf16),
            jax.ShapeDtypeStruct((2 * LANES, 2 * LANES), bf16),
        ],
        compiler_params=pltpu.CompilerParams(vmem_limit_bytes=20 * 2**20),
        cost_estimate=pl.CostEstimate(flops=10**9, bytes_accessed=8 * 2**20, transcendentals=0),
        name="energies",
    )(ids, own)


def blend_kernel(rows, me, *refs):
    pieces = len(refs) - 3
    extras, (select, share, held) = refs[:pieces], refs[pieces:]
    size = select.shape[2]
    tall = CAMS * rows
    sub, lane = iotas((tall, size))
    same_row = (sub & (rows - 1)) == (lane & (rows - 1))
    camera = (sub >> log2(rows)).astype(f32)
    for distance, extra in enumerate(extras):
        notes = extra[2 * rows :, :].astype(f32)
        select[distance] = indicator((camera == notes[2:3, :size]) & same_row)
        held[me[0] ^ distance] = extra[...].astype(f32)
    ones = jnp.ones((rows, share.shape[3]), f32)
    for device in range(pieces):
        if device == 0:
            share[me[0] ^ device, 0] = ones
        if device == pieces - 1:
            share[me[0] ^ device, 1] = ones
            continue
        late = held[device, rows : 2 * rows]
        early = held[device + 1, :rows]
        crosses = held[device, 2 * rows + 1 : 2 * rows + 2] == held[device + 1, 2 * rows : 2 * rows + 1]
        joint = 1.0 / (late + early)
        share[me[0] ^ device, 1] = jnp.where(crosses, late * joint, 1.0)
        share[me[0] ^ (device + 1), 0] = jnp.where(crosses, early * joint, 1.0)


def blend(me, extras, rows, size):
    pieces, width = len(extras), extras[0].shape[1]
    vmem = pl.BlockSpec(memory_space=pltpu.VMEM)
    smem = pl.BlockSpec(memory_space=pltpu.SMEM)
    return pl.pallas_call(
        functools.partial(blend_kernel, rows),
        in_specs=[smem] + [vmem] * pieces,
        out_specs=[vmem, vmem],
        out_shape=[
            jax.ShapeDtypeStruct((pieces, CAMS * rows, size), bf16),
            jax.ShapeDtypeStruct((pieces, 2, rows, width), f32),
        ],
        scratch_shapes=[pltpu.VMEM((pieces, 3 * rows, width), f32)],
        compiler_params=pltpu.CompilerParams(vmem_limit_bytes=20 * 2**20),
        name="blend",
    )(me, *extras)


def main_kernel(
    count, rows, chunk, own_all, above_all, below_all, inverse, select, box, merge, out,
    own, above, below, sums, rest, least, product, scale, select_in, box_in, merge_in,
    arrived, ready,
):
    cells = rows // 2
    size = count * rows
    width = out.shape[1]
    blocks = width // (2 * LANES)
    slot_rows = out.shape[0]
    base = chunk[0] * width
    inner = []
    edges = ([], [])
    for at, (whole, local, lanes) in enumerate(
        ((own_all, own, 2 * LANES), (above_all, above, LANES), (below_all, below, LANES))
    ):
        length = blocks * lanes
        start = chunk[0] * length
        for place, size_here, offset, group in (
            (start, length, lanes, inner),
            (jnp.maximum(start - lanes, 0), lanes, 0, edges[0]),
            (jnp.minimum(start + length, whole.shape[1] - lanes), lanes, lanes + length, edges[1]),
        ):
            index = 3 * at + (0 if group is inner else 1 if group is edges[0] else 2)
            group.append(
                pltpu.make_async_copy(
                    whole.at[:, pl.ds(pl.multiple_of(place, lanes), size_here)],
                    local.at[:, pl.ds(offset, size_here)],
                    arrived.at[index],
                )
            )
    late = [
        pltpu.make_async_copy(box, box_in, ready.at[0]),
        pltpu.make_async_copy(select.at[pl.ds(0, slot_rows)], select_in, ready.at[1]),
        pltpu.make_async_copy(
            inverse.at[pl.ds(0, slot_rows), pl.ds(pl.multiple_of(base, width), width)],
            scale,
            ready.at[2],
        ),
        pltpu.make_async_copy(merge, merge_in, ready.at[3]),
    ]
    for copy in inner + edges[0] + edges[1] + late:
        copy.start()

    def pixels_of(i, start):
        top = slice(2 * i * count, (2 * i + 1) * count)
        low = slice((2 * i + 1) * count, (2 * i + 2) * count)
        even = pl.ds(pl.multiple_of(start, 2 * LANES), LANES)
        odd = pl.ds(pl.multiple_of(start + LANES, LANES), LANES)
        return tuple(
            own[at, cols].astype(f32)
            for at, cols in ((top, even), (top, odd), (low, even), (low, odd))
        )

    def add_up(block, fine):
        cols = pl.ds(pl.multiple_of(block * LANES, LANES), LANES)
        squares = [[], [], []]
        for i in range(cells):
            bands = haar_rows(*pixels_of(i, block * 2 * LANES))
            for band in range(3):
                squares[band].append(bands[band] * bands[band])
        for band in range(3):
            first = band * RADII * count
            over, under = (
                [
                    halo[first + i * count : first + (i + 1) * count, cols].astype(f32)
                    for i in range(RADII)
                ]
                for halo in (above, below)
            )
            column = over + squares[band] + under
            for i in range(cells):
                total = column[i + RADII]
                at_row = (band * cells + i) * count
                for radius in range(1, RADII + 1):
                    total = total + (column[i + RADII - radius] + column[i + RADII + radius])
                    upper = total.astype(bf16)
                    sums[radius - 1, at_row : at_row + count, cols] = upper
                    if radius <= FINE and fine:
                        lower = (total - upper.astype(f32)).astype(bf16)
                        rest[radius - 1, at_row : at_row + count, cols] = lower

    for copy in inner:
        copy.wait()

    @pl.loop(1, blocks + 1)
    def _(block):
        add_up(block, True)

    for copy in edges[0] + edges[1]:
        copy.wait()

    @pl.loop(0, 2)
    def _(side):
        add_up(side * (blocks + 1), False)

    for side, outside in enumerate((base == 0, base + width == own_all.shape[1])):

        @pl.when(outside)
        def _():
            at = side * (blocks + 1) * LANES
            sums[:, :, at : at + LANES] = jnp.zeros(sums.shape[:2] + (LANES,), bf16)

    late[0].wait()

    @pl.loop(0, blocks // 2)
    def _(group):
        first = pl.multiple_of(group * 2 * LANES, 2 * LANES)
        window = pl.ds(first, 4 * LANES)
        middle = pl.ds(pl.multiple_of(first + LANES, LANES), 2 * LANES)
        for radius in range(1, RADII + 1):
            narrow, weights = sums[radius - 1, :, window], box_in[radius - 1]
            if radius <= FINE:
                narrow = jnp.concatenate([narrow, rest[radius - 1, :, middle]], axis=1)
                weights = jnp.concatenate([weights, weights[LANES : 3 * LANES]], axis=0)
            wide = jnp.dot(narrow, weights, preferred_element_type=f32)
            mean = wide * (1.0 / float((2 * radius + 1) ** 2))
            least[...] = mean if radius == 1 else jnp.minimum(least[...], mean)

        for half in range(2):
            start = pl.multiple_of((2 * group + half) * 2 * LANES, 2 * LANES)
            even = pl.ds(start, LANES)
            odd = pl.ds(pl.multiple_of(start + LANES, LANES), LANES)
            lanes = slice(half * LANES, (half + 1) * LANES)
            for i in range(cells):
                top, low = 2 * i * count, (2 * i + 1) * count
                pixels = pixels_of(i, start + 2 * LANES)
                bands = haar_rows(*pixels)
                shrunk = []
                for band in range(3):
                    at_row = (band * cells + i) * count
                    variance = least[at_row : at_row + count, lanes]
                    bound = jnp.maximum(variance, 4.0 * noise_power)
                    shrunk.append(bands[band] * (noise_power * inverted(bound)))
                horiz, vertic, diagon = shrunk
                both, cross = vertic + diagon, vertic - diagon
                noise = (horiz + both, horiz - both, cross - horiz, -horiz - cross)
                for at, cols, pixel, part in zip(
                    (top, top, low, low), (even, odd, even, odd), pixels, noise
                ):
                    upper, lower = halves(part.astype(bf16).astype(f32) * pixel)
                    product[at : at + count, cols] = upper
                    product[size + at : size + at + count, cols] = lower

    for copy in late[1:]:
        copy.wait()

    @pl.loop(0, blocks)
    def _(block):
        cols = pl.ds(pl.multiple_of(block * 2 * LANES, 2 * LANES), 2 * LANES)
        weighted = jnp.dot(select_in[...], product[:, cols], preferred_element_type=f32)
        part = (weighted * scale[:, cols]).astype(bf16)
        out[:, cols] = jnp.dot(part, merge_in[...], preferred_element_type=f32).astype(bf16)


def main_part(chunk, own, above, below, inverse, select, box, merge, rows, pieces, slots):
    size, width_all = own.shape
    count = size // rows
    width = width_all // pieces
    halo = above.shape[0]
    cell_rows = 3 * (rows // 2) * count
    return pl.pallas_call(
        functools.partial(main_kernel, count, rows),
        in_specs=[pl.BlockSpec(memory_space=pltpu.SMEM)] + [pl.BlockSpec(memory_space=pl.ANY)] * 7,
        out_specs=pl.BlockSpec(memory_space=pltpu.VMEM),
        scratch_shapes=[
            pltpu.VMEM((size, width + 4 * LANES), bf16),
            pltpu.VMEM((halo, width // 2 + 2 * LANES), bf16),
            pltpu.VMEM((halo, width // 2 + 2 * LANES), bf16),
            pltpu.VMEM((RADII, cell_rows, width // 2 + 2 * LANES), bf16),
            pltpu.VMEM((FINE, cell_rows, width // 2 + 2 * LANES), bf16),
            pltpu.VMEM((cell_rows, 2 * LANES), f32),
            pltpu.VMEM((2 * size, width), bf16),
            pltpu.VMEM((slots * rows, width), f32),
            pltpu.VMEM((slots * rows, 2 * size), bf16),
            pltpu.VMEM((RADII, 4 * LANES, 2 * LANES), bf16),
            pltpu.VMEM((2 * LANES, 2 * LANES), bf16),
            pltpu.SemaphoreType.DMA((9,)),
            pltpu.SemaphoreType.DMA((4,)),
        ],
        out_shape=jax.ShapeDtypeStruct((slots * rows, width), bf16),
        compiler_params=pltpu.CompilerParams(vmem_limit_bytes=20 * 2**20),
        cost_estimate=pl.CostEstimate(
            flops=2 * 10**9, bytes_accessed=4 * 2**20, transcendentals=0
        ),
        name="residual",
    )(chunk, own, above, below, inverse, select, box, merge)


def most_kernel(*refs):
    notes, most = refs[:-1], refs[-1]
    highest = notes[0][...].astype(f32)
    for note in notes[1:]:
        highest = jnp.maximum(highest, note[...].astype(f32))
    most[0, 0] = jnp.max(highest[3:4]).astype(jnp.int32)


def most_cameras(extras, rows):
    return pl.pallas_call(
        most_kernel,
        grid=(1,),
        in_specs=[pl.BlockSpec((rows, LANES), lambda i: (2, 0))] * len(extras),
        out_specs=pl.BlockSpec(memory_space=pltpu.SMEM),
        out_shape=jax.ShapeDtypeStruct((1, 1), jnp.int32),
        compiler_params=pltpu.CompilerParams(vmem_limit_bytes=4 * 2**20),
        name="most_cameras",
    )(*extras)[0, 0]


def assemble_kernel(rows, select, share, *refs):
    pieces = len(refs) - 4
    parts, (flat, partial, scaled, total) = refs[:pieces], refs[pieces:]
    size, width = parts[0].shape
    tall = CAMS * rows
    for place, part in enumerate(parts):
        edges = part[: 2 * rows, :].astype(f32) * share[place].reshape(2 * rows, width)
        scaled[place, : 2 * rows, :] = edges.astype(bf16)
    total[...] = jnp.zeros((tall, LANES), f32)

    @pl.loop(0, width // (2 * LANES))
    def _(block):
        cols = pl.ds(pl.multiple_of(block * 2 * LANES, 2 * LANES), 2 * LANES)
        joined = jnp.zeros((tall, 2 * LANES), f32)
        for place, part in enumerate(parts):
            source = jnp.concatenate([scaled[place, :, cols], part[2 * rows :, cols]], axis=0)
            joined = joined + jnp.dot(
                select[place, :, :size], source, preferred_element_type=f32
            )
        flat[:, cols] = joined.astype(bf16)
        total[...] += joined[:, :LANES] + joined[:, LANES:]

    gram = lax.dot_general(
        flat[...], flat[...], (((1,), (1,)), ((), ())), preferred_element_type=f32
    )
    sub = lax.broadcasted_iota(jnp.int32, (tall, tall), 0)
    lane = lax.broadcasted_iota(jnp.int32, (tall, tall), 1)
    gram = jnp.where((sub & (rows - 1)) == (lane & (rows - 1)), gram, 0.0)
    gram = jnp.sum(gram.reshape(CAMS, rows, tall), axis=1)
    sub = lax.broadcasted_iota(jnp.int32, (tall, LANES), 0)
    lane = lax.broadcasted_iota(jnp.int32, (tall, LANES), 1)
    gather = jnp.where((sub >> log2(rows)) == lane, 1.0, 0.0).astype(f32)
    gram = jnp.dot(gram, gather, precision=lax.Precision.HIGHEST, preferred_element_type=f32)
    sums = jnp.sum(total[...], axis=1, keepdims=True)
    sums = jnp.sum(sums.reshape(CAMS, rows, 1), axis=1)
    lane = lax.broadcasted_iota(jnp.int32, (CAMS, LANES), 1)
    partial[...] = jnp.where(lane == CAMS, sums, gram)


def assemble(select, share, parts, rows):
    width = parts[0].shape[1]
    return pl.pallas_call(
        functools.partial(assemble_kernel, rows),
        out_shape=[
            jax.ShapeDtypeStruct((CAMS * rows, width), bf16),
            jax.ShapeDtypeStruct((CAMS, LANES), f32),
        ],
        scratch_shapes=[
            pltpu.VMEM((len(parts), 2 * rows, width), bf16),
            pltpu.VMEM((CAMS * rows, LANES), f32),
        ],
        compiler_params=pltpu.CompilerParams(vmem_limit_bytes=20 * 2**20),
        cost_estimate=pl.CostEstimate(
            flops=2 * 10**9, bytes_accessed=4 * 2**20, transcendentals=0
        ),
        name="assemble",
    )(select, share, *parts)


def correlate_kernel(pixels, *refs):
    parts, out = refs[:-1], refs[-1]
    whole = parts[0][...]
    for part in parts[1:]:
        whole = whole + part[...]
    gram = whole[:, :CAMS]
    mean = whole[:, CAMS : CAMS + 1] / pixels
    sub = lax.broadcasted_iota(jnp.int32, (CAMS, CAMS), 0)
    lane = lax.broadcasted_iota(jnp.int32, (CAMS, CAMS), 1)
    diagonal = sub == lane
    mean_row = jnp.sum(jnp.where(diagonal, mean, 0.0), axis=0, keepdims=True)
    covar = gram / pixels - mean * mean_row
    only = jnp.where(diagonal, covar, 0.0)
    spread = jnp.sum(only, axis=1, keepdims=True) + var_eps
    spread_row = jnp.sum(only, axis=0, keepdims=True) + var_eps
    out[...] = covar / jnp.sqrt(spread * spread_row)


def correlate(parts, pixels):
    return pl.pallas_call(
        functools.partial(correlate_kernel, pixels),
        out_shape=jax.ShapeDtypeStruct((CAMS, CAMS), f32),
        compiler_params=pltpu.CompilerParams(vmem_limit_bytes=4 * 2**20),
        name="correlate",
    )(*parts)


def exchange(array, axis, distance):
    size = lax.axis_size(axis)
    return lax.ppermute(array, axis, [(i, i ^ distance) for i in range(size)])


def summed(array, axis, distances):
    terms = [array] + [exchange(array, axis, distance) for distance in distances]
    while len(terms) > 1:
        terms = [terms[i] + terms[i + 1] for i in range(0, len(terms), 2)]
    return terms[0]


def on_device(photos, camera_id):
    count, rows, width = photos.shape
    pieces, tiles = lax.axis_size("photo"), lax.axis_size("tile")
    me = lax.axis_index("photo").astype(jnp.int32)
    own, up, down, *extras = prepare(me.reshape(1), camera_id, photos, pieces)
    above = lax.ppermute(down, "tile", [(i, i + 1) for i in range(tiles - 1)])
    below = lax.ppermute(up, "tile", [(i + 1, i) for i in range(tiles - 1)])
    extras = [
        exchange(extra, "photo", distance) if distance else extra
        for distance, extra in enumerate(extras)
    ]
    inverse, select, box, merge = energies(camera_id, own, rows)

    def finish(slots):
        parts = [None] * pieces
        for distance in reversed(range(pieces)):
            part = main_part(
                (me ^ distance).reshape(1), own, above, below, inverse, select, box, merge,
                rows, pieces, slots,
            )
            parts[distance] = exchange(part, "photo", distance) if distance else part
        place, share = blend(me.reshape(1), extras, rows, count * rows)
        return assemble(place, share, parts, rows)

    most = most_cameras(extras, rows)
    sizes = sorted({max(2, count * part // 16) for part in (10, 12, 16)})
    branch = sum((most > size).astype(jnp.int32) for size in sizes[:-1])
    flat, partial = lax.switch(branch, [functools.partial(finish, size) for size in sizes])
    flat, partial = lax.optimization_barrier((flat, partial))
    prints = flat.reshape(CAMS, rows, width // pieces).astype(f32)

    total = summed(partial, "tile", (1,))
    total = summed(total, "photo", range(1, pieces))
    total = summed(total, "tile", range(2, tiles, 2))
    return prints, correlate([total], float(rows * tiles * width))


def solution(mesh):
    return jax.shard_map(
        on_device,
        mesh=mesh,
        in_specs=(P("photo", "tile", None), P("photo")),
        out_specs=(P(None, "tile", "photo"), P()),
        check_vma=False,
    )
```

```python
import functools

import jax
import jax.numpy as jnp
from jax import lax
from jax.experimental import pallas as pl
from jax.experimental.pallas import tpu as pltpu
from jax.sharding import PartitionSpec as P

CAMS = 32
RADII = 4
FINE = 2
LANES = 128

noise_power = 1.0
var_eps = 1e-06

f32 = jnp.float32
bf16 = jnp.bfloat16


def log2(value):
    return value.bit_length() - 1


def indicator(condition):
    return jnp.where(condition, 1.0, 0.0).astype(bf16)


def iotas(shape):
    return (
        lax.broadcasted_iota(jnp.int32, shape, len(shape) - 2),
        lax.broadcasted_iota(jnp.int32, shape, len(shape) - 1),
    )


def row_permutation(photos, rows):
    sub, lane = iotas((photos * rows, photos * rows))
    same_row = (sub >> log2(photos)) == (lane & (rows - 1))
    same_photo = (sub & (photos - 1)) == (lane >> log2(rows))
    return indicator(same_row & same_photo)


def column_split():
    sub, lane = iotas((2 * LANES, 2 * LANES))
    return indicator(sub == 2 * (lane & (LANES - 1)) + (lane >> log2(LANES)))


def column_merge():
    sub, lane = iotas((2 * LANES, 2 * LANES))
    return indicator(lane == 2 * (sub & (LANES - 1)) + (sub >> log2(LANES)))


def box_matrix(radius):
    sub, lane = iotas((4 * LANES, 2 * LANES))
    return indicator(jnp.abs(sub - LANES - lane) <= radius)


def haar_rows(even0, odd0, even1, odd1):
    low0, low1 = even0 + odd0, even1 + odd1
    high0, high1 = even0 - odd0, even1 - odd1
    return (low0 - low1, high0 + high1, high0 - high1)


def halves(value):
    upper = value.astype(bf16)
    lower = (value - upper.astype(f32)).astype(bf16)
    return upper, lower


def inverted(value):
    guess = pl.reciprocal(value, approx=True)
    return guess * (2.0 - value * guess)


def slot_numbers(ids, count):
    ranks = [jnp.int32(0)]
    for photo in range(1, count):
        ranks.append(ranks[-1] + jnp.where(ids[photo] != ids[photo - 1], 1, 0))
    last = ranks[-1]
    slots = [jnp.where(rank == 0, 0, jnp.where(rank == last, 1, rank + 1)) for rank in ranks]
    return slots, last + 1


def prepare_kernel(me, ids, photos, sorted_out, up_out, down_out, *extras):
    count, rows, width = photos.shape
    cells = rows // 2
    pieces = len(extras)
    step = width // pieces
    perm = row_permutation(count, rows)
    split = column_split()

    slots, cameras = slot_numbers(ids, count)
    sub, lane = iotas((rows, step))
    slot_id = jnp.full((rows, step), -1, jnp.int32)
    in_first, in_last = jnp.int32(0), jnp.int32(0)
    for photo in range(count):
        slot_id = jnp.where((lane >> log2(rows)) == slots[photo], ids[photo], slot_id)
        in_first = in_first + jnp.where(ids[photo] == ids[0], 1, 0)
        in_last = in_last + jnp.where(ids[photo] == ids[count - 1], 1, 0)
    notes = jnp.where(sub == 0, ids[0], jnp.where(sub == 1, ids[count - 1], slot_id))
    notes = jnp.where(sub == 3, cameras, notes).astype(f32).astype(bf16)

    for piece in range(pieces):
        flat = photos[:, :, piece * step : (piece + 1) * step].reshape(count * rows, step)
        by_row = jnp.dot(perm, flat, preferred_element_type=f32).astype(bf16)
        for inner in range(step // (2 * LANES)):
            block = piece * (step // (2 * LANES)) + inner
            cols = slice(block * 2 * LANES, (block + 1) * 2 * LANES)
            cell_cols = slice(block * LANES, (block + 1) * LANES)
            pixels = by_row[:, inner * 2 * LANES : (inner + 1) * 2 * LANES]
            parted = jnp.dot(pixels, split, preferred_element_type=f32)
            sorted_out[:, cols] = parted.astype(bf16)
            for i in range(cells):
                if RADII <= i < cells - RADII:
                    continue
                top = parted[2 * i * count : (2 * i + 1) * count]
                low = parted[(2 * i + 1) * count : (2 * i + 2) * count]
                bands = haar_rows(top[:, :LANES], top[:, LANES:], low[:, :LANES], low[:, LANES:])
                for band in range(3):
                    square = (bands[band] * bands[band]).astype(bf16)
                    if i < RADII:
                        start = (band * RADII + i) * count
                        up_out[start : start + count, cell_cols] = square
                    if i >= cells - RADII:
                        start = (band * RADII + i - (cells - RADII)) * count
                        down_out[start : start + count, cell_cols] = square

    none = jnp.zeros((rows, step), f32)
    for distance, extra in enumerate(extras):
        cols = pl.ds(pl.multiple_of((me[0] ^ distance) * step, step), step)

        def add(photo, total):
            pixel = photos[photo, :, cols].astype(f32)
            return total + pixel * pixel

        extra[:rows, :] = lax.fori_loop(0, in_first, add, none).astype(bf16)
        extra[rows : 2 * rows, :] = lax.fori_loop(count - in_last, count, add, none).astype(bf16)
        extra[2 * rows :, :] = notes


def prepare(me, ids, photos, pieces):
    count, rows, width = photos.shape
    step = width // pieces
    size = count * rows
    halo = 3 * RADII * count
    vmem = pl.BlockSpec(memory_space=pltpu.VMEM)
    smem = pl.BlockSpec(memory_space=pltpu.SMEM)
    return pl.pallas_call(
        prepare_kernel,
        in_specs=[smem, smem, vmem],
        out_specs=[vmem] * (3 + pieces),
        out_shape=[
            jax.ShapeDtypeStruct((size, width), bf16),
            jax.ShapeDtypeStruct((halo, width // 2), bf16),
            jax.ShapeDtypeStruct((halo, width // 2), bf16),
        ]
        + [jax.ShapeDtypeStruct((3 * rows, step), bf16)] * pieces,
        compiler_params=pltpu.CompilerParams(vmem_limit_bytes=20 * 2**20),
        cost_estimate=pl.CostEstimate(flops=10**9, bytes_accessed=8 * 2**20, transcendentals=0),
        name="prepare",
    )(me, ids, photos)


def energy_kernel(count, rows, ids, own, inverse, select_out, box_out, merge_out):
    size, width = own.shape
    slots, _ = slot_numbers(ids, count)
    sub, lane = iotas((size, size))
    lane_photo = lane & (count - 1)
    lane_slot = jnp.zeros_like(lane)
    for photo in range(count):
        lane_slot = jnp.where(lane_photo == photo, slots[photo], lane_slot)
    in_slot = lane_slot == (sub >> log2(rows))
    same_row = (sub & (rows - 1)) == (lane >> log2(count))
    select = indicator(in_slot & same_row)
    select = jnp.concatenate([select, select], axis=1)
    select_out[...] = select
    for radius in range(1, RADII + 1):
        box_out[radius - 1] = box_matrix(radius)
    merge_out[...] = column_merge()

    for block in range(width // (2 * LANES)):
        cols = slice(block * 2 * LANES, (block + 1) * 2 * LANES)
        pixel = own[:, cols].astype(f32)
        pair = jnp.concatenate(halves(pixel * pixel), axis=0)
        energy = jnp.dot(select, pair, preferred_element_type=f32)
        inverse[:, cols] = inverted(jnp.maximum(energy, 2.0**-20))


def energies(ids, own, rows):
    size, width = own.shape
    vmem = pl.BlockSpec(memory_space=pltpu.VMEM)
    smem = pl.BlockSpec(memory_space=pltpu.SMEM)
    return pl.pallas_call(
        functools.partial(energy_kernel, size // rows, rows),
        in_specs=[smem, vmem],
        out_specs=[vmem] * 4,
        out_shape=[
            jax.ShapeDtypeStruct((size, width), f32),
            jax.ShapeDtypeStruct((size, 2 * size), bf16),
            jax.ShapeDtypeStruct((RADII, 4 * LANES, 2 * LANES), bf16),
            jax.ShapeDtypeStruct((2 * LANES, 2 * LANES), bf16),
        ],
        compiler_params=pltpu.CompilerParams(vmem_limit_bytes=20 * 2**20),
        cost_estimate=pl.CostEstimate(flops=10**9, bytes_accessed=8 * 2**20, transcendentals=0),
        name="energies",
    )(ids, own)


def blend_kernel(rows, me, *refs):
    pieces = len(refs) - 3
    extras, (select, share, held) = refs[:pieces], refs[pieces:]
    size = select.shape[2]
    tall = CAMS * rows
    sub, lane = iotas((tall, size))
    same_row = (sub & (rows - 1)) == (lane & (rows - 1))
    camera = (sub >> log2(rows)).astype(f32)
    for distance, extra in enumerate(extras):
        notes = extra[2 * rows :, :].astype(f32)
        select[distance] = indicator((camera == notes[2:3, :size]) & same_row)
        held[me[0] ^ distance] = extra[...].astype(f32)
    ones = jnp.ones((rows, share.shape[3]), f32)
    for device in range(pieces):
        if device == 0:
            share[me[0] ^ device, 0] = ones
        if device == pieces - 1:
            share[me[0] ^ device, 1] = ones
            continue
        late = held[device, rows : 2 * rows]
        early = held[device + 1, :rows]
        crosses = held[device, 2 * rows + 1 : 2 * rows + 2] == held[device + 1, 2 * rows : 2 * rows + 1]
        joint = 1.0 / (late + early)
        share[me[0] ^ device, 1] = jnp.where(crosses, late * joint, 1.0)
        share[me[0] ^ (device + 1), 0] = jnp.where(crosses, early * joint, 1.0)


def blend(me, extras, rows, size):
    pieces, width = len(extras), extras[0].shape[1]
    vmem = pl.BlockSpec(memory_space=pltpu.VMEM)
    smem = pl.BlockSpec(memory_space=pltpu.SMEM)
    return pl.pallas_call(
        functools.partial(blend_kernel, rows),
        in_specs=[smem] + [vmem] * pieces,
        out_specs=[vmem, vmem],
        out_shape=[
            jax.ShapeDtypeStruct((pieces, CAMS * rows, size), bf16),
            jax.ShapeDtypeStruct((pieces, 2, rows, width), f32),
        ],
        scratch_shapes=[pltpu.VMEM((pieces, 3 * rows, width), f32)],
        compiler_params=pltpu.CompilerParams(vmem_limit_bytes=20 * 2**20),
        name="blend",
    )(me, *extras)


def main_kernel(
    count, rows, chunk, own_all, above_all, below_all, inverse, select, box, merge, out, other,
    own, above, below, sums, rest, least, product, scale, select_in, box_in, merge_in,
    arrived, ready,
):
    cells = rows // 2
    size = count * rows
    width = out.shape[1]
    blocks = width // (2 * LANES)
    slot_rows = out.shape[0]
    base = chunk[0] * width
    inner = []
    edges = ([], [])
    for at, (whole, local, lanes) in enumerate(
        ((own_all, own, 2 * LANES), (above_all, above, LANES), (below_all, below, LANES))
    ):
        length = blocks * lanes
        start = chunk[0] * length
        for place, size_here, offset, group in (
            (start, length, lanes, inner),
            (jnp.maximum(start - lanes, 0), lanes, 0, edges[0]),
            (jnp.minimum(start + length, whole.shape[1] - lanes), lanes, lanes + length, edges[1]),
        ):
            index = 3 * at + (0 if group is inner else 1 if group is edges[0] else 2)
            group.append(
                pltpu.make_async_copy(
                    whole.at[:, pl.ds(pl.multiple_of(place, lanes), size_here)],
                    local.at[:, pl.ds(offset, size_here)],
                    arrived.at[index],
                )
            )
    late = [
        pltpu.make_async_copy(box, box_in, ready.at[0]),
        pltpu.make_async_copy(select, select_in, ready.at[1]),
        pltpu.make_async_copy(
            inverse.at[:, pl.ds(pl.multiple_of(base, width), width)],
            scale,
            ready.at[2],
        ),
        pltpu.make_async_copy(merge, merge_in, ready.at[3]),
    ]
    for copy in inner + edges[0] + edges[1] + late:
        copy.start()

    def pixels_of(i, start):
        top = slice(2 * i * count, (2 * i + 1) * count)
        low = slice((2 * i + 1) * count, (2 * i + 2) * count)
        even, odd = slice(start, start + LANES), slice(start + LANES, start + 2 * LANES)
        return tuple(
            own[at, cols].astype(f32)
            for at, cols in ((top, even), (top, odd), (low, even), (low, odd))
        )

    def add_up(block, fine):
        cols = slice(block * LANES, (block + 1) * LANES)
        squares = [[], [], []]
        for i in range(cells):
            bands = haar_rows(*pixels_of(i, block * 2 * LANES))
            for band in range(3):
                squares[band].append(bands[band] * bands[band])
        for band in range(3):
            first = band * RADII * count
            over, under = (
                [
                    halo[first + i * count : first + (i + 1) * count, cols].astype(f32)
                    for i in range(RADII)
                ]
                for halo in (above, below)
            )
            column = over + squares[band] + under
            for i in range(cells):
                total = column[i + RADII]
                at_row = (band * cells + i) * count
                for radius in range(1, RADII + 1):
                    total = total + (column[i + RADII - radius] + column[i + RADII + radius])
                    upper = total.astype(bf16)
                    sums[radius - 1, at_row : at_row + count, cols] = upper
                    if radius <= FINE and fine:
                        lower = (total - upper.astype(f32)).astype(bf16)
                        rest[radius - 1, at_row : at_row + count, cols] = lower

    for copy in inner:
        copy.wait()

    for block in range(1, blocks + 1):
        add_up(block, True)

    for copy in edges[0] + edges[1]:
        copy.wait()

    add_up(0, False)
    add_up(blocks + 1, False)

    for side, outside in enumerate((base == 0, base + width == own_all.shape[1])):

        @pl.when(outside)
        def _():
            at = side * (blocks + 1) * LANES
            sums[:, :, at : at + LANES] = jnp.zeros(sums.shape[:2] + (LANES,), bf16)

    late[0].wait()

    for group in range(blocks // 2):
        first = group * 2 * LANES
        window = slice(first, first + 4 * LANES)
        middle = slice(first + LANES, first + 3 * LANES)
        for radius in range(1, RADII + 1):
            narrow, weights = sums[radius - 1, :, window], box_in[radius - 1]
            if radius <= FINE:
                narrow = jnp.concatenate([narrow, rest[radius - 1, :, middle]], axis=1)
                weights = jnp.concatenate([weights, weights[LANES : 3 * LANES]], axis=0)
            wide = jnp.dot(narrow, weights, preferred_element_type=f32)
            mean = wide * (1.0 / float((2 * radius + 1) ** 2))
            least[...] = mean if radius == 1 else jnp.minimum(least[...], mean)

        for half in range(2):
            start = (2 * group + half) * 2 * LANES
            even = slice(start, start + LANES)
            odd = slice(start + LANES, start + 2 * LANES)
            lanes = slice(half * LANES, (half + 1) * LANES)
            for i in range(cells):
                top, low = 2 * i * count, (2 * i + 1) * count
                pixels = pixels_of(i, start + 2 * LANES)
                bands = haar_rows(*pixels)
                shrunk = []
                for band in range(3):
                    at_row = (band * cells + i) * count
                    variance = least[at_row : at_row + count, lanes]
                    bound = jnp.maximum(variance, 4.0 * noise_power)
                    shrunk.append(bands[band] * (noise_power * inverted(bound)))
                horiz, vertic, diagon = shrunk
                both, cross = vertic + diagon, vertic - diagon
                noise = (horiz + both, horiz - both, cross - horiz, -horiz - cross)
                for at, cols, pixel, part in zip(
                    (top, top, low, low), (even, odd, even, odd), pixels, noise
                ):
                    upper, lower = halves(part.astype(bf16).astype(f32) * pixel)
                    product[at : at + count, cols] = upper
                    product[size + at : size + at + count, cols] = lower

    for copy in late[1:]:
        copy.wait()

    for block in range(blocks):
        cols = slice(2 * block * LANES, (2 * block + 2) * LANES)
        weighted = jnp.dot(select_in[...], product[:, cols], preferred_element_type=f32)
        part = (weighted * scale[:, cols]).astype(bf16)
        both = jnp.dot(part, merge_in[...], preferred_element_type=f32).astype(bf16)
        out[:, cols] = both[:slot_rows]
        other[:, cols] = both[slot_rows:]


def main_part(chunk, own, above, below, inverse, select, box, merge, rows, pieces, slots):
    size, width_all = own.shape
    count = size // rows
    width = width_all // pieces
    halo = above.shape[0]
    cell_rows = 3 * (rows // 2) * count
    return pl.pallas_call(
        functools.partial(main_kernel, count, rows),
        in_specs=[pl.BlockSpec(memory_space=pltpu.SMEM)] + [pl.BlockSpec(memory_space=pl.ANY)] * 7,
        out_specs=[pl.BlockSpec(memory_space=pltpu.VMEM)] * 2,
        scratch_shapes=[
            pltpu.VMEM((size, width + 4 * LANES), bf16),
            pltpu.VMEM((halo, width // 2 + 2 * LANES), bf16),
            pltpu.VMEM((halo, width // 2 + 2 * LANES), bf16),
            pltpu.VMEM((RADII, cell_rows, width // 2 + 2 * LANES), bf16),
            pltpu.VMEM((FINE, cell_rows, width // 2 + 2 * LANES), bf16),
            pltpu.VMEM((cell_rows, 2 * LANES), f32),
            pltpu.VMEM((2 * size, width), bf16),
            pltpu.VMEM((size, width), f32),
            pltpu.VMEM((size, 2 * size), bf16),
            pltpu.VMEM((RADII, 4 * LANES, 2 * LANES), bf16),
            pltpu.VMEM((2 * LANES, 2 * LANES), bf16),
            pltpu.SemaphoreType.DMA((9,)),
            pltpu.SemaphoreType.DMA((4,)),
        ],
        out_shape=[
            jax.ShapeDtypeStruct((slots * rows, width), bf16),
            jax.ShapeDtypeStruct((size - slots * rows, width), bf16),
        ],
        compiler_params=pltpu.CompilerParams(vmem_limit_bytes=20 * 2**20),
        cost_estimate=pl.CostEstimate(
            flops=2 * 10**9, bytes_accessed=4 * 2**20, transcendentals=0
        ),
        name="residual",
    )(chunk, own, above, below, inverse, select, box, merge)


def most_kernel(*refs):
    notes, most = refs[:-1], refs[-1]
    highest = notes[0][...].astype(f32)
    for note in notes[1:]:
        highest = jnp.maximum(highest, note[...].astype(f32))
    most[0, 0] = jnp.max(highest[3:4]).astype(jnp.int32)


def most_cameras(extras, rows):
    return pl.pallas_call(
        most_kernel,
        grid=(1,),
        in_specs=[pl.BlockSpec((rows, LANES), lambda i: (2, 0))] * len(extras),
        out_specs=pl.BlockSpec(memory_space=pltpu.SMEM),
        out_shape=jax.ShapeDtypeStruct((1, 1), jnp.int32),
        compiler_params=pltpu.CompilerParams(vmem_limit_bytes=4 * 2**20),
        name="most_cameras",
    )(*extras)[0, 0]


def assemble_kernel(rows, pieces, select, share, *refs):
    parts, others = refs[:pieces], refs[pieces:-7]
    prints, partial, flat, scaled, wide, total, sent = refs[-7:]
    width = parts[0].shape[1]
    size = parts[0].shape[0] + sum(other.shape[0] for other in others[:1])
    tall = CAMS * rows
    for place, part in enumerate(parts):
        edges = part[: 2 * rows, :].astype(f32) * share[place].reshape(2 * rows, width)
        scaled[place, : 2 * rows, :] = edges.astype(bf16)
    total[...] = jnp.zeros((tall, LANES), f32)
    copies = []
    for block in range(width // (2 * LANES)):
        cols = slice(block * 2 * LANES, (block + 1) * 2 * LANES)
        joined = jnp.zeros((tall, 2 * LANES), f32)
        for place, part in enumerate(parts):
            pieces_of = [scaled[place, :, cols], part[2 * rows :, cols]]
            if others:
                pieces_of.append(others[place][:, cols])
            source = jnp.concatenate(pieces_of, axis=0)
            joined = joined + jnp.dot(
                select[place, :, :size], source, preferred_element_type=f32
            )
        flat[:, cols] = joined.astype(bf16)
        total[...] += joined[:, :LANES] + joined[:, LANES:]
        wide[:, :, cols] = joined.reshape(CAMS, rows, 2 * LANES)
        there = pl.ds(block * 2 * LANES, 2 * LANES)
        copies.append(
            pltpu.make_async_copy(wide.at[:, :, there], prints.at[:, :, there], sent.at[block])
        )
        copies[-1].start()
    gram = lax.dot_general(
        flat[...], flat[...], (((1,), (1,)), ((), ())), preferred_element_type=f32
    )
    sub = lax.broadcasted_iota(jnp.int32, (tall, tall), 0)
    lane = lax.broadcasted_iota(jnp.int32, (tall, tall), 1)
    gram = jnp.where((sub & (rows - 1)) == (lane & (rows - 1)), gram, 0.0)
    gram = jnp.sum(gram.reshape(CAMS, rows, tall), axis=1)
    sub = lax.broadcasted_iota(jnp.int32, (tall, LANES), 0)
    lane = lax.broadcasted_iota(jnp.int32, (tall, LANES), 1)
    gather = jnp.where((sub >> log2(rows)) == lane, 1.0, 0.0).astype(f32)
    gram = jnp.dot(gram, gather, precision=lax.Precision.HIGHEST, preferred_element_type=f32)
    sums = jnp.sum(total[...], axis=1, keepdims=True)
    sums = jnp.sum(sums.reshape(CAMS, rows, 1), axis=1)
    lane = lax.broadcasted_iota(jnp.int32, (CAMS, LANES), 1)
    partial[...] = jnp.where(lane == CAMS, sums, gram)
    for copy in copies:
        copy.wait()


def assemble(select, share, parts, others, rows):
    width = parts[0].shape[1]
    tall = CAMS * rows
    vmem = pl.BlockSpec(memory_space=pltpu.VMEM)
    return pl.pallas_call(
        functools.partial(assemble_kernel, rows, len(parts)),
        in_specs=[vmem] * (2 + len(parts) + len(others)),
        out_specs=[pl.BlockSpec(memory_space=pl.ANY), vmem],
        out_shape=[
            jax.ShapeDtypeStruct((CAMS, rows, width), f32),
            jax.ShapeDtypeStruct((CAMS, LANES), f32),
        ],
        scratch_shapes=[
            pltpu.VMEM((tall, width), bf16),
            pltpu.VMEM((len(parts), 2 * rows, width), bf16),
            pltpu.VMEM((CAMS, rows, width), f32),
            pltpu.VMEM((tall, LANES), f32),
            pltpu.SemaphoreType.DMA((width // (2 * LANES),)),
        ],
        compiler_params=pltpu.CompilerParams(vmem_limit_bytes=20 * 2**20),
        cost_estimate=pl.CostEstimate(
            flops=2 * 10**9, bytes_accessed=4 * 2**20, transcendentals=0
        ),
        name="assemble",
    )(select, share, *parts, *others)


def correlate_kernel(pixels, *refs):
    parts, out = refs[:-1], refs[-1]
    whole = parts[0][...]
    for part in parts[1:]:
        whole = whole + part[...]
    gram = whole[:, :CAMS]
    mean = whole[:, CAMS : CAMS + 1] / pixels
    sub = lax.broadcasted_iota(jnp.int32, (CAMS, CAMS), 0)
    lane = lax.broadcasted_iota(jnp.int32, (CAMS, CAMS), 1)
    diagonal = sub == lane
    mean_row = jnp.sum(jnp.where(diagonal, mean, 0.0), axis=0, keepdims=True)
    covar = gram / pixels - mean * mean_row
    only = jnp.where(diagonal, covar, 0.0)
    spread = jnp.sum(only, axis=1, keepdims=True) + var_eps
    spread_row = jnp.sum(only, axis=0, keepdims=True) + var_eps
    out[...] = covar / jnp.sqrt(spread * spread_row)


def correlate(parts, pixels):
    return pl.pallas_call(
        functools.partial(correlate_kernel, pixels),
        out_shape=jax.ShapeDtypeStruct((CAMS, CAMS), f32),
        compiler_params=pltpu.CompilerParams(vmem_limit_bytes=4 * 2**20),
        name="correlate",
    )(*parts)


def exchange(array, axis, distance):
    size = lax.axis_size(axis)
    return lax.ppermute(array, axis, [(i, i ^ distance) for i in range(size)])


def summed(array, axis, distances):
    terms = [array] + [exchange(array, axis, distance) for distance in distances]
    while len(terms) > 1:
        terms = [terms[i] + terms[i + 1] for i in range(0, len(terms), 2)]
    return terms[0]


def on_device(photos, camera_id):
    count, rows, width = photos.shape
    pieces, tiles = lax.axis_size("photo"), lax.axis_size("tile")
    me = lax.axis_index("photo").astype(jnp.int32)
    own, up, down, *extras = prepare(me.reshape(1), camera_id, photos, pieces)
    above = lax.ppermute(down, "tile", [(i, i + 1) for i in range(tiles - 1)])
    below = lax.ppermute(up, "tile", [(i + 1, i) for i in range(tiles - 1)])
    extras = [
        exchange(extra, "photo", distance) if distance else extra
        for distance, extra in enumerate(extras)
    ]
    inverse, select, box, merge = energies(camera_id, own, rows)

    few = max(2, 11 * count // 16)
    parts, others = [None] * pieces, [None] * pieces
    for distance in reversed(range(pieces)):
        part, other = main_part(
            (me ^ distance).reshape(1), own, above, below, inverse, select, box, merge,
            rows, pieces, few,
        )
        parts[distance] = exchange(part, "photo", distance) if distance else part
        others[distance] = other
    place, share = blend(me.reshape(1), extras, rows, count * rows)

    def finish_few():
        return assemble(place, share, parts, [], rows)

    def finish_all():
        late = [
            exchange(other, "photo", distance) if distance else other
            for distance, other in enumerate(others)
        ]
        return assemble(place, share, parts, late, rows)

    prints, partial = lax.cond(most_cameras(extras, rows) > few, finish_all, finish_few)

    total = summed(partial, "tile", (1,))
    total = summed(total, "photo", range(1, pieces))
    total = summed(total, "tile", range(2, tiles, 2))
    return prints, correlate([total], float(rows * tiles * width))


def solution(mesh):
    return jax.shard_map(
        on_device,
        mesh=mesh,
        in_specs=(P("photo", "tile", None), P("photo")),
        out_specs=(P(None, "tile", "photo"), P()),
        check_vma=False,
    )
```

```python
import functools

import jax
import jax.numpy as jnp
from jax import lax
from jax.experimental import pallas as pl
from jax.experimental.pallas import tpu as pltpu
from jax.sharding import PartitionSpec as P

CAMS = 32
RADII = 4
FINE = 2
LANES = 128

noise_power = 1.0
var_eps = 1e-06

f32 = jnp.float32
bf16 = jnp.bfloat16


def log2(value):
    return value.bit_length() - 1


def indicator(condition):
    return jnp.where(condition, 1.0, 0.0).astype(bf16)


def iotas(shape):
    return (
        lax.broadcasted_iota(jnp.int32, shape, len(shape) - 2),
        lax.broadcasted_iota(jnp.int32, shape, len(shape) - 1),
    )


def row_permutation(photos, rows):
    sub, lane = iotas((photos * rows, photos * rows))
    same_row = (sub >> log2(photos)) == (lane & (rows - 1))
    same_photo = (sub & (photos - 1)) == (lane >> log2(rows))
    return indicator(same_row & same_photo)


def column_split():
    sub, lane = iotas((2 * LANES, 2 * LANES))
    return indicator(sub == 2 * (lane & (LANES - 1)) + (lane >> log2(LANES)))


def column_merge():
    sub, lane = iotas((2 * LANES, 2 * LANES))
    return indicator(lane == 2 * (sub & (LANES - 1)) + (sub >> log2(LANES)))


def box_matrix(radius):
    sub, lane = iotas((4 * LANES, 2 * LANES))
    return indicator(jnp.abs(sub - LANES - lane) <= radius)


def haar_rows(even0, odd0, even1, odd1):
    low0, low1 = even0 + odd0, even1 + odd1
    high0, high1 = even0 - odd0, even1 - odd1
    return (low0 - low1, high0 + high1, high0 - high1)


def halves(value):
    upper = value.astype(bf16)
    lower = (value - upper.astype(f32)).astype(bf16)
    return upper, lower


def inverted(value):
    guess = pl.reciprocal(value, approx=True)
    return guess * (2.0 - value * guess)


def slot_numbers(ids, count):
    ranks = [jnp.int32(0)]
    for photo in range(1, count):
        ranks.append(ranks[-1] + jnp.where(ids[photo] != ids[photo - 1], 1, 0))
    last = ranks[-1]
    slots = [jnp.where(rank == 0, 0, jnp.where(rank == last, 1, rank + 1)) for rank in ranks]
    return slots, last + 1


def prepare_kernel(me, ids, photos, sorted_out, up_out, down_out, *extras):
    count, rows, width = photos.shape
    cells = rows // 2
    pieces = len(extras)
    step = width // pieces
    perm = row_permutation(count, rows)
    split = column_split()

    slots, cameras = slot_numbers(ids, count)
    sub, lane = iotas((rows, step))
    slot_id = jnp.full((rows, step), -1, jnp.int32)
    in_first, in_last = jnp.int32(0), jnp.int32(0)
    for photo in range(count):
        slot_id = jnp.where((lane >> log2(rows)) == slots[photo], ids[photo], slot_id)
        in_first = in_first + jnp.where(ids[photo] == ids[0], 1, 0)
        in_last = in_last + jnp.where(ids[photo] == ids[count - 1], 1, 0)
    notes = jnp.where(sub == 0, ids[0], jnp.where(sub == 1, ids[count - 1], slot_id))
    notes = jnp.where(sub == 3, cameras, notes).astype(f32).astype(bf16)

    for piece in range(pieces):
        flat = photos[:, :, piece * step : (piece + 1) * step].reshape(count * rows, step)
        by_row = jnp.dot(perm, flat, preferred_element_type=f32).astype(bf16)
        for inner in range(step // (2 * LANES)):
            block = piece * (step // (2 * LANES)) + inner
            cols = slice(block * 2 * LANES, (block + 1) * 2 * LANES)
            cell_cols = slice(block * LANES, (block + 1) * LANES)
            pixels = by_row[:, inner * 2 * LANES : (inner + 1) * 2 * LANES]
            parted = jnp.dot(pixels, split, preferred_element_type=f32)
            sorted_out[:, cols] = parted.astype(bf16)
            for i in range(cells):
                if RADII <= i < cells - RADII:
                    continue
                top = parted[2 * i * count : (2 * i + 1) * count]
                low = parted[(2 * i + 1) * count : (2 * i + 2) * count]
                bands = haar_rows(top[:, :LANES], top[:, LANES:], low[:, :LANES], low[:, LANES:])
                for band in range(3):
                    square = (bands[band] * bands[band]).astype(bf16)
                    if i < RADII:
                        start = (band * RADII + i) * count
                        up_out[start : start + count, cell_cols] = square
                    if i >= cells - RADII:
                        start = (band * RADII + i - (cells - RADII)) * count
                        down_out[start : start + count, cell_cols] = square

    none = jnp.zeros((rows, step), f32)
    for distance, extra in enumerate(extras):
        cols = pl.ds(pl.multiple_of((me[0] ^ distance) * step, step), step)

        def add(photo, total):
            pixel = photos[photo, :, cols].astype(f32)
            return total + pixel * pixel

        extra[:rows, :] = lax.fori_loop(0, in_first, add, none).astype(bf16)
        extra[rows : 2 * rows, :] = lax.fori_loop(count - in_last, count, add, none).astype(bf16)
        extra[2 * rows :, :] = notes


def prepare(me, ids, photos, pieces):
    count, rows, width = photos.shape
    step = width // pieces
    size = count * rows
    halo = 3 * RADII * count
    vmem = pl.BlockSpec(memory_space=pltpu.VMEM)
    smem = pl.BlockSpec(memory_space=pltpu.SMEM)
    return pl.pallas_call(
        prepare_kernel,
        in_specs=[smem, smem, vmem],
        out_specs=[vmem] * (3 + pieces),
        out_shape=[
            jax.ShapeDtypeStruct((size, width), bf16),
            jax.ShapeDtypeStruct((halo, width // 2), bf16),
            jax.ShapeDtypeStruct((halo, width // 2), bf16),
        ]
        + [jax.ShapeDtypeStruct((3 * rows, step), bf16)] * pieces,
        compiler_params=pltpu.CompilerParams(vmem_limit_bytes=20 * 2**20),
        cost_estimate=pl.CostEstimate(flops=10**9, bytes_accessed=8 * 2**20, transcendentals=0),
        name="prepare",
    )(me, ids, photos)


def energy_kernel(count, rows, ids, own, inverse, select_out, box_out, merge_out):
    size, width = own.shape
    slots, _ = slot_numbers(ids, count)
    sub, lane = iotas((size, size))
    lane_photo = lane & (count - 1)
    lane_slot = jnp.zeros_like(lane)
    for photo in range(count):
        lane_slot = jnp.where(lane_photo == photo, slots[photo], lane_slot)
    in_slot = lane_slot == (sub >> log2(rows))
    same_row = (sub & (rows - 1)) == (lane >> log2(count))
    select = indicator(in_slot & same_row)
    select = jnp.concatenate([select, select], axis=1)
    select_out[...] = select
    for radius in range(1, RADII + 1):
        box_out[radius - 1] = box_matrix(radius)
    merge_out[...] = column_merge()

    for block in range(width // (2 * LANES)):
        cols = slice(block * 2 * LANES, (block + 1) * 2 * LANES)
        pixel = own[:, cols].astype(f32)
        pair = jnp.concatenate(halves(pixel * pixel), axis=0)
        energy = jnp.dot(select, pair, preferred_element_type=f32)
        inverse[:, cols] = inverted(jnp.maximum(energy, 2.0**-20))


def energies(ids, own, rows):
    size, width = own.shape
    vmem = pl.BlockSpec(memory_space=pltpu.VMEM)
    smem = pl.BlockSpec(memory_space=pltpu.SMEM)
    return pl.pallas_call(
        functools.partial(energy_kernel, size // rows, rows),
        in_specs=[smem, vmem],
        out_specs=[vmem] * 4,
        out_shape=[
            jax.ShapeDtypeStruct((size, width), f32),
            jax.ShapeDtypeStruct((size, 2 * size), bf16),
            jax.ShapeDtypeStruct((RADII, 4 * LANES, 2 * LANES), bf16),
            jax.ShapeDtypeStruct((2 * LANES, 2 * LANES), bf16),
        ],
        compiler_params=pltpu.CompilerParams(vmem_limit_bytes=20 * 2**20),
        cost_estimate=pl.CostEstimate(flops=10**9, bytes_accessed=8 * 2**20, transcendentals=0),
        name="energies",
    )(ids, own)


def blend_kernel(rows, me, *refs):
    pieces = len(refs) - 4
    extras, (select, share, most, held) = refs[:pieces], refs[pieces:]
    size = select.shape[2]
    tall = CAMS * rows
    sub, lane = iotas((tall, size))
    same_row = (sub & (rows - 1)) == (lane & (rows - 1))
    camera = (sub >> log2(rows)).astype(f32)
    highest = jnp.float32(0)
    for distance, extra in enumerate(extras):
        notes = extra[2 * rows :, :].astype(f32)
        highest = jnp.maximum(highest, jnp.max(notes[3:4, :LANES]))
        select[distance] = indicator((camera == notes[2:3, :size]) & same_row)
        held[me[0] ^ distance] = extra[...].astype(f32)
    most[0] = highest.astype(jnp.int32)
    ones = jnp.ones((rows, share.shape[3]), f32)
    for device in range(pieces):
        if device == 0:
            share[me[0] ^ device, 0] = ones
        if device == pieces - 1:
            share[me[0] ^ device, 1] = ones
            continue
        late = held[device, rows : 2 * rows]
        early = held[device + 1, :rows]
        crosses = held[device, 2 * rows + 1 : 2 * rows + 2] == held[device + 1, 2 * rows : 2 * rows + 1]
        joint = 1.0 / (late + early)
        share[me[0] ^ device, 1] = jnp.where(crosses, late * joint, 1.0)
        share[me[0] ^ (device + 1), 0] = jnp.where(crosses, early * joint, 1.0)


def blend(me, extras, rows, size):
    pieces, width = len(extras), extras[0].shape[1]
    vmem = pl.BlockSpec(memory_space=pltpu.VMEM)
    smem = pl.BlockSpec(memory_space=pltpu.SMEM)
    return pl.pallas_call(
        functools.partial(blend_kernel, rows),
        in_specs=[smem] + [vmem] * pieces,
        out_specs=[vmem, vmem, smem],
        out_shape=[
            jax.ShapeDtypeStruct((pieces, CAMS * rows, size), bf16),
            jax.ShapeDtypeStruct((pieces, 2, rows, width), f32),
            jax.ShapeDtypeStruct((1,), jnp.int32),
        ],
        scratch_shapes=[pltpu.VMEM((pieces, 3 * rows, width), f32)],
        compiler_params=pltpu.CompilerParams(vmem_limit_bytes=20 * 2**20),
        name="blend",
    )(me, *extras)


def main_kernel(
    count, rows, chunk, most, own_all, above_all, below_all, inverse, select, box, merge, out, other,
    own, above, below, sums, rest, least, product, scale, select_in, box_in, merge_in,
    arrived, ready,
):
    cells = rows // 2
    size = count * rows
    width = out.shape[1]
    blocks = width // (2 * LANES)
    slot_rows = out.shape[0]
    base = chunk[0] * width
    inner = []
    edges = ([], [])
    for at, (whole, local, lanes) in enumerate(
        ((own_all, own, 2 * LANES), (above_all, above, LANES), (below_all, below, LANES))
    ):
        length = blocks * lanes
        start = chunk[0] * length
        for place, size_here, offset, group in (
            (start, length, lanes, inner),
            (jnp.maximum(start - lanes, 0), lanes, 0, edges[0]),
            (jnp.minimum(start + length, whole.shape[1] - lanes), lanes, lanes + length, edges[1]),
        ):
            index = 3 * at + (0 if group is inner else 1 if group is edges[0] else 2)
            group.append(
                pltpu.make_async_copy(
                    whole.at[:, pl.ds(pl.multiple_of(place, lanes), size_here)],
                    local.at[:, pl.ds(offset, size_here)],
                    arrived.at[index],
                )
            )
    late = [
        pltpu.make_async_copy(box, box_in, ready.at[0]),
        pltpu.make_async_copy(select, select_in, ready.at[1]),
        pltpu.make_async_copy(
            inverse.at[:, pl.ds(pl.multiple_of(base, width), width)],
            scale,
            ready.at[2],
        ),
        pltpu.make_async_copy(merge, merge_in, ready.at[3]),
    ]
    for copy in inner + edges[0] + edges[1] + late:
        copy.start()

    def pixels_of(i, start):
        top = slice(2 * i * count, (2 * i + 1) * count)
        low = slice((2 * i + 1) * count, (2 * i + 2) * count)
        even, odd = slice(start, start + LANES), slice(start + LANES, start + 2 * LANES)
        return tuple(
            own[at, cols].astype(f32)
            for at, cols in ((top, even), (top, odd), (low, even), (low, odd))
        )

    def add_up(block, fine):
        cols = slice(block * LANES, (block + 1) * LANES)
        squares = [[], [], []]
        for i in range(cells):
            bands = haar_rows(*pixels_of(i, block * 2 * LANES))
            for band in range(3):
                squares[band].append(bands[band] * bands[band])
        for band in range(3):
            first = band * RADII * count
            over, under = (
                [
                    halo[first + i * count : first + (i + 1) * count, cols].astype(f32)
                    for i in range(RADII)
                ]
                for halo in (above, below)
            )
            column = over + squares[band] + under
            for i in range(cells):
                total = column[i + RADII]
                at_row = (band * cells + i) * count
                for radius in range(1, RADII + 1):
                    total = total + (column[i + RADII - radius] + column[i + RADII + radius])
                    upper = total.astype(bf16)
                    sums[radius - 1, at_row : at_row + count, cols] = upper
                    if radius <= FINE and fine:
                        lower = (total - upper.astype(f32)).astype(bf16)
                        rest[radius - 1, at_row : at_row + count, cols] = lower

    for copy in inner:
        copy.wait()

    for block in range(1, blocks + 1):
        add_up(block, True)

    for copy in edges[0] + edges[1]:
        copy.wait()

    add_up(0, False)
    add_up(blocks + 1, False)

    for side, outside in enumerate((base == 0, base + width == own_all.shape[1])):

        @pl.when(outside)
        def _():
            at = side * (blocks + 1) * LANES
            sums[:, :, at : at + LANES] = jnp.zeros(sums.shape[:2] + (LANES,), bf16)

    late[0].wait()

    for group in range(blocks // 2):
        first = group * 2 * LANES
        window = slice(first, first + 4 * LANES)
        middle = slice(first + LANES, first + 3 * LANES)
        for radius in range(1, RADII + 1):
            narrow, weights = sums[radius - 1, :, window], box_in[radius - 1]
            if radius <= FINE:
                narrow = jnp.concatenate([narrow, rest[radius - 1, :, middle]], axis=1)
                weights = jnp.concatenate([weights, weights[LANES : 3 * LANES]], axis=0)
            wide = jnp.dot(narrow, weights, preferred_element_type=f32)
            mean = wide * (1.0 / float((2 * radius + 1) ** 2))
            least[...] = mean if radius == 1 else jnp.minimum(least[...], mean)

        for half in range(2):
            start = (2 * group + half) * 2 * LANES
            even = slice(start, start + LANES)
            odd = slice(start + LANES, start + 2 * LANES)
            lanes = slice(half * LANES, (half + 1) * LANES)
            for i in range(cells):
                top, low = 2 * i * count, (2 * i + 1) * count
                pixels = pixels_of(i, start + 2 * LANES)
                bands = haar_rows(*pixels)
                shrunk = []
                for band in range(3):
                    at_row = (band * cells + i) * count
                    variance = least[at_row : at_row + count, lanes]
                    bound = jnp.maximum(variance, 4.0 * noise_power)
                    shrunk.append(bands[band] * (noise_power * inverted(bound)))
                horiz, vertic, diagon = shrunk
                both, cross = vertic + diagon, vertic - diagon
                noise = (horiz + both, horiz - both, cross - horiz, -horiz - cross)
                for at, cols, pixel, part in zip(
                    (top, top, low, low), (even, odd, even, odd), pixels, noise
                ):
                    upper, lower = halves(part.astype(bf16).astype(f32) * pixel)
                    product[at : at + count, cols] = upper
                    product[size + at : size + at + count, cols] = lower

    for copy in late[1:]:
        copy.wait()

    for block in range(blocks):
        cols = slice(2 * block * LANES, (2 * block + 2) * LANES)
        weighted = jnp.dot(select_in[...], product[:, cols], preferred_element_type=f32)
        part = (weighted * scale[:, cols]).astype(bf16)
        both = jnp.dot(part, merge_in[...], preferred_element_type=f32).astype(bf16)
        out[:, cols] = both[:slot_rows]
        other[:, cols] = both[slot_rows:]


def main_part(chunk, most, own, above, below, inverse, select, box, merge, rows, pieces, slots):
    size, width_all = own.shape
    count = size // rows
    width = width_all // pieces
    halo = above.shape[0]
    cell_rows = 3 * (rows // 2) * count
    return pl.pallas_call(
        functools.partial(main_kernel, count, rows),
        in_specs=[pl.BlockSpec(memory_space=pltpu.SMEM)] * 2
        + [pl.BlockSpec(memory_space=pl.ANY)] * 7,
        out_specs=[pl.BlockSpec(memory_space=pltpu.VMEM)] * 2,
        scratch_shapes=[
            pltpu.VMEM((size, width + 4 * LANES), bf16),
            pltpu.VMEM((halo, width // 2 + 2 * LANES), bf16),
            pltpu.VMEM((halo, width // 2 + 2 * LANES), bf16),
            pltpu.VMEM((RADII, cell_rows, width // 2 + 2 * LANES), bf16),
            pltpu.VMEM((FINE, cell_rows, width // 2 + 2 * LANES), bf16),
            pltpu.VMEM((cell_rows, 2 * LANES), f32),
            pltpu.VMEM((2 * size, width), bf16),
            pltpu.VMEM((size, width), f32),
            pltpu.VMEM((size, 2 * size), bf16),
            pltpu.VMEM((RADII, 4 * LANES, 2 * LANES), bf16),
            pltpu.VMEM((2 * LANES, 2 * LANES), bf16),
            pltpu.SemaphoreType.DMA((9,)),
            pltpu.SemaphoreType.DMA((4,)),
        ],
        out_shape=[
            jax.ShapeDtypeStruct((slots * rows, width), bf16),
            jax.ShapeDtypeStruct((size - slots * rows, width), bf16),
        ],
        compiler_params=pltpu.CompilerParams(vmem_limit_bytes=20 * 2**20),
        cost_estimate=pl.CostEstimate(
            flops=2 * 10**9, bytes_accessed=4 * 2**20, transcendentals=0
        ),
        name="residual",
    )(chunk, most, own, above, below, inverse, select, box, merge)


def assemble_kernel(rows, pieces, select, share, *refs):
    parts, others = refs[:pieces], refs[pieces:-7]
    prints, partial, flat, scaled, wide, total, sent = refs[-7:]
    width = parts[0].shape[1]
    size = parts[0].shape[0] + sum(other.shape[0] for other in others[:1])
    tall = CAMS * rows
    for place, part in enumerate(parts):
        edges = part[: 2 * rows, :].astype(f32) * share[place].reshape(2 * rows, width)
        scaled[place, : 2 * rows, :] = edges.astype(bf16)
    total[...] = jnp.zeros((tall, LANES), f32)
    copies = []
    for block in range(width // (2 * LANES)):
        cols = slice(block * 2 * LANES, (block + 1) * 2 * LANES)
        joined = jnp.zeros((tall, 2 * LANES), f32)
        for place, part in enumerate(parts):
            pieces_of = [scaled[place, :, cols], part[2 * rows :, cols]]
            if others:
                pieces_of.append(others[place][:, cols])
            source = jnp.concatenate(pieces_of, axis=0)
            joined = joined + jnp.dot(
                select[place, :, :size], source, preferred_element_type=f32
            )
        flat[:, cols] = joined.astype(bf16)
        total[...] += joined[:, :LANES] + joined[:, LANES:]
        wide[:, :, cols] = joined.reshape(CAMS, rows, 2 * LANES)
        there = pl.ds(block * 2 * LANES, 2 * LANES)
        copies.append(
            pltpu.make_async_copy(wide.at[:, :, there], prints.at[:, :, there], sent.at[block])
        )
        copies[-1].start()
    gram = lax.dot_general(
        flat[...], flat[...], (((1,), (1,)), ((), ())), preferred_element_type=f32
    )
    sub = lax.broadcasted_iota(jnp.int32, (tall, tall), 0)
    lane = lax.broadcasted_iota(jnp.int32, (tall, tall), 1)
    gram = jnp.where((sub & (rows - 1)) == (lane & (rows - 1)), gram, 0.0)
    gram = jnp.sum(gram.reshape(CAMS, rows, tall), axis=1)
    sub = lax.broadcasted_iota(jnp.int32, (tall, LANES), 0)
    lane = lax.broadcasted_iota(jnp.int32, (tall, LANES), 1)
    gather = jnp.where((sub >> log2(rows)) == lane, 1.0, 0.0).astype(f32)
    gram = jnp.dot(gram, gather, precision=lax.Precision.HIGHEST, preferred_element_type=f32)
    sums = jnp.sum(total[...], axis=1, keepdims=True)
    sums = jnp.sum(sums.reshape(CAMS, rows, 1), axis=1)
    lane = lax.broadcasted_iota(jnp.int32, (CAMS, LANES), 1)
    partial[...] = jnp.where(lane == CAMS, sums, gram)
    for copy in copies:
        copy.wait()


def assemble(select, share, parts, others, rows):
    width = parts[0].shape[1]
    tall = CAMS * rows
    vmem = pl.BlockSpec(memory_space=pltpu.VMEM)
    return pl.pallas_call(
        functools.partial(assemble_kernel, rows, len(parts)),
        in_specs=[vmem] * (2 + len(parts) + len(others)),
        out_specs=[pl.BlockSpec(memory_space=pl.ANY), vmem],
        out_shape=[
            jax.ShapeDtypeStruct((CAMS, rows, width), f32),
            jax.ShapeDtypeStruct((CAMS, LANES), f32),
        ],
        scratch_shapes=[
            pltpu.VMEM((tall, width), bf16),
            pltpu.VMEM((len(parts), 2 * rows, width), bf16),
            pltpu.VMEM((CAMS, rows, width), f32),
            pltpu.VMEM((tall, LANES), f32),
            pltpu.SemaphoreType.DMA((width // (2 * LANES),)),
        ],
        compiler_params=pltpu.CompilerParams(vmem_limit_bytes=20 * 2**20),
        cost_estimate=pl.CostEstimate(
            flops=2 * 10**9, bytes_accessed=4 * 2**20, transcendentals=0
        ),
        name="assemble",
    )(select, share, *parts, *others)


def correlate_kernel(pixels, *refs):
    parts, out = refs[:-1], refs[-1]
    whole = parts[0][...]
    for part in parts[1:]:
        whole = whole + part[...]
    gram = whole[:, :CAMS]
    mean = whole[:, CAMS : CAMS + 1] / pixels
    sub = lax.broadcasted_iota(jnp.int32, (CAMS, CAMS), 0)
    lane = lax.broadcasted_iota(jnp.int32, (CAMS, CAMS), 1)
    diagonal = sub == lane
    mean_row = jnp.sum(jnp.where(diagonal, mean, 0.0), axis=0, keepdims=True)
    covar = gram / pixels - mean * mean_row
    only = jnp.where(diagonal, covar, 0.0)
    spread = jnp.sum(only, axis=1, keepdims=True) + var_eps
    spread_row = jnp.sum(only, axis=0, keepdims=True) + var_eps
    out[...] = covar / jnp.sqrt(spread * spread_row)


def correlate(parts, pixels):
    return pl.pallas_call(
        functools.partial(correlate_kernel, pixels),
        out_shape=jax.ShapeDtypeStruct((CAMS, CAMS), f32),
        compiler_params=pltpu.CompilerParams(vmem_limit_bytes=4 * 2**20),
        name="correlate",
    )(*parts)


def exchange(array, axis, distance):
    size = lax.axis_size(axis)
    return lax.ppermute(array, axis, [(i, i ^ distance) for i in range(size)])


def summed(array, axis, distances):
    terms = [array] + [exchange(array, axis, distance) for distance in distances]
    while len(terms) > 1:
        terms = [terms[i] + terms[i + 1] for i in range(0, len(terms), 2)]
    return terms[0]


def on_device(photos, camera_id):
    count, rows, width = photos.shape
    pieces, tiles = lax.axis_size("photo"), lax.axis_size("tile")
    me = lax.axis_index("photo").astype(jnp.int32)
    own, up, down, *extras = prepare(me.reshape(1), camera_id, photos, pieces)
    above = lax.ppermute(down, "tile", [(i, i + 1) for i in range(tiles - 1)])
    below = lax.ppermute(up, "tile", [(i + 1, i) for i in range(tiles - 1)])
    extras = [
        exchange(extra, "photo", distance) if distance else extra
        for distance, extra in enumerate(extras)
    ]
    inverse, select, box, merge = energies(camera_id, own, rows)

    place, share, most = blend(me.reshape(1), extras, rows, count * rows)
    few = max(2, 11 * count // 16)
    parts, others = [None] * pieces, [None] * pieces
    for distance in reversed(range(pieces)):
        part, other = main_part(
            (me ^ distance).reshape(1), most, own, above, below, inverse, select, box, merge,
            rows, pieces, few,
        )
        parts[distance] = exchange(part, "photo", distance) if distance else part
        others[distance] = other

    def finish_few():
        return assemble(place, share, parts, [], rows)

    def finish_all():
        late = [
            exchange(other, "photo", distance) if distance else other
            for distance, other in enumerate(others)
        ]
        return assemble(place, share, parts, late, rows)

    prints, partial = lax.cond(most[0] > few, finish_all, finish_few)

    total = summed(partial, "tile", (1,))
    total = summed(total, "photo", range(1, pieces))
    total = summed(total, "tile", range(2, tiles, 2))
    return prints, correlate([total], float(rows * tiles * width))


def solution(mesh):
    return jax.shard_map(
        on_device,
        mesh=mesh,
        in_specs=(P("photo", "tile", None), P("photo")),
        out_specs=(P(None, "tile", "photo"), P()),
        check_vma=False,
    )
```

```python
import functools

import jax
import jax.numpy as jnp
from jax import lax
from jax.experimental import pallas as pl
from jax.experimental.pallas import tpu as pltpu
from jax.sharding import PartitionSpec as P

CAMS = 32
RADII = 4
FINE = 2
LANES = 128

noise_power = 1.0
var_eps = 1e-06

f32 = jnp.float32
bf16 = jnp.bfloat16


def log2(value):
    return value.bit_length() - 1


def indicator(condition):
    return jnp.where(condition, 1.0, 0.0).astype(bf16)


def iotas(shape):
    return (
        lax.broadcasted_iota(jnp.int32, shape, len(shape) - 2),
        lax.broadcasted_iota(jnp.int32, shape, len(shape) - 1),
    )


def row_permutation(photos, rows):
    sub, lane = iotas((photos * rows, photos * rows))
    same_row = (sub >> log2(photos)) == (lane & (rows - 1))
    same_photo = (sub & (photos - 1)) == (lane >> log2(rows))
    return indicator(same_row & same_photo)


def column_split():
    sub, lane = iotas((2 * LANES, 2 * LANES))
    return indicator(sub == 2 * (lane & (LANES - 1)) + (lane >> log2(LANES)))


def column_merge():
    sub, lane = iotas((2 * LANES, 2 * LANES))
    return indicator(lane == 2 * (sub & (LANES - 1)) + (sub >> log2(LANES)))


def box_matrix(radius):
    sub, lane = iotas((4 * LANES, 2 * LANES))
    return indicator(jnp.abs(sub - LANES - lane) <= radius)


def haar_rows(even0, odd0, even1, odd1):
    low0, low1 = even0 + odd0, even1 + odd1
    high0, high1 = even0 - odd0, even1 - odd1
    return (low0 - low1, high0 + high1, high0 - high1)


def halves(value):
    upper = value.astype(bf16)
    lower = (value - upper.astype(f32)).astype(bf16)
    return upper, lower


def inverted(value):
    guess = pl.reciprocal(value, approx=True)
    return guess * (2.0 - value * guess)


def slot_numbers(ids, count):
    ranks = [jnp.int32(0)]
    for photo in range(1, count):
        ranks.append(ranks[-1] + jnp.where(ids[photo] != ids[photo - 1], 1, 0))
    last = ranks[-1]
    slots = [jnp.where(rank == 0, 0, jnp.where(rank == last, 1, rank + 1)) for rank in ranks]
    return slots, last + 1


def prepare_kernel(ids_all, photos, sorted_out, up_out, down_out, *refs):
    extras, (ids, ready) = refs[:-2], refs[-2:]
    count, rows, width = photos.shape
    cells = rows // 2
    pieces = len(extras)
    step = width // pieces
    me = lax.axis_index("photo")
    copy = pltpu.make_async_copy(ids_all, ids, ready)
    copy.start()
    perm = row_permutation(count, rows)
    split = column_split()

    for piece in range(pieces):
        flat = photos[:, :, piece * step : (piece + 1) * step].reshape(count * rows, step)
        by_row = jnp.dot(perm, flat, preferred_element_type=f32).astype(bf16)
        for inner in range(step // (2 * LANES)):
            block = piece * (step // (2 * LANES)) + inner
            cols = slice(block * 2 * LANES, (block + 1) * 2 * LANES)
            cell_cols = slice(block * LANES, (block + 1) * LANES)
            pixels = by_row[:, inner * 2 * LANES : (inner + 1) * 2 * LANES]
            parted = jnp.dot(pixels, split, preferred_element_type=f32)
            sorted_out[:, cols] = parted.astype(bf16)
            for i in range(cells):
                if RADII <= i < cells - RADII:
                    continue
                top = parted[2 * i * count : (2 * i + 1) * count]
                low = parted[(2 * i + 1) * count : (2 * i + 2) * count]
                bands = haar_rows(top[:, :LANES], top[:, LANES:], low[:, :LANES], low[:, LANES:])
                for band in range(3):
                    square = (bands[band] * bands[band]).astype(bf16)
                    if i < RADII:
                        start = (band * RADII + i) * count
                        up_out[start : start + count, cell_cols] = square
                    if i >= cells - RADII:
                        start = (band * RADII + i - (cells - RADII)) * count
                        down_out[start : start + count, cell_cols] = square

    copy.wait()
    slots, cameras = slot_numbers(ids, count)
    sub, lane = iotas((rows, step))
    slot_id = jnp.full((rows, step), -1, jnp.int32)
    in_first, in_last = jnp.int32(0), jnp.int32(0)
    for photo in range(count):
        slot_id = jnp.where((lane >> log2(rows)) == slots[photo], ids[photo], slot_id)
        in_first = in_first + jnp.where(ids[photo] == ids[0], 1, 0)
        in_last = in_last + jnp.where(ids[photo] == ids[count - 1], 1, 0)
    notes = jnp.where(sub == 0, ids[0], jnp.where(sub == 1, ids[count - 1], slot_id))
    notes = jnp.where(sub == 3, cameras, notes).astype(f32).astype(bf16)

    none = jnp.zeros((rows, step), f32)
    for distance, extra in enumerate(extras):
        cols = pl.ds(pl.multiple_of((me ^ distance) * step, step), step)

        def add(photo, total):
            pixel = photos[photo, :, cols].astype(f32)
            return total + pixel * pixel

        extra[:rows, :] = lax.fori_loop(0, in_first, add, none).astype(bf16)
        extra[rows : 2 * rows, :] = lax.fori_loop(count - in_last, count, add, none).astype(bf16)
        extra[2 * rows :, :] = notes


def prepare(ids, photos, pieces):
    count, rows, width = photos.shape
    step = width // pieces
    size = count * rows
    halo = 3 * RADII * count
    vmem = pl.BlockSpec(memory_space=pltpu.VMEM)
    return pl.pallas_call(
        prepare_kernel,
        in_specs=[pl.BlockSpec(memory_space=pl.ANY), vmem],
        out_specs=[vmem] * (3 + pieces),
        out_shape=[
            jax.ShapeDtypeStruct((size, width), bf16),
            jax.ShapeDtypeStruct((halo, width // 2), bf16),
            jax.ShapeDtypeStruct((halo, width // 2), bf16),
        ]
        + [jax.ShapeDtypeStruct((3 * rows, step), bf16)] * pieces,
        scratch_shapes=[pltpu.SMEM((count,), jnp.int32), pltpu.SemaphoreType.DMA(())],
        compiler_params=pltpu.CompilerParams(vmem_limit_bytes=20 * 2**20),
        cost_estimate=pl.CostEstimate(flops=10**9, bytes_accessed=8 * 2**20, transcendentals=0),
        name="prepare",
    )(ids, photos)


def energy_kernel(count, rows, ids, own, inverse, select_out, box_out, merge_out):
    size, width = own.shape
    slots, _ = slot_numbers(ids, count)
    sub, lane = iotas((size, size))
    lane_photo = lane & (count - 1)
    lane_slot = jnp.zeros_like(lane)
    for photo in range(count):
        lane_slot = jnp.where(lane_photo == photo, slots[photo], lane_slot)
    in_slot = lane_slot == (sub >> log2(rows))
    same_row = (sub & (rows - 1)) == (lane >> log2(count))
    select = indicator(in_slot & same_row)
    select = jnp.concatenate([select, select], axis=1)
    select_out[...] = select
    for radius in range(1, RADII + 1):
        box_out[radius - 1] = box_matrix(radius)
    merge_out[...] = column_merge()

    for block in range(width // (2 * LANES)):
        cols = slice(block * 2 * LANES, (block + 1) * 2 * LANES)
        pixel = own[:, cols].astype(f32)
        pair = jnp.concatenate(halves(pixel * pixel), axis=0)
        energy = jnp.dot(select, pair, preferred_element_type=f32)
        inverse[:, cols] = inverted(jnp.maximum(energy, 2.0**-20))


def energies(ids, own, rows):
    size, width = own.shape
    vmem = pl.BlockSpec(memory_space=pltpu.VMEM)
    smem = pl.BlockSpec(memory_space=pltpu.SMEM)
    return pl.pallas_call(
        functools.partial(energy_kernel, size // rows, rows),
        in_specs=[smem, vmem],
        out_specs=[vmem] * 4,
        out_shape=[
            jax.ShapeDtypeStruct((size, width), f32),
            jax.ShapeDtypeStruct((size, 2 * size), bf16),
            jax.ShapeDtypeStruct((RADII, 4 * LANES, 2 * LANES), bf16),
            jax.ShapeDtypeStruct((2 * LANES, 2 * LANES), bf16),
        ],
        compiler_params=pltpu.CompilerParams(vmem_limit_bytes=20 * 2**20),
        cost_estimate=pl.CostEstimate(flops=10**9, bytes_accessed=8 * 2**20, transcendentals=0),
        name="energies",
    )(ids, own)


def blend_kernel(rows, *refs):
    pieces = len(refs) - 5
    me = lax.axis_index("photo")
    extras, (select, share, most, most_row, held) = refs[:pieces], refs[pieces:]
    size = select.shape[2]
    tall = CAMS * rows
    sub, lane = iotas((tall, size))
    same_row = (sub & (rows - 1)) == (lane & (rows - 1))
    camera = (sub >> log2(rows)).astype(f32)
    highest = jnp.float32(0)
    for distance, extra in enumerate(extras):
        notes = extra[2 * rows :, :].astype(f32)
        highest = jnp.maximum(highest, jnp.max(notes[3:4, :LANES]))
        select[distance] = indicator((camera == notes[2:3, :size]) & same_row)
        held[me ^ distance] = extra[...].astype(f32)
    most[0] = highest.astype(jnp.int32)
    most_row[...] = jnp.full(most_row.shape, highest)
    ones = jnp.ones((rows, share.shape[3]), f32)
    for device in range(pieces):
        if device == 0:
            share[me ^ device, 0] = ones
        if device == pieces - 1:
            share[me ^ device, 1] = ones
            continue
        late = held[device, rows : 2 * rows]
        early = held[device + 1, :rows]
        crosses = held[device, 2 * rows + 1 : 2 * rows + 2] == held[device + 1, 2 * rows : 2 * rows + 1]
        joint = 1.0 / (late + early)
        share[me ^ device, 1] = jnp.where(crosses, late * joint, 1.0)
        share[me ^ (device + 1), 0] = jnp.where(crosses, early * joint, 1.0)


def blend(extras, rows, size):
    pieces, width = len(extras), extras[0].shape[1]
    vmem = pl.BlockSpec(memory_space=pltpu.VMEM)
    smem = pl.BlockSpec(memory_space=pltpu.SMEM)
    return pl.pallas_call(
        functools.partial(blend_kernel, rows),
        in_specs=[vmem] * pieces,
        out_specs=[vmem, vmem, smem, vmem],
        out_shape=[
            jax.ShapeDtypeStruct((pieces, CAMS * rows, size), bf16),
            jax.ShapeDtypeStruct((pieces, 2, rows, width), f32),
            jax.ShapeDtypeStruct((1,), jnp.int32),
            jax.ShapeDtypeStruct((8, LANES), f32),
        ],
        scratch_shapes=[pltpu.VMEM((pieces, 3 * rows, width), f32)],
        compiler_params=pltpu.CompilerParams(vmem_limit_bytes=20 * 2**20),
        name="blend",
    )(*extras)


def main_kernel(
    count, rows, distance, most, own_all, above_all, below_all, inverse, select, box, merge,
    out, other, own, above, below, sums, rest, least, product, scale, scale_other, select_in, box_in, merge_in,
    arrived, ready,
):
    cells = rows // 2
    size = count * rows
    width = out.shape[1]
    blocks = width // (2 * LANES)
    slot_rows = out.shape[0]
    chunk = lax.axis_index("photo") ^ distance
    base = chunk * width
    inner = []
    edges = ([], [])
    for at, (whole, local, lanes) in enumerate(
        ((own_all, own, 2 * LANES), (above_all, above, LANES), (below_all, below, LANES))
    ):
        length = blocks * lanes
        start = chunk * length
        for place, size_here, offset, group in (
            (start, length, lanes, inner),
            (jnp.maximum(start - lanes, 0), lanes, 0, edges[0]),
            (jnp.minimum(start + length, whole.shape[1] - lanes), lanes, lanes + length, edges[1]),
        ):
            index = 3 * at + (0 if group is inner else 1 if group is edges[0] else 2)
            group.append(
                pltpu.make_async_copy(
                    whole.at[:, pl.ds(pl.multiple_of(place, lanes), size_here)],
                    local.at[:, pl.ds(offset, size_here)],
                    arrived.at[index],
                )
            )
    late = [
        pltpu.make_async_copy(box, box_in, ready.at[0]),
        pltpu.make_async_copy(select, select_in, ready.at[1]),
        pltpu.make_async_copy(
            inverse.at[pl.ds(0, slot_rows), pl.ds(pl.multiple_of(base, width), width)],
            scale,
            ready.at[2],
        ),
        pltpu.make_async_copy(merge, merge_in, ready.at[3]),
    ]
    for copy in inner + edges[0] + edges[1] + late:
        copy.start()

    def pixels_of(i, start):
        top = slice(2 * i * count, (2 * i + 1) * count)
        low = slice((2 * i + 1) * count, (2 * i + 2) * count)
        even, odd = slice(start, start + LANES), slice(start + LANES, start + 2 * LANES)
        return tuple(
            own[at, cols].astype(f32)
            for at, cols in ((top, even), (top, odd), (low, even), (low, odd))
        )

    def add_up(block, fine):
        cols = slice(block * LANES, (block + 1) * LANES)
        squares = [[], [], []]
        for i in range(cells):
            bands = haar_rows(*pixels_of(i, block * 2 * LANES))
            for band in range(3):
                squares[band].append(bands[band] * bands[band])
        for band in range(3):
            first = band * RADII * count
            over, under = (
                [
                    halo[first + i * count : first + (i + 1) * count, cols].astype(f32)
                    for i in range(RADII)
                ]
                for halo in (above, below)
            )
            column = over + squares[band] + under
            for i in range(cells):
                total = column[i + RADII]
                at_row = (band * cells + i) * count
                for radius in range(1, RADII + 1):
                    total = total + (column[i + RADII - radius] + column[i + RADII + radius])
                    upper = total.astype(bf16)
                    sums[radius - 1, at_row : at_row + count, cols] = upper
                    if radius <= FINE and fine:
                        lower = (total - upper.astype(f32)).astype(bf16)
                        rest[radius - 1, at_row : at_row + count, cols] = lower

    for copy in inner:
        copy.wait()

    for block in range(1, blocks + 1):
        add_up(block, True)

    for copy in edges[0] + edges[1]:
        copy.wait()

    add_up(0, False)
    add_up(blocks + 1, False)

    for side, outside in enumerate((base == 0, base + width == own_all.shape[1])):

        @pl.when(outside)
        def _():
            at = side * (blocks + 1) * LANES
            sums[:, :, at : at + LANES] = jnp.zeros(sums.shape[:2] + (LANES,), bf16)

    late[0].wait()

    for group in range(blocks // 2):
        first = group * 2 * LANES
        window = slice(first, first + 4 * LANES)
        middle = slice(first + LANES, first + 3 * LANES)
        for radius in range(1, RADII + 1):
            narrow, weights = sums[radius - 1, :, window], box_in[radius - 1]
            if radius <= FINE:
                narrow = jnp.concatenate([narrow, rest[radius - 1, :, middle]], axis=1)
                weights = jnp.concatenate([weights, weights[LANES : 3 * LANES]], axis=0)
            wide = jnp.dot(narrow, weights, preferred_element_type=f32)
            mean = wide * (1.0 / float((2 * radius + 1) ** 2))
            least[...] = mean if radius == 1 else jnp.minimum(least[...], mean)

        for half in range(2):
            start = (2 * group + half) * 2 * LANES
            even = slice(start, start + LANES)
            odd = slice(start + LANES, start + 2 * LANES)
            lanes = slice(half * LANES, (half + 1) * LANES)
            for i in range(cells):
                top, low = 2 * i * count, (2 * i + 1) * count
                pixels = pixels_of(i, start + 2 * LANES)
                bands = haar_rows(*pixels)
                shrunk = []
                for band in range(3):
                    at_row = (band * cells + i) * count
                    variance = least[at_row : at_row + count, lanes]
                    bound = jnp.maximum(variance, 4.0 * noise_power)
                    shrunk.append(bands[band] * (noise_power * inverted(bound)))
                horiz, vertic, diagon = shrunk
                both, cross = vertic + diagon, vertic - diagon
                noise = (horiz + both, horiz - both, cross - horiz, -horiz - cross)
                for at, cols, pixel, part in zip(
                    (top, top, low, low), (even, odd, even, odd), pixels, noise
                ):
                    upper, lower = halves(part.astype(bf16).astype(f32) * pixel)
                    product[at : at + count, cols] = upper
                    product[size + at : size + at + count, cols] = lower

    for copy in late[1:]:
        copy.wait()

    def fingerprints(cols, slot_slice, scale_here):
        weighted = jnp.dot(
            select_in[slot_slice, :], product[:, cols], preferred_element_type=f32
        )
        part = (weighted * scale_here[:, cols]).astype(bf16)
        return jnp.dot(part, merge_in[...], preferred_element_type=f32).astype(bf16)

    for block in range(blocks):
        cols = slice(2 * block * LANES, (2 * block + 2) * LANES)
        out[:, cols] = fingerprints(cols, slice(0, slot_rows), scale)

    @pl.when(jnp.max(most[...]) * rows > slot_rows)
    def _():
        copy = pltpu.make_async_copy(
            inverse.at[
                pl.ds(slot_rows, size - slot_rows), pl.ds(pl.multiple_of(base, width), width)
            ],
            scale_other,
            ready.at[4],
        )
        copy.start()
        copy.wait()

        @pl.loop(0, blocks)
        def _(block):
            cols = pl.ds(pl.multiple_of(block * 2 * LANES, 2 * LANES), 2 * LANES)
            other[:, cols] = fingerprints(cols, slice(slot_rows, size), scale_other)


def main_part(distance, most, own, above, below, inverse, select, box, merge, rows, pieces, slots):
    size, width_all = own.shape
    count = size // rows
    width = width_all // pieces
    halo = above.shape[0]
    cell_rows = 3 * (rows // 2) * count
    return pl.pallas_call(
        functools.partial(main_kernel, count, rows, distance),
        in_specs=[pl.BlockSpec(memory_space=pltpu.VMEM)]
        + [pl.BlockSpec(memory_space=pl.ANY)] * 7,
        out_specs=[pl.BlockSpec(memory_space=pltpu.VMEM)] * 2,
        scratch_shapes=[
            pltpu.VMEM((size, width + 4 * LANES), bf16),
            pltpu.VMEM((halo, width // 2 + 2 * LANES), bf16),
            pltpu.VMEM((halo, width // 2 + 2 * LANES), bf16),
            pltpu.VMEM((RADII, cell_rows, width // 2 + 2 * LANES), bf16),
            pltpu.VMEM((FINE, cell_rows, width // 2 + 2 * LANES), bf16),
            pltpu.VMEM((cell_rows, 2 * LANES), f32),
            pltpu.VMEM((2 * size, width), bf16),
            pltpu.VMEM((slots * rows, width), f32),
            pltpu.VMEM((size - slots * rows, width), f32),
            pltpu.VMEM((size, 2 * size), bf16),
            pltpu.VMEM((RADII, 4 * LANES, 2 * LANES), bf16),
            pltpu.VMEM((2 * LANES, 2 * LANES), bf16),
            pltpu.SemaphoreType.DMA((9,)),
            pltpu.SemaphoreType.DMA((5,)),
        ],
        out_shape=[
            jax.ShapeDtypeStruct((slots * rows, width), bf16),
            jax.ShapeDtypeStruct((size - slots * rows, width), bf16),
        ],
        compiler_params=pltpu.CompilerParams(vmem_limit_bytes=20 * 2**20),
        cost_estimate=pl.CostEstimate(
            flops=2 * 10**9, bytes_accessed=4 * 2**20, transcendentals=0
        ),
        name="residual",
    )(most, own, above, below, inverse, select, box, merge)


def assemble_kernel(rows, pieces, select, share, *refs):
    parts, others = refs[:pieces], refs[pieces:-7]
    prints, partial, flat, scaled, wide, total, sent = refs[-7:]
    width = parts[0].shape[1]
    size = parts[0].shape[0] + sum(other.shape[0] for other in others[:1])
    tall = CAMS * rows
    for place, part in enumerate(parts):
        edges = part[: 2 * rows, :].astype(f32) * share[place].reshape(2 * rows, width)
        scaled[place, : 2 * rows, :] = edges.astype(bf16)
    total[...] = jnp.zeros((tall, LANES), f32)
    copies = []
    for block in range(width // (2 * LANES)):
        cols = slice(block * 2 * LANES, (block + 1) * 2 * LANES)
        joined = jnp.zeros((tall, 2 * LANES), f32)
        for place, part in enumerate(parts):
            pieces_of = [scaled[place, :, cols], part[2 * rows :, cols]]
            if others:
                pieces_of.append(others[place][:, cols])
            source = jnp.concatenate(pieces_of, axis=0)
            joined = joined + jnp.dot(
                select[place, :, :size], source, preferred_element_type=f32
            )
        flat[:, cols] = joined.astype(bf16)
        total[...] += joined[:, :LANES] + joined[:, LANES:]
        wide[:, :, cols] = joined.reshape(CAMS, rows, 2 * LANES)
        there = pl.ds(block * 2 * LANES, 2 * LANES)
        copies.append(
            pltpu.make_async_copy(wide.at[:, :, there], prints.at[:, :, there], sent.at[block])
        )
        copies[-1].start()
    gram = lax.dot_general(
        flat[...], flat[...], (((1,), (1,)), ((), ())), preferred_element_type=f32
    )
    sub = lax.broadcasted_iota(jnp.int32, (tall, tall), 0)
    lane = lax.broadcasted_iota(jnp.int32, (tall, tall), 1)
    gram = jnp.where((sub & (rows - 1)) == (lane & (rows - 1)), gram, 0.0)
    gram = jnp.sum(gram.reshape(CAMS, rows, tall), axis=1)
    sub = lax.broadcasted_iota(jnp.int32, (tall, LANES), 0)
    lane = lax.broadcasted_iota(jnp.int32, (tall, LANES), 1)
    gather = jnp.where((sub >> log2(rows)) == lane, 1.0, 0.0).astype(f32)
    gram = jnp.dot(gram, gather, precision=lax.Precision.HIGHEST, preferred_element_type=f32)
    sums = jnp.sum(total[...], axis=1, keepdims=True)
    sums = jnp.sum(sums.reshape(CAMS, rows, 1), axis=1)
    lane = lax.broadcasted_iota(jnp.int32, (CAMS, LANES), 1)
    partial[...] = jnp.where(lane == CAMS, sums, gram)
    for copy in copies:
        copy.wait()


def assemble(select, share, parts, others, rows):
    width = parts[0].shape[1]
    tall = CAMS * rows
    vmem = pl.BlockSpec(memory_space=pltpu.VMEM)
    return pl.pallas_call(
        functools.partial(assemble_kernel, rows, len(parts)),
        in_specs=[vmem] * (2 + len(parts) + len(others)),
        out_specs=[pl.BlockSpec(memory_space=pl.ANY), vmem],
        out_shape=[
            jax.ShapeDtypeStruct((CAMS, rows, width), f32),
            jax.ShapeDtypeStruct((CAMS, LANES), f32),
        ],
        scratch_shapes=[
            pltpu.VMEM((tall, width), bf16),
            pltpu.VMEM((len(parts), 2 * rows, width), bf16),
            pltpu.VMEM((CAMS, rows, width), f32),
            pltpu.VMEM((tall, LANES), f32),
            pltpu.SemaphoreType.DMA((width // (2 * LANES),)),
        ],
        compiler_params=pltpu.CompilerParams(vmem_limit_bytes=20 * 2**20),
        cost_estimate=pl.CostEstimate(
            flops=2 * 10**9, bytes_accessed=4 * 2**20, transcendentals=0
        ),
        name="assemble",
    )(select, share, *parts, *others)


def correlate_kernel(pixels, *refs):
    parts, out = refs[:-1], refs[-1]
    whole = parts[0][...]
    for part in parts[1:]:
        whole = whole + part[...]
    gram = whole[:, :CAMS]
    mean = whole[:, CAMS : CAMS + 1] / pixels
    sub = lax.broadcasted_iota(jnp.int32, (CAMS, CAMS), 0)
    lane = lax.broadcasted_iota(jnp.int32, (CAMS, CAMS), 1)
    diagonal = sub == lane
    mean_row = jnp.sum(jnp.where(diagonal, mean, 0.0), axis=0, keepdims=True)
    covar = gram / pixels - mean * mean_row
    only = jnp.where(diagonal, covar, 0.0)
    spread = jnp.sum(only, axis=1, keepdims=True) + var_eps
    spread_row = jnp.sum(only, axis=0, keepdims=True) + var_eps
    out[...] = covar / jnp.sqrt(spread * spread_row)


def correlate(parts, pixels):
    return pl.pallas_call(
        functools.partial(correlate_kernel, pixels),
        out_shape=jax.ShapeDtypeStruct((CAMS, CAMS), f32),
        compiler_params=pltpu.CompilerParams(vmem_limit_bytes=4 * 2**20),
        name="correlate",
    )(*parts)


def exchange(array, axis, distance):
    size = lax.axis_size(axis)
    return lax.ppermute(array, axis, [(i, i ^ distance) for i in range(size)])


def summed(array, axis, distances):
    terms = [array] + [exchange(array, axis, distance) for distance in distances]
    while len(terms) > 1:
        terms = [terms[i] + terms[i + 1] for i in range(0, len(terms), 2)]
    return terms[0]


def on_device(photos, camera_id):
    count, rows, width = photos.shape
    pieces, tiles = lax.axis_size("photo"), lax.axis_size("tile")
    own, up, down, *extras = prepare(camera_id, photos, pieces)
    above = lax.ppermute(down, "tile", [(i, i + 1) for i in range(tiles - 1)])
    below = lax.ppermute(up, "tile", [(i + 1, i) for i in range(tiles - 1)])
    extras = [
        exchange(extra, "photo", distance) if distance else extra
        for distance, extra in enumerate(extras)
    ]
    inverse, select, box, merge = energies(camera_id, own, rows)

    place, share, most, most_row = blend(extras, rows, count * rows)
    few = max(2, 11 * count // 16)
    parts, others = [None] * pieces, [None] * pieces
    for distance in reversed(range(pieces)):
        part, other = main_part(
            distance, most_row, own, above, below, inverse, select, box, merge,
            rows, pieces, few,
        )
        parts[distance] = exchange(part, "photo", distance) if distance else part
        others[distance] = other

    def finish_few():
        return assemble(place, share, parts, [], rows)

    def finish_all():
        late = [
            exchange(other, "photo", distance) if distance else other
            for distance, other in enumerate(others)
        ]
        return assemble(place, share, parts, late, rows)

    prints, partial = lax.cond(most[0] > few, finish_all, finish_few)

    total = summed(partial, "tile", (1,))
    total = summed(total, "photo", range(1, pieces))
    total = summed(total, "tile", range(2, tiles, 2))
    return prints, correlate([total], float(rows * tiles * width))


def solution(mesh):
    return jax.shard_map(
        on_device,
        mesh=mesh,
        in_specs=(P("photo", "tile", None), P("photo")),
        out_specs=(P(None, "tile", "photo"), P()),
        check_vma=False,
    )
```

```python
import functools

import jax
import jax.numpy as jnp
from jax import lax
from jax.experimental import pallas as pl
from jax.experimental.pallas import tpu as pltpu
from jax.sharding import PartitionSpec as P

CAMS = 32
RADII = 4
FINE = 2
LANES = 128

noise_power = 1.0
var_eps = 1e-06

f32 = jnp.float32
bf16 = jnp.bfloat16


def log2(value):
    return value.bit_length() - 1


def indicator(condition):
    return jnp.where(condition, 1.0, 0.0).astype(bf16)


def iotas(shape):
    return (
        lax.broadcasted_iota(jnp.int32, shape, len(shape) - 2),
        lax.broadcasted_iota(jnp.int32, shape, len(shape) - 1),
    )


def row_permutation(photos, rows):
    sub, lane = iotas((photos * rows, photos * rows))
    same_row = (sub >> log2(photos)) == (lane & (rows - 1))
    same_photo = (sub & (photos - 1)) == (lane >> log2(rows))
    return indicator(same_row & same_photo)


def column_split():
    sub, lane = iotas((2 * LANES, 2 * LANES))
    return indicator(sub == 2 * (lane & (LANES - 1)) + (lane >> log2(LANES)))


def column_merge():
    sub, lane = iotas((2 * LANES, 2 * LANES))
    return indicator(lane == 2 * (sub & (LANES - 1)) + (sub >> log2(LANES)))


def box_matrix(radius):
    sub, lane = iotas((4 * LANES, 2 * LANES))
    return indicator(jnp.abs(sub - LANES - lane) <= radius)


def haar_rows(even0, odd0, even1, odd1):
    low0, low1 = even0 + odd0, even1 + odd1
    high0, high1 = even0 - odd0, even1 - odd1
    return (low0 - low1, high0 + high1, high0 - high1)


def halves(value):
    upper = value.astype(bf16)
    lower = (value - upper.astype(f32)).astype(bf16)
    return upper, lower


def inverted(value):
    guess = pl.reciprocal(value, approx=True)
    return guess * (2.0 - value * guess)


def slot_numbers(ids, count):
    ranks = [jnp.int32(0)]
    for photo in range(1, count):
        ranks.append(ranks[-1] + jnp.where(ids[photo] != ids[photo - 1], 1, 0))
    last = ranks[-1]
    slots = [jnp.where(rank == 0, 0, jnp.where(rank == last, 1, rank + 1)) for rank in ranks]
    return slots, last + 1


def prepare_kernel(ids_all, photos_all, sorted_all, near_all, far_all, *refs):
    extras = refs[:-8]
    photos, sorted_out, near_out, far_out, arrived, sent, ids, ready = refs[-8:]
    count, rows, width = photos.shape
    cells = rows // 2
    pieces = len(extras)
    step = width // pieces
    me = lax.axis_index("photo")
    odd_tile = (lax.axis_index("tile") & 1) == 1
    copies = []
    for piece in range(pieces):
        cols = pl.ds(piece * step, step)
        copies.append(
            pltpu.make_async_copy(
                photos_all.at[:, :, cols], photos.at[:, :, cols], arrived.at[piece]
            )
        )
        copies[-1].start()
    copy = pltpu.make_async_copy(ids_all, ids, ready)
    copy.start()
    perm = row_permutation(count, rows)
    split = column_split()

    for piece in range(pieces):
        copies[piece].wait()
        flat = photos[:, :, piece * step : (piece + 1) * step].reshape(count * rows, step)
        by_row = jnp.dot(perm, flat, preferred_element_type=f32).astype(bf16)
        for inner in range(step // (2 * LANES)):
            block = piece * (step // (2 * LANES)) + inner
            cols = slice(block * 2 * LANES, (block + 1) * 2 * LANES)
            cell_cols = slice(block * LANES, (block + 1) * LANES)
            pixels = by_row[:, inner * 2 * LANES : (inner + 1) * 2 * LANES]
            parted = jnp.dot(pixels, split, preferred_element_type=f32)
            sorted_out[:, cols] = parted.astype(bf16)
            edges = {}
            for i in range(cells):
                if RADII <= i < cells - RADII:
                    continue
                top = parted[2 * i * count : (2 * i + 1) * count]
                low = parted[(2 * i + 1) * count : (2 * i + 2) * count]
                bands = haar_rows(top[:, :LANES], top[:, LANES:], low[:, :LANES], low[:, LANES:])
                for band in range(3):
                    edges[band, i] = bands[band] * bands[band]
            for band in range(3):
                for i in range(RADII):
                    start = (band * RADII + i) * count
                    upper, lower = edges[band, i], edges[band, cells - RADII + i]
                    near_out[start : start + count, cell_cols] = jnp.where(
                        odd_tile, upper, lower
                    ).astype(bf16)
                    far_out[start : start + count, cell_cols] = jnp.where(
                        odd_tile, lower, upper
                    ).astype(bf16)
        for at, (local, whole) in enumerate(
            ((sorted_out, sorted_all), (near_out, near_all), (far_out, far_all))
        ):
            length = whole.shape[1] // pieces
            there = pl.ds(piece * length, length)
            copies.append(
                pltpu.make_async_copy(
                    local.at[:, there], whole.at[:, there], sent.at[at * pieces + piece]
                )
            )
            copies[-1].start()

    copy.wait()
    slots, cameras = slot_numbers(ids, count)
    sub, lane = iotas((rows, step))
    slot_id = jnp.full((rows, step), -1, jnp.int32)
    in_first, in_last = jnp.int32(0), jnp.int32(0)
    for photo in range(count):
        slot_id = jnp.where((lane >> log2(rows)) == slots[photo], ids[photo], slot_id)
        in_first = in_first + jnp.where(ids[photo] == ids[0], 1, 0)
        in_last = in_last + jnp.where(ids[photo] == ids[count - 1], 1, 0)
    notes = jnp.where(sub == 0, ids[0], jnp.where(sub == 1, ids[count - 1], slot_id))
    notes = jnp.where(sub == 3, cameras, notes).astype(f32).astype(bf16)

    none = jnp.zeros((rows, step), f32)
    for distance, extra in enumerate(extras):
        cols = pl.ds(pl.multiple_of((me ^ distance) * step, step), step)

        def add(photo, total):
            pixel = photos[photo, :, cols].astype(f32)
            return total + pixel * pixel

        extra[:rows, :] = lax.fori_loop(0, in_first, add, none).astype(bf16)
        extra[rows : 2 * rows, :] = lax.fori_loop(count - in_last, count, add, none).astype(bf16)
        extra[2 * rows :, :] = notes
    for copy_out in copies[pieces:]:
        copy_out.wait()


def prepare(ids, photos, pieces):
    count, rows, width = photos.shape
    step = width // pieces
    size = count * rows
    halo = 3 * RADII * count
    vmem = pl.BlockSpec(memory_space=pltpu.VMEM)
    return pl.pallas_call(
        prepare_kernel,
        in_specs=[pl.BlockSpec(memory_space=pl.ANY)] * 2,
        out_specs=[pl.BlockSpec(memory_space=pl.ANY)] * 3 + [vmem] * pieces,
        out_shape=[
            jax.ShapeDtypeStruct((size, width), bf16),
            jax.ShapeDtypeStruct((halo, width // 2), bf16),
            jax.ShapeDtypeStruct((halo, width // 2), bf16),
        ]
        + [jax.ShapeDtypeStruct((3 * rows, step), bf16)] * pieces,
        scratch_shapes=[
            pltpu.VMEM((count, rows, width), bf16),
            pltpu.VMEM((size, width), bf16),
            pltpu.VMEM((halo, width // 2), bf16),
            pltpu.VMEM((halo, width // 2), bf16),
            pltpu.SemaphoreType.DMA((pieces,)),
            pltpu.SemaphoreType.DMA((3 * pieces,)),
            pltpu.SMEM((count,), jnp.int32),
            pltpu.SemaphoreType.DMA(()),
        ],
        compiler_params=pltpu.CompilerParams(vmem_limit_bytes=56 * 2**20),
        cost_estimate=pl.CostEstimate(flops=10**9, bytes_accessed=8 * 2**20, transcendentals=0),
        name="prepare",
    )(ids, photos)


def energy_kernel(
    count, rows, ids_all, own, inverse, select_out, box_out, merge_out, ids, ready
):
    size, width = own.shape
    copy = pltpu.make_async_copy(ids_all, ids, ready)
    copy.start()
    for radius in range(1, RADII + 1):
        box_out[radius - 1] = box_matrix(radius)
    merge_out[...] = column_merge()
    copy.wait()
    slots, _ = slot_numbers(ids, count)
    sub, lane = iotas((size, size))
    lane_photo = lane & (count - 1)
    lane_slot = jnp.zeros_like(lane)
    for photo in range(count):
        lane_slot = jnp.where(lane_photo == photo, slots[photo], lane_slot)
    in_slot = lane_slot == (sub >> log2(rows))
    same_row = (sub & (rows - 1)) == (lane >> log2(count))
    select = indicator(in_slot & same_row)
    select = jnp.concatenate([select, select], axis=1)
    select_out[...] = select

    for block in range(width // (2 * LANES)):
        cols = slice(block * 2 * LANES, (block + 1) * 2 * LANES)
        pixel = own[:, cols].astype(f32)
        pair = jnp.concatenate(halves(pixel * pixel), axis=0)
        energy = jnp.dot(select, pair, preferred_element_type=f32)
        inverse[:, cols] = inverted(jnp.maximum(energy, 2.0**-20))


def energies(ids, own, rows):
    size, width = own.shape
    vmem = pl.BlockSpec(memory_space=pltpu.VMEM)
    return pl.pallas_call(
        functools.partial(energy_kernel, size // rows, rows),
        in_specs=[pl.BlockSpec(memory_space=pl.ANY), vmem],
        out_specs=[vmem] * 4,
        out_shape=[
            jax.ShapeDtypeStruct((size, width), f32),
            jax.ShapeDtypeStruct((size, 2 * size), bf16),
            jax.ShapeDtypeStruct((RADII, 4 * LANES, 2 * LANES), bf16),
            jax.ShapeDtypeStruct((2 * LANES, 2 * LANES), bf16),
        ],
        scratch_shapes=[pltpu.SMEM((size // rows,), jnp.int32), pltpu.SemaphoreType.DMA(())],
        compiler_params=pltpu.CompilerParams(vmem_limit_bytes=20 * 2**20),
        cost_estimate=pl.CostEstimate(flops=10**9, bytes_accessed=8 * 2**20, transcendentals=0),
        name="energies",
    )(ids, own)


def blend_kernel(rows, *refs):
    pieces = len(refs) - 5
    me = lax.axis_index("photo")
    extras, (select, share, most, most_row, held) = refs[:pieces], refs[pieces:]
    size = select.shape[2]
    tall = CAMS * rows
    sub, lane = iotas((tall, size))
    same_row = (sub & (rows - 1)) == (lane & (rows - 1))
    camera = (sub >> log2(rows)).astype(f32)
    highest = jnp.float32(0)
    for distance, extra in enumerate(extras):
        notes = extra[2 * rows :, :].astype(f32)
        highest = jnp.maximum(highest, jnp.max(notes[3:4, :LANES]))
        select[distance] = indicator((camera == notes[2:3, :size]) & same_row)
        held[me ^ distance] = extra[...].astype(f32)
    most[0] = highest.astype(jnp.int32)
    most_row[...] = jnp.full(most_row.shape, highest)
    ones = jnp.ones((rows, share.shape[3]), f32)
    for device in range(pieces):
        if device == 0:
            share[me ^ device, 0] = ones
        if device == pieces - 1:
            share[me ^ device, 1] = ones
            continue
        late = held[device, rows : 2 * rows]
        early = held[device + 1, :rows]
        crosses = held[device, 2 * rows + 1 : 2 * rows + 2] == held[device + 1, 2 * rows : 2 * rows + 1]
        joint = 1.0 / (late + early)
        share[me ^ device, 1] = jnp.where(crosses, late * joint, 1.0)
        share[me ^ (device + 1), 0] = jnp.where(crosses, early * joint, 1.0)


def blend(extras, rows, size):
    pieces, width = len(extras), extras[0].shape[1]
    vmem = pl.BlockSpec(memory_space=pltpu.VMEM)
    smem = pl.BlockSpec(memory_space=pltpu.SMEM)
    return pl.pallas_call(
        functools.partial(blend_kernel, rows),
        in_specs=[vmem] * pieces,
        out_specs=[vmem, vmem, smem, vmem],
        out_shape=[
            jax.ShapeDtypeStruct((pieces, CAMS * rows, size), bf16),
            jax.ShapeDtypeStruct((pieces, 2, rows, width), f32),
            jax.ShapeDtypeStruct((1,), jnp.int32),
            jax.ShapeDtypeStruct((8, LANES), f32),
        ],
        scratch_shapes=[pltpu.VMEM((pieces, 3 * rows, width), f32)],
        compiler_params=pltpu.CompilerParams(vmem_limit_bytes=20 * 2**20),
        name="blend",
    )(*extras)


def main_kernel(
    count, rows, distance, most, own_all, near_all, far_all, inverse, select, box, merge,
    out, other, own, halos, sums, rest, least, product, scale, scale_other, select_in, box_in, merge_in,
    arrived, ready,
):
    cells = rows // 2
    size = count * rows
    width = out.shape[1]
    blocks = width // (2 * LANES)
    slot_rows = out.shape[0]
    chunk = lax.axis_index("photo") ^ distance
    base = chunk * width
    odd_tile = lax.axis_index("tile") & 1
    above, below = halos.at[0], halos.at[1]
    inner = []
    edges = ([], [])
    for at, (whole, local, lanes) in enumerate(
        ((own_all, own, 2 * LANES), (near_all, None, LANES), (far_all, None, LANES))
    ):
        length = blocks * lanes
        start = chunk * length
        if local is None:
            local = halos.at[1 - odd_tile if at == 1 else odd_tile]
        for place, size_here, offset, group in (
            (start, length, lanes, inner),
            (jnp.maximum(start - lanes, 0), lanes, 0, edges[0]),
            (jnp.minimum(start + length, whole.shape[1] - lanes), lanes, lanes + length, edges[1]),
        ):
            index = 3 * at + (0 if group is inner else 1 if group is edges[0] else 2)
            group.append(
                pltpu.make_async_copy(
                    whole.at[:, pl.ds(pl.multiple_of(place, lanes), size_here)],
                    local.at[:, pl.ds(offset, size_here)],
                    arrived.at[index],
                )
            )
    late = [
        pltpu.make_async_copy(box, box_in, ready.at[0]),
        pltpu.make_async_copy(select, select_in, ready.at[1]),
        pltpu.make_async_copy(
            inverse.at[pl.ds(0, slot_rows), pl.ds(pl.multiple_of(base, width), width)],
            scale,
            ready.at[2],
        ),
        pltpu.make_async_copy(merge, merge_in, ready.at[3]),
    ]
    for copy in inner + edges[0] + edges[1] + late:
        copy.start()

    def pixels_of(i, start):
        top = slice(2 * i * count, (2 * i + 1) * count)
        low = slice((2 * i + 1) * count, (2 * i + 2) * count)
        even, odd = slice(start, start + LANES), slice(start + LANES, start + 2 * LANES)
        return tuple(
            own[at, cols].astype(f32)
            for at, cols in ((top, even), (top, odd), (low, even), (low, odd))
        )

    def add_up(block, fine):
        cols = slice(block * LANES, (block + 1) * LANES)
        squares = [[], [], []]
        for i in range(cells):
            bands = haar_rows(*pixels_of(i, block * 2 * LANES))
            for band in range(3):
                squares[band].append(bands[band] * bands[band])
        for band in range(3):
            first = band * RADII * count
            over, under = (
                [
                    halo[first + i * count : first + (i + 1) * count, cols].astype(f32)
                    for i in range(RADII)
                ]
                for halo in (above, below)
            )
            column = over + squares[band] + under
            for i in range(cells):
                total = column[i + RADII]
                at_row = (band * cells + i) * count
                for radius in range(1, RADII + 1):
                    total = total + (column[i + RADII - radius] + column[i + RADII + radius])
                    upper = total.astype(bf16)
                    sums[radius - 1, at_row : at_row + count, cols] = upper
                    if radius <= FINE and fine:
                        lower = (total - upper.astype(f32)).astype(bf16)
                        rest[radius - 1, at_row : at_row + count, cols] = lower

    for copy in inner:
        copy.wait()

    for block in range(1, blocks + 1):
        add_up(block, True)

    for copy in edges[0] + edges[1]:
        copy.wait()

    add_up(0, False)
    add_up(blocks + 1, False)

    for side, outside in enumerate((base == 0, base + width == own_all.shape[1])):

        @pl.when(outside)
        def _():
            at = side * (blocks + 1) * LANES
            sums[:, :, at : at + LANES] = jnp.zeros(sums.shape[:2] + (LANES,), bf16)

    late[0].wait()

    for group in range(blocks // 2):
        first = group * 2 * LANES
        window = slice(first, first + 4 * LANES)
        middle = slice(first + LANES, first + 3 * LANES)
        for radius in range(1, RADII + 1):
            narrow, weights = sums[radius - 1, :, window], box_in[radius - 1]
            if radius <= FINE:
                narrow = jnp.concatenate([narrow, rest[radius - 1, :, middle]], axis=1)
                weights = jnp.concatenate([weights, weights[LANES : 3 * LANES]], axis=0)
            wide = jnp.dot(narrow, weights, preferred_element_type=f32)
            mean = wide * (1.0 / float((2 * radius + 1) ** 2))
            least[...] = mean if radius == 1 else jnp.minimum(least[...], mean)

        for half in range(2):
            start = (2 * group + half) * 2 * LANES
            even = slice(start, start + LANES)
            odd = slice(start + LANES, start + 2 * LANES)
            lanes = slice(half * LANES, (half + 1) * LANES)
            for i in range(cells):
                top, low = 2 * i * count, (2 * i + 1) * count
                pixels = pixels_of(i, start + 2 * LANES)
                bands = haar_rows(*pixels)
                shrunk = []
                for band in range(3):
                    at_row = (band * cells + i) * count
                    variance = least[at_row : at_row + count, lanes]
                    bound = jnp.maximum(variance, 4.0 * noise_power)
                    shrunk.append(bands[band] * (noise_power * inverted(bound)))
                horiz, vertic, diagon = shrunk
                both, cross = vertic + diagon, vertic - diagon
                noise = (horiz + both, horiz - both, cross - horiz, -horiz - cross)
                for at, cols, pixel, part in zip(
                    (top, top, low, low), (even, odd, even, odd), pixels, noise
                ):
                    upper, lower = halves(part.astype(bf16).astype(f32) * pixel)
                    product[at : at + count, cols] = upper
                    product[size + at : size + at + count, cols] = lower

    for copy in late[1:]:
        copy.wait()

    def fingerprints(cols, slot_slice, scale_here):
        weighted = jnp.dot(
            select_in[slot_slice, :], product[:, cols], preferred_element_type=f32
        )
        part = (weighted * scale_here[:, cols]).astype(bf16)
        return jnp.dot(part, merge_in[...], preferred_element_type=f32).astype(bf16)

    for block in range(blocks):
        cols = slice(2 * block * LANES, (2 * block + 2) * LANES)
        out[:, cols] = fingerprints(cols, slice(0, slot_rows), scale)

    @pl.when(jnp.max(most[...]) * rows > slot_rows)
    def _():
        copy = pltpu.make_async_copy(
            inverse.at[
                pl.ds(slot_rows, size - slot_rows), pl.ds(pl.multiple_of(base, width), width)
            ],
            scale_other,
            ready.at[4],
        )
        copy.start()
        copy.wait()

        @pl.loop(0, blocks)
        def _(block):
            cols = pl.ds(pl.multiple_of(block * 2 * LANES, 2 * LANES), 2 * LANES)
            other[:, cols] = fingerprints(cols, slice(slot_rows, size), scale_other)


def main_part(distance, most, own, near, far, inverse, select, box, merge, rows, pieces, slots):
    size, width_all = own.shape
    count = size // rows
    width = width_all // pieces
    halo = near.shape[0]
    cell_rows = 3 * (rows // 2) * count
    return pl.pallas_call(
        functools.partial(main_kernel, count, rows, distance),
        in_specs=[pl.BlockSpec(memory_space=pltpu.VMEM)]
        + [pl.BlockSpec(memory_space=pl.ANY)] * 7,
        out_specs=[pl.BlockSpec(memory_space=pltpu.VMEM)] * 2,
        scratch_shapes=[
            pltpu.VMEM((size, width + 4 * LANES), bf16),
            pltpu.VMEM((2, halo, width // 2 + 2 * LANES), bf16),
            pltpu.VMEM((RADII, cell_rows, width // 2 + 2 * LANES), bf16),
            pltpu.VMEM((FINE, cell_rows, width // 2 + 2 * LANES), bf16),
            pltpu.VMEM((cell_rows, 2 * LANES), f32),
            pltpu.VMEM((2 * size, width), bf16),
            pltpu.VMEM((slots * rows, width), f32),
            pltpu.VMEM((size - slots * rows, width), f32),
            pltpu.VMEM((size, 2 * size), bf16),
            pltpu.VMEM((RADII, 4 * LANES, 2 * LANES), bf16),
            pltpu.VMEM((2 * LANES, 2 * LANES), bf16),
            pltpu.SemaphoreType.DMA((9,)),
            pltpu.SemaphoreType.DMA((5,)),
        ],
        out_shape=[
            jax.ShapeDtypeStruct((slots * rows, width), bf16),
            jax.ShapeDtypeStruct((size - slots * rows, width), bf16),
        ],
        compiler_params=pltpu.CompilerParams(vmem_limit_bytes=20 * 2**20),
        cost_estimate=pl.CostEstimate(
            flops=2 * 10**9, bytes_accessed=4 * 2**20, transcendentals=0
        ),
        name="residual",
    )(most, own, near, far, inverse, select, box, merge)


def assemble_kernel(rows, pieces, select, share, *refs):
    parts, others = refs[:pieces], refs[pieces:-7]
    prints, partial, flat, scaled, wide, total, sent = refs[-7:]
    width = parts[0].shape[1]
    size = parts[0].shape[0] + sum(other.shape[0] for other in others[:1])
    tall = CAMS * rows
    for place, part in enumerate(parts):
        edges = part[: 2 * rows, :].astype(f32) * share[place].reshape(2 * rows, width)
        scaled[place, : 2 * rows, :] = edges.astype(bf16)
    total[...] = jnp.zeros((tall, LANES), f32)
    copies = []
    for block in range(width // (2 * LANES)):
        cols = slice(block * 2 * LANES, (block + 1) * 2 * LANES)
        joined = jnp.zeros((tall, 2 * LANES), f32)
        for place, part in enumerate(parts):
            pieces_of = [scaled[place, :, cols], part[2 * rows :, cols]]
            if others:
                pieces_of.append(others[place][:, cols])
            source = jnp.concatenate(pieces_of, axis=0)
            joined = joined + jnp.dot(
                select[place, :, :size], source, preferred_element_type=f32
            )
        flat[:, cols] = joined.astype(bf16)
        total[...] += joined[:, :LANES] + joined[:, LANES:]
        wide[:, :, cols] = joined.reshape(CAMS, rows, 2 * LANES)
        there = pl.ds(block * 2 * LANES, 2 * LANES)
        copies.append(
            pltpu.make_async_copy(wide.at[:, :, there], prints.at[:, :, there], sent.at[block])
        )
        copies[-1].start()
    gram = lax.dot_general(
        flat[...], flat[...], (((1,), (1,)), ((), ())), preferred_element_type=f32
    )
    sub = lax.broadcasted_iota(jnp.int32, (tall, tall), 0)
    lane = lax.broadcasted_iota(jnp.int32, (tall, tall), 1)
    gram = jnp.where((sub & (rows - 1)) == (lane & (rows - 1)), gram, 0.0)
    gram = jnp.sum(gram.reshape(CAMS, rows, tall), axis=1)
    sub = lax.broadcasted_iota(jnp.int32, (tall, LANES), 0)
    lane = lax.broadcasted_iota(jnp.int32, (tall, LANES), 1)
    gather = jnp.where((sub >> log2(rows)) == lane, 1.0, 0.0).astype(f32)
    gram = jnp.dot(gram, gather, precision=lax.Precision.HIGHEST, preferred_element_type=f32)
    sums = jnp.sum(total[...], axis=1, keepdims=True)
    sums = jnp.sum(sums.reshape(CAMS, rows, 1), axis=1)
    lane = lax.broadcasted_iota(jnp.int32, (CAMS, LANES), 1)
    partial[...] = jnp.where(lane == CAMS, sums, gram)
    for copy in copies:
        copy.wait()


def assemble(select, share, parts, others, rows):
    width = parts[0].shape[1]
    tall = CAMS * rows
    vmem = pl.BlockSpec(memory_space=pltpu.VMEM)
    return pl.pallas_call(
        functools.partial(assemble_kernel, rows, len(parts)),
        in_specs=[vmem] * (2 + len(parts) + len(others)),
        out_specs=[pl.BlockSpec(memory_space=pl.ANY), vmem],
        out_shape=[
            jax.ShapeDtypeStruct((CAMS, rows, width), f32),
            jax.ShapeDtypeStruct((CAMS, LANES), f32),
        ],
        scratch_shapes=[
            pltpu.VMEM((tall, width), bf16),
            pltpu.VMEM((len(parts), 2 * rows, width), bf16),
            pltpu.VMEM((CAMS, rows, width), f32),
            pltpu.VMEM((tall, LANES), f32),
            pltpu.SemaphoreType.DMA((width // (2 * LANES),)),
        ],
        compiler_params=pltpu.CompilerParams(vmem_limit_bytes=20 * 2**20),
        cost_estimate=pl.CostEstimate(
            flops=2 * 10**9, bytes_accessed=4 * 2**20, transcendentals=0
        ),
        name="assemble",
    )(select, share, *parts, *others)


def correlate_kernel(pixels, *refs):
    parts, out = refs[:-1], refs[-1]
    whole = parts[0][...]
    for part in parts[1:]:
        whole = whole + part[...]
    gram = whole[:, :CAMS]
    mean = whole[:, CAMS : CAMS + 1] / pixels
    sub = lax.broadcasted_iota(jnp.int32, (CAMS, CAMS), 0)
    lane = lax.broadcasted_iota(jnp.int32, (CAMS, CAMS), 1)
    diagonal = sub == lane
    mean_row = jnp.sum(jnp.where(diagonal, mean, 0.0), axis=0, keepdims=True)
    covar = gram / pixels - mean * mean_row
    only = jnp.where(diagonal, covar, 0.0)
    spread = jnp.sum(only, axis=1, keepdims=True) + var_eps
    spread_row = jnp.sum(only, axis=0, keepdims=True) + var_eps
    out[...] = covar / jnp.sqrt(spread * spread_row)


def correlate(parts, pixels):
    return pl.pallas_call(
        functools.partial(correlate_kernel, pixels),
        out_shape=jax.ShapeDtypeStruct((CAMS, CAMS), f32),
        compiler_params=pltpu.CompilerParams(vmem_limit_bytes=4 * 2**20),
        name="correlate",
    )(*parts)


def exchange(array, axis, distance):
    size = lax.axis_size(axis)
    return lax.ppermute(array, axis, [(i, i ^ distance) for i in range(size)])


def summed(array, axis, distances):
    terms = [array] + [exchange(array, axis, distance) for distance in distances]
    while len(terms) > 1:
        terms = [terms[i] + terms[i + 1] for i in range(0, len(terms), 2)]
    return terms[0]


def on_device(photos, camera_id):
    count, rows, width = photos.shape
    pieces, tiles = lax.axis_size("photo"), lax.axis_size("tile")
    own, near, far, *extras = prepare(camera_id, photos, pieces)
    near = exchange(near, "tile", 1)
    across = [(i, i + 1) for i in range(1, tiles - 1, 2)]
    far = lax.ppermute(far, "tile", across + [(j, i) for i, j in across])
    extras = [
        exchange(extra, "photo", distance) if distance else extra
        for distance, extra in enumerate(extras)
    ]
    inverse, select, box, merge = energies(camera_id, own, rows)

    place, share, most, most_row = blend(extras, rows, count * rows)
    few = max(2, 11 * count // 16)
    parts, others = [None] * pieces, [None] * pieces
    for distance in reversed(range(pieces)):
        part, other = main_part(
            distance, most_row, own, near, far, inverse, select, box, merge,
            rows, pieces, few,
        )
        parts[distance] = exchange(part, "photo", distance) if distance else part
        others[distance] = other

    def finish_few():
        return assemble(place, share, parts, [], rows)

    def finish_all():
        late = [
            exchange(other, "photo", distance) if distance else other
            for distance, other in enumerate(others)
        ]
        return assemble(place, share, parts, late, rows)

    prints, partial = lax.cond(most[0] > few, finish_all, finish_few)

    total = summed(partial, "tile", (1,))
    total = summed(total, "photo", range(1, pieces))
    total = summed(total, "tile", range(2, tiles, 2))
    return prints, correlate([total], float(rows * tiles * width))


def solution(mesh):
    return jax.shard_map(
        on_device,
        mesh=mesh,
        in_specs=(P("photo", "tile", None), P("photo")),
        out_specs=(P(None, "tile", "photo"), P()),
        check_vma=False,
    )
```

```python
import functools

import jax
import jax.numpy as jnp
from jax import lax
from jax.experimental import pallas as pl
from jax.experimental.pallas import tpu as pltpu
from jax.sharding import PartitionSpec as P

CAMS = 32
RADII = 4
FINE = 2
LANES = 128

noise_power = 1.0
var_eps = 1e-06

f32 = jnp.float32
bf16 = jnp.bfloat16


def log2(value):
    return value.bit_length() - 1


def indicator(condition):
    return jnp.where(condition, 1.0, 0.0).astype(bf16)


def iotas(shape):
    return (
        lax.broadcasted_iota(jnp.int32, shape, len(shape) - 2),
        lax.broadcasted_iota(jnp.int32, shape, len(shape) - 1),
    )


def row_permutation(photos, rows):
    sub, lane = iotas((photos * rows, photos * rows))
    same_row = (sub >> log2(photos)) == (lane & (rows - 1))
    same_photo = (sub & (photos - 1)) == (lane >> log2(rows))
    return indicator(same_row & same_photo)


def column_split():
    sub, lane = iotas((2 * LANES, 2 * LANES))
    return indicator(sub == 2 * (lane & (LANES - 1)) + (lane >> log2(LANES)))


def column_merge():
    sub, lane = iotas((2 * LANES, 2 * LANES))
    return indicator(lane == 2 * (sub & (LANES - 1)) + (sub >> log2(LANES)))


def box_matrix(radius):
    sub, lane = iotas((4 * LANES, 2 * LANES))
    return indicator(jnp.abs(sub - LANES - lane) <= radius)


def haar_rows(even0, odd0, even1, odd1):
    low0, low1 = even0 + odd0, even1 + odd1
    high0, high1 = even0 - odd0, even1 - odd1
    return (low0 - low1, high0 + high1, high0 - high1)


def halves(value):
    upper = value.astype(bf16)
    lower = (value - upper.astype(f32)).astype(bf16)
    return upper, lower


def inverted(value):
    guess = pl.reciprocal(value, approx=True)
    return guess * (2.0 - value * guess)


def slot_numbers(ids, count):
    ranks = [jnp.int32(0)]
    for photo in range(1, count):
        ranks.append(ranks[-1] + jnp.where(ids[photo] != ids[photo - 1], 1, 0))
    last = ranks[-1]
    slots = [jnp.where(rank == 0, 0, jnp.where(rank == last, 1, rank + 1)) for rank in ranks]
    return slots, last + 1


def prepare_kernel(ids_all, photos, sorted_out, near_out, far_out, *refs):
    extras, (ids, ready) = refs[:-2], refs[-2:]
    count, rows, width = photos.shape
    cells = rows // 2
    pieces = len(extras)
    step = width // pieces
    me = lax.axis_index("photo")
    odd_tile = (lax.axis_index("tile") & 1) == 1
    copy = pltpu.make_async_copy(ids_all, ids, ready)
    copy.start()
    perm = row_permutation(count, rows)
    split = column_split()

    for piece in range(pieces):
        flat = photos[:, :, piece * step : (piece + 1) * step].reshape(count * rows, step)
        by_row = jnp.dot(perm, flat, preferred_element_type=f32).astype(bf16)
        for inner in range(step // (2 * LANES)):
            block = piece * (step // (2 * LANES)) + inner
            cols = slice(block * 2 * LANES, (block + 1) * 2 * LANES)
            cell_cols = slice(block * LANES, (block + 1) * LANES)
            pixels = by_row[:, inner * 2 * LANES : (inner + 1) * 2 * LANES]
            parted = jnp.dot(pixels, split, preferred_element_type=f32)
            sorted_out[:, cols] = parted.astype(bf16)
            edges = {}
            for i in range(cells):
                if RADII <= i < cells - RADII:
                    continue
                top = parted[2 * i * count : (2 * i + 1) * count]
                low = parted[(2 * i + 1) * count : (2 * i + 2) * count]
                bands = haar_rows(top[:, :LANES], top[:, LANES:], low[:, :LANES], low[:, LANES:])
                for band in range(3):
                    edges[band, i] = bands[band] * bands[band]
            for band in range(3):
                for i in range(RADII):
                    start = (band * RADII + i) * count
                    upper, lower = edges[band, i], edges[band, cells - RADII + i]
                    near_out[start : start + count, cell_cols] = jnp.where(
                        odd_tile, upper, lower
                    ).astype(bf16)
                    far_out[start : start + count, cell_cols] = jnp.where(
                        odd_tile, lower, upper
                    ).astype(bf16)

    copy.wait()
    slots, cameras = slot_numbers(ids, count)
    sub, lane = iotas((rows, step))
    slot_id = jnp.full((rows, step), -1, jnp.int32)
    in_first, in_last = jnp.int32(0), jnp.int32(0)
    for photo in range(count):
        slot_id = jnp.where((lane >> log2(rows)) == slots[photo], ids[photo], slot_id)
        in_first = in_first + jnp.where(ids[photo] == ids[0], 1, 0)
        in_last = in_last + jnp.where(ids[photo] == ids[count - 1], 1, 0)
    notes = jnp.where(sub == 0, ids[0], jnp.where(sub == 1, ids[count - 1], slot_id))
    notes = jnp.where(sub == 3, cameras, notes).astype(f32).astype(bf16)

    none = jnp.zeros((rows, step), f32)
    for distance, extra in enumerate(extras):
        cols = pl.ds(pl.multiple_of((me ^ distance) * step, step), step)

        def add(photo, total):
            pixel = photos[photo, :, cols].astype(f32)
            return total + pixel * pixel

        extra[:rows, :] = lax.fori_loop(0, in_first, add, none).astype(bf16)
        extra[rows : 2 * rows, :] = lax.fori_loop(count - in_last, count, add, none).astype(bf16)
        extra[2 * rows :, :] = notes


def prepare(ids, photos, pieces):
    count, rows, width = photos.shape
    step = width // pieces
    size = count * rows
    halo = 3 * RADII * count
    vmem = pl.BlockSpec(memory_space=pltpu.VMEM)
    return pl.pallas_call(
        prepare_kernel,
        in_specs=[pl.BlockSpec(memory_space=pl.ANY), vmem],
        out_specs=[vmem] * (3 + pieces),
        out_shape=[
            jax.ShapeDtypeStruct((size, width), bf16),
            jax.ShapeDtypeStruct((halo, width // 2), bf16),
            jax.ShapeDtypeStruct((halo, width // 2), bf16),
        ]
        + [jax.ShapeDtypeStruct((3 * rows, step), bf16)] * pieces,
        scratch_shapes=[
            pltpu.SMEM((count,), jnp.int32),
            pltpu.SemaphoreType.DMA(()),
        ],
        compiler_params=pltpu.CompilerParams(vmem_limit_bytes=20 * 2**20),
        cost_estimate=pl.CostEstimate(flops=10**9, bytes_accessed=8 * 2**20, transcendentals=0),
        name="prepare",
    )(ids, photos)


def energy_kernel(
    count, rows, ids_all, own, inverse, select_out, box_out, merge_out, ids, ready
):
    size, width = own.shape
    copy = pltpu.make_async_copy(ids_all, ids, ready)
    copy.start()
    for radius in range(1, RADII + 1):
        box_out[radius - 1] = box_matrix(radius)
    merge_out[...] = column_merge()
    copy.wait()
    slots, _ = slot_numbers(ids, count)
    sub, lane = iotas((size, size))
    lane_photo = lane & (count - 1)
    lane_slot = jnp.zeros_like(lane)
    for photo in range(count):
        lane_slot = jnp.where(lane_photo == photo, slots[photo], lane_slot)
    in_slot = lane_slot == (sub >> log2(rows))
    same_row = (sub & (rows - 1)) == (lane >> log2(count))
    select = indicator(in_slot & same_row)
    select = jnp.concatenate([select, select], axis=1)
    select_out[...] = select

    for block in range(width // (2 * LANES)):
        cols = slice(block * 2 * LANES, (block + 1) * 2 * LANES)
        pixel = own[:, cols].astype(f32)
        pair = jnp.concatenate(halves(pixel * pixel), axis=0)
        energy = jnp.dot(select, pair, preferred_element_type=f32)
        inverse[:, cols] = inverted(jnp.maximum(energy, 2.0**-20))


def energies(ids, own, rows):
    size, width = own.shape
    vmem = pl.BlockSpec(memory_space=pltpu.VMEM)
    return pl.pallas_call(
        functools.partial(energy_kernel, size // rows, rows),
        in_specs=[pl.BlockSpec(memory_space=pl.ANY), vmem],
        out_specs=[vmem] * 4,
        out_shape=[
            jax.ShapeDtypeStruct((size, width), f32),
            jax.ShapeDtypeStruct((size, 2 * size), bf16),
            jax.ShapeDtypeStruct((RADII, 4 * LANES, 2 * LANES), bf16),
            jax.ShapeDtypeStruct((2 * LANES, 2 * LANES), bf16),
        ],
        scratch_shapes=[pltpu.SMEM((size // rows,), jnp.int32), pltpu.SemaphoreType.DMA(())],
        compiler_params=pltpu.CompilerParams(vmem_limit_bytes=20 * 2**20),
        cost_estimate=pl.CostEstimate(flops=10**9, bytes_accessed=8 * 2**20, transcendentals=0),
        name="energies",
    )(ids, own)


def blend_kernel(rows, *refs):
    pieces = len(refs) - 5
    me = lax.axis_index("photo")
    extras, (select, share, most, most_row, held) = refs[:pieces], refs[pieces:]
    size = select.shape[2]
    tall = CAMS * rows
    sub, lane = iotas((tall, size))
    same_row = (sub & (rows - 1)) == (lane & (rows - 1))
    camera = (sub >> log2(rows)).astype(f32)
    highest = jnp.float32(0)
    for distance, extra in enumerate(extras):
        notes = extra[2 * rows :, :].astype(f32)
        highest = jnp.maximum(highest, jnp.max(notes[3:4, :LANES]))
        select[distance] = indicator((camera == notes[2:3, :size]) & same_row)
        held[me ^ distance] = extra[...].astype(f32)
    most[0] = highest.astype(jnp.int32)
    most_row[...] = jnp.full(most_row.shape, highest)
    ones = jnp.ones((rows, share.shape[3]), f32)
    for device in range(pieces):
        if device == 0:
            share[me ^ device, 0] = ones
        if device == pieces - 1:
            share[me ^ device, 1] = ones
            continue
        late = held[device, rows : 2 * rows]
        early = held[device + 1, :rows]
        crosses = held[device, 2 * rows + 1 : 2 * rows + 2] == held[device + 1, 2 * rows : 2 * rows + 1]
        joint = 1.0 / (late + early)
        share[me ^ device, 1] = jnp.where(crosses, late * joint, 1.0)
        share[me ^ (device + 1), 0] = jnp.where(crosses, early * joint, 1.0)


def blend(extras, rows, size):
    pieces, width = len(extras), extras[0].shape[1]
    vmem = pl.BlockSpec(memory_space=pltpu.VMEM)
    smem = pl.BlockSpec(memory_space=pltpu.SMEM)
    return pl.pallas_call(
        functools.partial(blend_kernel, rows),
        in_specs=[vmem] * pieces,
        out_specs=[vmem, vmem, smem, vmem],
        out_shape=[
            jax.ShapeDtypeStruct((pieces, CAMS * rows, size), bf16),
            jax.ShapeDtypeStruct((pieces, 2, rows, width), f32),
            jax.ShapeDtypeStruct((1,), jnp.int32),
            jax.ShapeDtypeStruct((8, LANES), f32),
        ],
        scratch_shapes=[pltpu.VMEM((pieces, 3 * rows, width), f32)],
        compiler_params=pltpu.CompilerParams(vmem_limit_bytes=20 * 2**20),
        name="blend",
    )(*extras)


def main_kernel(
    count, rows, distance, most, own_all, near_all, far_all, inverse, select, box, merge,
    out, other, own, halos, sums, rest, least, product, scale, scale_other, select_in, box_in, merge_in,
    arrived, ready,
):
    cells = rows // 2
    size = count * rows
    width = out.shape[1]
    blocks = width // (2 * LANES)
    slot_rows = out.shape[0]
    chunk = lax.axis_index("photo") ^ distance
    base = chunk * width
    odd_tile = lax.axis_index("tile") & 1
    above, below = halos.at[0], halos.at[1]
    inner = []
    edges = ([], [])
    for at, (whole, local, lanes) in enumerate(
        ((own_all, own, 2 * LANES), (near_all, None, LANES), (far_all, None, LANES))
    ):
        length = blocks * lanes
        start = chunk * length
        if local is None:
            local = halos.at[1 - odd_tile if at == 1 else odd_tile]
        for place, size_here, offset, group in (
            (start, length, lanes, inner),
            (jnp.maximum(start - lanes, 0), lanes, 0, edges[0]),
            (jnp.minimum(start + length, whole.shape[1] - lanes), lanes, lanes + length, edges[1]),
        ):
            index = 3 * at + (0 if group is inner else 1 if group is edges[0] else 2)
            group.append(
                pltpu.make_async_copy(
                    whole.at[:, pl.ds(pl.multiple_of(place, lanes), size_here)],
                    local.at[:, pl.ds(offset, size_here)],
                    arrived.at[index],
                )
            )
    late = [
        pltpu.make_async_copy(box, box_in, ready.at[0]),
        pltpu.make_async_copy(select, select_in, ready.at[1]),
        pltpu.make_async_copy(
            inverse.at[pl.ds(0, slot_rows), pl.ds(pl.multiple_of(base, width), width)],
            scale,
            ready.at[2],
        ),
        pltpu.make_async_copy(merge, merge_in, ready.at[3]),
    ]
    for copy in inner + edges[0] + edges[1] + late:
        copy.start()

    def pixels_of(i, start):
        top = slice(2 * i * count, (2 * i + 1) * count)
        low = slice((2 * i + 1) * count, (2 * i + 2) * count)
        even, odd = slice(start, start + LANES), slice(start + LANES, start + 2 * LANES)
        return tuple(
            own[at, cols].astype(f32)
            for at, cols in ((top, even), (top, odd), (low, even), (low, odd))
        )

    def add_up(block, fine):
        cols = slice(block * LANES, (block + 1) * LANES)
        squares = [[], [], []]
        for i in range(cells):
            bands = haar_rows(*pixels_of(i, block * 2 * LANES))
            for band in range(3):
                squares[band].append(bands[band] * bands[band])
        for band in range(3):
            first = band * RADII * count
            over, under = (
                [
                    halo[first + i * count : first + (i + 1) * count, cols].astype(f32)
                    for i in range(RADII)
                ]
                for halo in (above, below)
            )
            column = over + squares[band] + under
            for i in range(cells):
                total = column[i + RADII]
                at_row = (band * cells + i) * count
                for radius in range(1, RADII + 1):
                    total = total + (column[i + RADII - radius] + column[i + RADII + radius])
                    upper = total.astype(bf16)
                    sums[radius - 1, at_row : at_row + count, cols] = upper
                    if radius <= FINE and fine:
                        lower = (total - upper.astype(f32)).astype(bf16)
                        rest[radius - 1, at_row : at_row + count, cols] = lower

    for copy in inner:
        copy.wait()

    for block in range(1, blocks + 1):
        add_up(block, True)

    for copy in edges[0] + edges[1]:
        copy.wait()

    add_up(0, False)
    add_up(blocks + 1, False)

    for side, outside in enumerate((base == 0, base + width == own_all.shape[1])):

        @pl.when(outside)
        def _():
            at = side * (blocks + 1) * LANES
            sums[:, :, at : at + LANES] = jnp.zeros(sums.shape[:2] + (LANES,), bf16)

    late[0].wait()

    for group in range(blocks // 2):
        first = group * 2 * LANES
        window = slice(first, first + 4 * LANES)
        middle = slice(first + LANES, first + 3 * LANES)
        for radius in range(1, RADII + 1):
            narrow, weights = sums[radius - 1, :, window], box_in[radius - 1]
            if radius <= FINE:
                narrow = jnp.concatenate([narrow, rest[radius - 1, :, middle]], axis=1)
                weights = jnp.concatenate([weights, weights[LANES : 3 * LANES]], axis=0)
            wide = jnp.dot(narrow, weights, preferred_element_type=f32)
            mean = wide * (1.0 / float((2 * radius + 1) ** 2))
            least[...] = mean if radius == 1 else jnp.minimum(least[...], mean)

        for half in range(2):
            start = (2 * group + half) * 2 * LANES
            even = slice(start, start + LANES)
            odd = slice(start + LANES, start + 2 * LANES)
            lanes = slice(half * LANES, (half + 1) * LANES)
            for i in range(cells):
                top, low = 2 * i * count, (2 * i + 1) * count
                pixels = pixels_of(i, start + 2 * LANES)
                bands = haar_rows(*pixels)
                shrunk = []
                for band in range(3):
                    at_row = (band * cells + i) * count
                    variance = least[at_row : at_row + count, lanes]
                    bound = jnp.maximum(variance, 4.0 * noise_power)
                    shrunk.append(bands[band] * (noise_power * inverted(bound)))
                horiz, vertic, diagon = shrunk
                both, cross = vertic + diagon, vertic - diagon
                noise = (horiz + both, horiz - both, cross - horiz, -horiz - cross)
                for at, cols, pixel, part in zip(
                    (top, top, low, low), (even, odd, even, odd), pixels, noise
                ):
                    upper, lower = halves(part.astype(bf16).astype(f32) * pixel)
                    product[at : at + count, cols] = upper
                    product[size + at : size + at + count, cols] = lower

    for copy in late[1:]:
        copy.wait()

    def fingerprints(cols, slot_slice, scale_here):
        weighted = jnp.dot(
            select_in[slot_slice, :], product[:, cols], preferred_element_type=f32
        )
        part = (weighted * scale_here[:, cols]).astype(bf16)
        return jnp.dot(part, merge_in[...], preferred_element_type=f32).astype(bf16)

    for block in range(blocks):
        cols = slice(2 * block * LANES, (2 * block + 2) * LANES)
        out[:, cols] = fingerprints(cols, slice(0, slot_rows), scale)

    @pl.when(jnp.max(most[...]) * rows > slot_rows)
    def _():
        copy = pltpu.make_async_copy(
            inverse.at[
                pl.ds(slot_rows, size - slot_rows), pl.ds(pl.multiple_of(base, width), width)
            ],
            scale_other,
            ready.at[4],
        )
        copy.start()
        copy.wait()

        @pl.loop(0, blocks)
        def _(block):
            cols = pl.ds(pl.multiple_of(block * 2 * LANES, 2 * LANES), 2 * LANES)
            other[:, cols] = fingerprints(cols, slice(slot_rows, size), scale_other)


def main_part(distance, most, own, near, far, inverse, select, box, merge, rows, pieces, slots):
    size, width_all = own.shape
    count = size // rows
    width = width_all // pieces
    halo = near.shape[0]
    cell_rows = 3 * (rows // 2) * count
    return pl.pallas_call(
        functools.partial(main_kernel, count, rows, distance),
        in_specs=[pl.BlockSpec(memory_space=pltpu.VMEM)]
        + [pl.BlockSpec(memory_space=pl.ANY)] * 7,
        out_specs=[pl.BlockSpec(memory_space=pltpu.VMEM)] * 2,
        scratch_shapes=[
            pltpu.VMEM((size, width + 4 * LANES), bf16),
            pltpu.VMEM((2, halo, width // 2 + 2 * LANES), bf16),
            pltpu.VMEM((RADII, cell_rows, width // 2 + 2 * LANES), bf16),
            pltpu.VMEM((FINE, cell_rows, width // 2 + 2 * LANES), bf16),
            pltpu.VMEM((cell_rows, 2 * LANES), f32),
            pltpu.VMEM((2 * size, width), bf16),
            pltpu.VMEM((slots * rows, width), f32),
            pltpu.VMEM((size - slots * rows, width), f32),
            pltpu.VMEM((size, 2 * size), bf16),
            pltpu.VMEM((RADII, 4 * LANES, 2 * LANES), bf16),
            pltpu.VMEM((2 * LANES, 2 * LANES), bf16),
            pltpu.SemaphoreType.DMA((9,)),
            pltpu.SemaphoreType.DMA((5,)),
        ],
        out_shape=[
            jax.ShapeDtypeStruct((slots * rows, width), bf16),
            jax.ShapeDtypeStruct((size - slots * rows, width), bf16),
        ],
        compiler_params=pltpu.CompilerParams(vmem_limit_bytes=20 * 2**20),
        cost_estimate=pl.CostEstimate(
            flops=2 * 10**9, bytes_accessed=4 * 2**20, transcendentals=0
        ),
        name="residual",
    )(most, own, near, far, inverse, select, box, merge)


def assemble_kernel(rows, pieces, select, share, *refs):
    parts, others = refs[:pieces], refs[pieces:-7]
    prints, partial, flat, scaled, wide, total, sent = refs[-7:]
    width = parts[0].shape[1]
    size = parts[0].shape[0] + sum(other.shape[0] for other in others[:1])
    tall = CAMS * rows
    for place, part in enumerate(parts):
        edges = part[: 2 * rows, :].astype(f32) * share[place].reshape(2 * rows, width)
        scaled[place, : 2 * rows, :] = edges.astype(bf16)
    total[...] = jnp.zeros((tall, LANES), f32)
    copies = []
    for block in range(width // (2 * LANES)):
        cols = slice(block * 2 * LANES, (block + 1) * 2 * LANES)
        joined = jnp.zeros((tall, 2 * LANES), f32)
        for place, part in enumerate(parts):
            pieces_of = [scaled[place, :, cols], part[2 * rows :, cols]]
            if others:
                pieces_of.append(others[place][:, cols])
            source = jnp.concatenate(pieces_of, axis=0)
            joined = joined + jnp.dot(
                select[place, :, :size], source, preferred_element_type=f32
            )
        flat[:, cols] = joined.astype(bf16)
        total[...] += joined[:, :LANES] + joined[:, LANES:]
        wide[:, :, cols] = joined.reshape(CAMS, rows, 2 * LANES)
        there = pl.ds(block * 2 * LANES, 2 * LANES)
        copies.append(
            pltpu.make_async_copy(wide.at[:, :, there], prints.at[:, :, there], sent.at[block])
        )
        copies[-1].start()
    gram = lax.dot_general(
        flat[...], flat[...], (((1,), (1,)), ((), ())), preferred_element_type=f32
    )
    sub = lax.broadcasted_iota(jnp.int32, (tall, tall), 0)
    lane = lax.broadcasted_iota(jnp.int32, (tall, tall), 1)
    gram = jnp.where((sub & (rows - 1)) == (lane & (rows - 1)), gram, 0.0)
    gram = jnp.sum(gram.reshape(CAMS, rows, tall), axis=1)
    sub = lax.broadcasted_iota(jnp.int32, (tall, LANES), 0)
    lane = lax.broadcasted_iota(jnp.int32, (tall, LANES), 1)
    gather = jnp.where((sub >> log2(rows)) == lane, 1.0, 0.0).astype(f32)
    gram = jnp.dot(gram, gather, precision=lax.Precision.HIGHEST, preferred_element_type=f32)
    sums = jnp.sum(total[...], axis=1, keepdims=True)
    sums = jnp.sum(sums.reshape(CAMS, rows, 1), axis=1)
    lane = lax.broadcasted_iota(jnp.int32, (CAMS, LANES), 1)
    partial[...] = jnp.where(lane == CAMS, sums, gram)
    for copy in copies:
        copy.wait()


def assemble(select, share, parts, others, rows):
    width = parts[0].shape[1]
    tall = CAMS * rows
    vmem = pl.BlockSpec(memory_space=pltpu.VMEM)
    return pl.pallas_call(
        functools.partial(assemble_kernel, rows, len(parts)),
        in_specs=[vmem] * (2 + len(parts) + len(others)),
        out_specs=[pl.BlockSpec(memory_space=pl.ANY), vmem],
        out_shape=[
            jax.ShapeDtypeStruct((CAMS, rows, width), f32),
            jax.ShapeDtypeStruct((CAMS, LANES), f32),
        ],
        scratch_shapes=[
            pltpu.VMEM((tall, width), bf16),
            pltpu.VMEM((len(parts), 2 * rows, width), bf16),
            pltpu.VMEM((CAMS, rows, width), f32),
            pltpu.VMEM((tall, LANES), f32),
            pltpu.SemaphoreType.DMA((width // (2 * LANES),)),
        ],
        compiler_params=pltpu.CompilerParams(vmem_limit_bytes=20 * 2**20),
        cost_estimate=pl.CostEstimate(
            flops=2 * 10**9, bytes_accessed=4 * 2**20, transcendentals=0
        ),
        name="assemble",
    )(select, share, *parts, *others)


def correlate_kernel(pixels, *refs):
    parts, out = refs[:-1], refs[-1]
    whole = parts[0][...]
    for part in parts[1:]:
        whole = whole + part[...]
    gram = whole[:, :CAMS]
    mean = whole[:, CAMS : CAMS + 1] / pixels
    sub = lax.broadcasted_iota(jnp.int32, (CAMS, CAMS), 0)
    lane = lax.broadcasted_iota(jnp.int32, (CAMS, CAMS), 1)
    diagonal = sub == lane
    mean_row = jnp.sum(jnp.where(diagonal, mean, 0.0), axis=0, keepdims=True)
    covar = gram / pixels - mean * mean_row
    only = jnp.where(diagonal, covar, 0.0)
    spread = jnp.sum(only, axis=1, keepdims=True) + var_eps
    spread_row = jnp.sum(only, axis=0, keepdims=True) + var_eps
    out[...] = covar / jnp.sqrt(spread * spread_row)


def correlate(parts, pixels):
    return pl.pallas_call(
        functools.partial(correlate_kernel, pixels),
        out_shape=jax.ShapeDtypeStruct((CAMS, CAMS), f32),
        compiler_params=pltpu.CompilerParams(vmem_limit_bytes=4 * 2**20),
        name="correlate",
    )(*parts)


def exchange(array, axis, distance):
    size = lax.axis_size(axis)
    return lax.ppermute(array, axis, [(i, i ^ distance) for i in range(size)])


def summed(array, axis, distances):
    terms = [array] + [exchange(array, axis, distance) for distance in distances]
    while len(terms) > 1:
        terms = [terms[i] + terms[i + 1] for i in range(0, len(terms), 2)]
    return terms[0]


def on_device(photos, camera_id):
    count, rows, width = photos.shape
    pieces, tiles = lax.axis_size("photo"), lax.axis_size("tile")
    own, near, far, *extras = prepare(camera_id, photos, pieces)
    near = exchange(near, "tile", 1)
    across = [(i, i + 1) for i in range(1, tiles - 1, 2)]
    far = lax.ppermute(far, "tile", across + [(j, i) for i, j in across])
    extras = [
        exchange(extra, "photo", distance) if distance else extra
        for distance, extra in enumerate(extras)
    ]
    inverse, select, box, merge = energies(camera_id, own, rows)

    place, share, most, most_row = blend(extras, rows, count * rows)
    few = max(2, 11 * count // 16)
    parts, others = [None] * pieces, [None] * pieces
    for distance in reversed(range(pieces)):
        part, other = main_part(
            distance, most_row, own, near, far, inverse, select, box, merge,
            rows, pieces, few,
        )
        parts[distance] = exchange(part, "photo", distance) if distance else part
        others[distance] = other

    def finish_few():
        return assemble(place, share, parts, [], rows)

    def finish_all():
        late = [
            exchange(other, "photo", distance) if distance else other
            for distance, other in enumerate(others)
        ]
        return assemble(place, share, parts, late, rows)

    prints, partial = lax.cond(most[0] > few, finish_all, finish_few)

    total = summed(partial, "tile", (1,))
    total = summed(total, "photo", range(1, pieces))
    total = summed(total, "tile", range(2, tiles, 2))
    return prints, correlate([total], float(rows * tiles * width))


def solution(mesh):
    return jax.shard_map(
        on_device,
        mesh=mesh,
        in_specs=(P("photo", "tile", None), P("photo")),
        out_specs=(P(None, "tile", "photo"), P()),
        check_vma=False,
    )
```

```python
import functools

import jax
import jax.numpy as jnp
from jax import lax
from jax.experimental import pallas as pl
from jax.experimental.pallas import tpu as pltpu
from jax.sharding import PartitionSpec as P

CAMS = 32
RADII = 4
FINE = 2
LANES = 128

noise_power = 1.0
var_eps = 1e-06

f32 = jnp.float32
bf16 = jnp.bfloat16


def log2(value):
    return value.bit_length() - 1


def indicator(condition):
    return jnp.where(condition, 1.0, 0.0).astype(bf16)


def iotas(shape):
    return (
        lax.broadcasted_iota(jnp.int32, shape, len(shape) - 2),
        lax.broadcasted_iota(jnp.int32, shape, len(shape) - 1),
    )


def row_permutation(photos, rows):
    sub, lane = iotas((photos * rows, photos * rows))
    same_row = (sub >> log2(photos)) == (lane & (rows - 1))
    same_photo = (sub & (photos - 1)) == (lane >> log2(rows))
    return indicator(same_row & same_photo)


def column_split():
    sub, lane = iotas((2 * LANES, 2 * LANES))
    return indicator(sub == 2 * (lane & (LANES - 1)) + (lane >> log2(LANES)))


def column_merge():
    sub, lane = iotas((2 * LANES, 2 * LANES))
    return indicator(lane == 2 * (sub & (LANES - 1)) + (sub >> log2(LANES)))


def box_matrix(radius):
    sub, lane = iotas((4 * LANES, 2 * LANES))
    return indicator(jnp.abs(sub - LANES - lane) <= radius)


def haar_rows(even0, odd0, even1, odd1):
    low0, low1 = even0 + odd0, even1 + odd1
    high0, high1 = even0 - odd0, even1 - odd1
    return (low0 - low1, high0 + high1, high0 - high1)


def halves(value):
    upper = value.astype(bf16)
    lower = (value - upper.astype(f32)).astype(bf16)
    return upper, lower


def inverted(value):
    guess = pl.reciprocal(value, approx=True)
    return guess * (2.0 - value * guess)


def slot_numbers(ids, count):
    ranks = [jnp.int32(0)]
    for photo in range(1, count):
        ranks.append(ranks[-1] + jnp.where(ids[photo] != ids[photo - 1], 1, 0))
    last = ranks[-1]
    slots = [jnp.where(rank == 0, 0, jnp.where(rank == last, 1, rank + 1)) for rank in ranks]
    return slots, last + 1


def prepare_kernel(ids_all, photos, sorted_out, near_out, far_out, *refs):
    extras, (ids, ready) = refs[:-2], refs[-2:]
    count, rows, width = photos.shape
    cells = rows // 2
    pieces = len(extras)
    step = width // pieces
    me = lax.axis_index("photo")
    odd_tile = (lax.axis_index("tile") & 1) == 1
    copy = pltpu.make_async_copy(ids_all, ids, ready)
    copy.start()
    perm = row_permutation(count, rows)
    split = column_split()

    for piece in range(pieces):
        flat = photos[:, :, piece * step : (piece + 1) * step].reshape(count * rows, step)
        by_row = jnp.dot(perm, flat, preferred_element_type=f32).astype(bf16)
        for inner in range(step // (2 * LANES)):
            block = piece * (step // (2 * LANES)) + inner
            cols = slice(block * 2 * LANES, (block + 1) * 2 * LANES)
            cell_cols = slice(block * LANES, (block + 1) * LANES)
            pixels = by_row[:, inner * 2 * LANES : (inner + 1) * 2 * LANES]
            parted = jnp.dot(pixels, split, preferred_element_type=f32)
            sorted_out[:, cols] = parted.astype(bf16)
            edges = {}
            for i in range(cells):
                if RADII <= i < cells - RADII:
                    continue
                top = parted[2 * i * count : (2 * i + 1) * count]
                low = parted[(2 * i + 1) * count : (2 * i + 2) * count]
                bands = haar_rows(top[:, :LANES], top[:, LANES:], low[:, :LANES], low[:, LANES:])
                for band in range(3):
                    edges[band, i] = bands[band] * bands[band]
            for band in range(3):
                for i in range(RADII):
                    start = (band * RADII + i) * count
                    upper, lower = edges[band, i], edges[band, cells - RADII + i]
                    near_out[start : start + count, cell_cols] = jnp.where(
                        odd_tile, upper, lower
                    ).astype(bf16)
                    far_out[start : start + count, cell_cols] = jnp.where(
                        odd_tile, lower, upper
                    ).astype(bf16)

    copy.wait()
    slots, cameras = slot_numbers(ids, count)
    sub, lane = iotas((rows, step))
    slot_id = jnp.full((rows, step), -1, jnp.int32)
    in_first, in_last = jnp.int32(0), jnp.int32(0)
    for photo in range(count):
        slot_id = jnp.where((lane >> log2(rows)) == slots[photo], ids[photo], slot_id)
        in_first = in_first + jnp.where(ids[photo] == ids[0], 1, 0)
        in_last = in_last + jnp.where(ids[photo] == ids[count - 1], 1, 0)
    notes = jnp.where(sub == 0, ids[0], jnp.where(sub == 1, ids[count - 1], slot_id))
    notes = jnp.where(sub == 3, cameras, notes).astype(f32).astype(bf16)

    none = jnp.zeros((rows, step), f32)
    for distance, extra in enumerate(extras):
        cols = pl.ds(pl.multiple_of((me ^ distance) * step, step), step)

        def add(photo, total):
            pixel = photos[photo, :, cols].astype(f32)
            return total + pixel * pixel

        extra[:rows, :] = lax.fori_loop(0, in_first, add, none).astype(bf16)
        extra[rows : 2 * rows, :] = lax.fori_loop(count - in_last, count, add, none).astype(bf16)
        extra[2 * rows :, :] = notes


def prepare(ids, photos, pieces):
    count, rows, width = photos.shape
    step = width // pieces
    size = count * rows
    halo = 3 * RADII * count
    vmem = pl.BlockSpec(memory_space=pltpu.VMEM)
    return pl.pallas_call(
        prepare_kernel,
        in_specs=[pl.BlockSpec(memory_space=pl.ANY), vmem],
        out_specs=[vmem] * (3 + pieces),
        out_shape=[
            jax.ShapeDtypeStruct((size, width), bf16),
            jax.ShapeDtypeStruct((halo, width // 2), bf16),
            jax.ShapeDtypeStruct((halo, width // 2), bf16),
        ]
        + [jax.ShapeDtypeStruct((3 * rows, step), bf16)] * pieces,
        scratch_shapes=[
            pltpu.SMEM((count,), jnp.int32),
            pltpu.SemaphoreType.DMA(()),
        ],
        compiler_params=pltpu.CompilerParams(vmem_limit_bytes=20 * 2**20),
        cost_estimate=pl.CostEstimate(flops=10**9, bytes_accessed=8 * 2**20, transcendentals=0),
        name="prepare",
    )(ids, photos)


def energy_kernel(
    count, rows, ids_all, own, inverse, select_out, box_out, merge_out, ids, ready
):
    size, width = own.shape
    copy = pltpu.make_async_copy(ids_all, ids, ready)
    copy.start()
    for radius in range(1, RADII + 1):
        box_out[radius - 1] = box_matrix(radius)
    merge_out[...] = column_merge()
    copy.wait()
    slots, _ = slot_numbers(ids, count)
    sub, lane = iotas((size, size))
    lane_photo = lane & (count - 1)
    lane_slot = jnp.zeros_like(lane)
    for photo in range(count):
        lane_slot = jnp.where(lane_photo == photo, slots[photo], lane_slot)
    in_slot = lane_slot == (sub >> log2(rows))
    same_row = (sub & (rows - 1)) == (lane >> log2(count))
    select = indicator(in_slot & same_row)
    select = jnp.concatenate([select, select], axis=1)
    select_out[...] = select

    for block in range(width // (2 * LANES)):
        cols = slice(block * 2 * LANES, (block + 1) * 2 * LANES)
        pixel = own[:, cols].astype(f32)
        pair = jnp.concatenate(halves(pixel * pixel), axis=0)
        energy = jnp.dot(select, pair, preferred_element_type=f32)
        inverse[:, cols] = inverted(jnp.maximum(energy, 2.0**-20))


def energies(ids, own, rows):
    size, width = own.shape
    vmem = pl.BlockSpec(memory_space=pltpu.VMEM)
    return pl.pallas_call(
        functools.partial(energy_kernel, size // rows, rows),
        in_specs=[pl.BlockSpec(memory_space=pl.ANY), vmem],
        out_specs=[vmem] * 4,
        out_shape=[
            jax.ShapeDtypeStruct((size, width), f32),
            jax.ShapeDtypeStruct((size, 2 * size), bf16),
            jax.ShapeDtypeStruct((RADII, 4 * LANES, 2 * LANES), bf16),
            jax.ShapeDtypeStruct((2 * LANES, 2 * LANES), bf16),
        ],
        scratch_shapes=[pltpu.SMEM((size // rows,), jnp.int32), pltpu.SemaphoreType.DMA(())],
        compiler_params=pltpu.CompilerParams(vmem_limit_bytes=20 * 2**20),
        cost_estimate=pl.CostEstimate(flops=10**9, bytes_accessed=8 * 2**20, transcendentals=0),
        name="energies",
    )(ids, own)


def blend_kernel(rows, *refs):
    pieces = len(refs) - 5
    me = lax.axis_index("photo")
    extras, (select, share, most, most_row, held) = refs[:pieces], refs[pieces:]
    size = select.shape[2]
    tall = CAMS * rows
    sub, lane = iotas((tall, size))
    same_row = (sub & (rows - 1)) == (lane & (rows - 1))
    camera = (sub >> log2(rows)).astype(f32)
    highest = jnp.float32(0)
    for distance, extra in enumerate(extras):
        notes = extra[2 * rows :, :].astype(f32)
        highest = jnp.maximum(highest, jnp.max(notes[3:4, :LANES]))
        select[distance] = indicator((camera == notes[2:3, :size]) & same_row)
        held[me ^ distance] = extra[...].astype(f32)
    most[0] = highest.astype(jnp.int32)
    most_row[...] = jnp.full(most_row.shape, highest)
    ones = jnp.ones((rows, share.shape[3]), f32)
    for device in range(pieces):
        if device == 0:
            share[me ^ device, 0] = ones
        if device == pieces - 1:
            share[me ^ device, 1] = ones
            continue
        late = held[device, rows : 2 * rows]
        early = held[device + 1, :rows]
        crosses = held[device, 2 * rows + 1 : 2 * rows + 2] == held[device + 1, 2 * rows : 2 * rows + 1]
        joint = 1.0 / (late + early)
        share[me ^ device, 1] = jnp.where(crosses, late * joint, 1.0)
        share[me ^ (device + 1), 0] = jnp.where(crosses, early * joint, 1.0)


def blend(extras, rows, size):
    pieces, width = len(extras), extras[0].shape[1]
    vmem = pl.BlockSpec(memory_space=pltpu.VMEM)
    smem = pl.BlockSpec(memory_space=pltpu.SMEM)
    return pl.pallas_call(
        functools.partial(blend_kernel, rows),
        in_specs=[vmem] * pieces,
        out_specs=[vmem, vmem, smem, vmem],
        out_shape=[
            jax.ShapeDtypeStruct((pieces, CAMS * rows, size), bf16),
            jax.ShapeDtypeStruct((pieces, 2, rows, width), f32),
            jax.ShapeDtypeStruct((1,), jnp.int32),
            jax.ShapeDtypeStruct((8, LANES), f32),
        ],
        scratch_shapes=[pltpu.VMEM((pieces, 3 * rows, width), f32)],
        compiler_params=pltpu.CompilerParams(vmem_limit_bytes=20 * 2**20),
        name="blend",
    )(*extras)


def main_kernel(
    count, rows, distance, most, own_all, near_all, far_all, inverse, select, box, merge,
    out, other, own, halos, sums, rest, least, product, scale, scale_other, select_in, box_in, merge_in,
    arrived, ready,
):
    cells = rows // 2
    size = count * rows
    width = out.shape[1]
    blocks = width // (2 * LANES)
    slot_rows = out.shape[0]
    chunk = lax.axis_index("photo") ^ distance
    base = chunk * width
    odd_tile = lax.axis_index("tile") & 1
    above, below = halos.at[0], halos.at[1]
    inner = []
    edges = ([], [])
    for at, (whole, local, lanes) in enumerate(
        ((own_all, own, 2 * LANES), (near_all, None, LANES), (far_all, None, LANES))
    ):
        length = blocks * lanes
        start = chunk * length
        if local is None:
            local = halos.at[1 - odd_tile if at == 1 else odd_tile]
        for place, size_here, offset, group in (
            (start, length, lanes, inner),
            (jnp.maximum(start - lanes, 0), lanes, 0, edges[0]),
            (jnp.minimum(start + length, whole.shape[1] - lanes), lanes, lanes + length, edges[1]),
        ):
            index = 3 * at + (0 if group is inner else 1 if group is edges[0] else 2)
            group.append(
                pltpu.make_async_copy(
                    whole.at[:, pl.ds(pl.multiple_of(place, lanes), size_here)],
                    local.at[:, pl.ds(offset, size_here)],
                    arrived.at[index],
                )
            )
    late = [
        pltpu.make_async_copy(box, box_in, ready.at[0]),
        pltpu.make_async_copy(select, select_in, ready.at[1]),
        pltpu.make_async_copy(
            inverse.at[pl.ds(0, slot_rows), pl.ds(pl.multiple_of(base, width), width)],
            scale,
            ready.at[2],
        ),
        pltpu.make_async_copy(merge, merge_in, ready.at[3]),
    ]
    for copy in inner + edges[0] + edges[1] + late:
        copy.start()

    def pixels_of(i, start):
        top = slice(2 * i * count, (2 * i + 1) * count)
        low = slice((2 * i + 1) * count, (2 * i + 2) * count)
        even, odd = slice(start, start + LANES), slice(start + LANES, start + 2 * LANES)
        return tuple(
            own[at, cols].astype(f32)
            for at, cols in ((top, even), (top, odd), (low, even), (low, odd))
        )

    def add_up(block, fine):
        cols = slice(block * LANES, (block + 1) * LANES)
        squares = [[], [], []]
        for i in range(cells):
            bands = haar_rows(*pixels_of(i, block * 2 * LANES))
            for band in range(3):
                squares[band].append(bands[band] * bands[band])
        for band in range(3):
            first = band * RADII * count
            over, under = (
                [
                    halo[first + i * count : first + (i + 1) * count, cols].astype(f32)
                    for i in range(RADII)
                ]
                for halo in (above, below)
            )
            column = over + squares[band] + under
            for i in range(cells):
                total = column[i + RADII]
                at_row = (band * cells + i) * count
                for radius in range(1, RADII + 1):
                    total = total + (column[i + RADII - radius] + column[i + RADII + radius])
                    upper = total.astype(bf16)
                    sums[radius - 1, at_row : at_row + count, cols] = upper
                    if radius <= FINE and fine:
                        lower = (total - upper.astype(f32)).astype(bf16)
                        rest[radius - 1, at_row : at_row + count, cols] = lower

    for copy in inner:
        copy.wait()

    for block in range(1, blocks + 1):
        add_up(block, True)

    for copy in edges[0] + edges[1]:
        copy.wait()

    add_up(0, False)
    add_up(blocks + 1, False)

    for side, outside in enumerate((base == 0, base + width == own_all.shape[1])):

        @pl.when(outside)
        def _():
            at = side * (blocks + 1) * LANES
            sums[:, :, at : at + LANES] = jnp.zeros(sums.shape[:2] + (LANES,), bf16)

    late[0].wait()

    for group in range(blocks // 2):
        first = group * 2 * LANES
        window = slice(first, first + 4 * LANES)
        middle = slice(first + LANES, first + 3 * LANES)
        for radius in range(1, RADII + 1):
            narrow, weights = sums[radius - 1, :, window], box_in[radius - 1]
            if radius <= FINE:
                narrow = jnp.concatenate([narrow, rest[radius - 1, :, middle]], axis=1)
                weights = jnp.concatenate([weights, weights[LANES : 3 * LANES]], axis=0)
            wide = jnp.dot(narrow, weights, preferred_element_type=f32)
            mean = wide * (1.0 / float((2 * radius + 1) ** 2))
            least[...] = mean if radius == 1 else jnp.minimum(least[...], mean)

        for half in range(2):
            start = (2 * group + half) * 2 * LANES
            even = slice(start, start + LANES)
            odd = slice(start + LANES, start + 2 * LANES)
            lanes = slice(half * LANES, (half + 1) * LANES)
            for i in range(cells):
                top, low = 2 * i * count, (2 * i + 1) * count
                pixels = pixels_of(i, start + 2 * LANES)
                bands = haar_rows(*pixels)
                shrunk = []
                for band in range(3):
                    at_row = (band * cells + i) * count
                    variance = least[at_row : at_row + count, lanes]
                    bound = jnp.maximum(variance, 4.0 * noise_power)
                    shrunk.append(bands[band] * (noise_power * inverted(bound)))
                horiz, vertic, diagon = shrunk
                both, cross = vertic + diagon, vertic - diagon
                noise = (horiz + both, horiz - both, cross - horiz, -horiz - cross)
                for at, cols, pixel, part in zip(
                    (top, top, low, low), (even, odd, even, odd), pixels, noise
                ):
                    upper, lower = halves(part.astype(bf16).astype(f32) * pixel)
                    product[at : at + count, cols] = upper
                    product[size + at : size + at + count, cols] = lower

    for copy in late[1:]:
        copy.wait()

    def fingerprints(cols, slot_slice, scale_here):
        weighted = jnp.dot(
            select_in[slot_slice, :], product[:, cols], preferred_element_type=f32
        )
        part = (weighted * scale_here[:, cols]).astype(bf16)
        return jnp.dot(part, merge_in[...], preferred_element_type=f32).astype(bf16)

    for block in range(blocks):
        cols = slice(2 * block * LANES, (2 * block + 2) * LANES)
        out[:, cols] = fingerprints(cols, slice(0, slot_rows), scale)

    @pl.when(jnp.max(most[...]) * rows > slot_rows)
    def _():
        copy = pltpu.make_async_copy(
            inverse.at[
                pl.ds(slot_rows, size - slot_rows), pl.ds(pl.multiple_of(base, width), width)
            ],
            scale_other,
            ready.at[4],
        )
        copy.start()
        copy.wait()

        @pl.loop(0, blocks)
        def _(block):
            cols = pl.ds(pl.multiple_of(block * 2 * LANES, 2 * LANES), 2 * LANES)
            other[:, cols] = fingerprints(cols, slice(slot_rows, size), scale_other)


def main_part(distance, most, own, near, far, inverse, select, box, merge, rows, pieces, slots):
    size, width_all = own.shape
    count = size // rows
    width = width_all // pieces
    halo = near.shape[0]
    cell_rows = 3 * (rows // 2) * count
    return pl.pallas_call(
        functools.partial(main_kernel, count, rows, distance),
        in_specs=[pl.BlockSpec(memory_space=pltpu.VMEM)]
        + [pl.BlockSpec(memory_space=pl.ANY)] * 7,
        out_specs=[pl.BlockSpec(memory_space=pltpu.VMEM)] * 2,
        scratch_shapes=[
            pltpu.VMEM((size, width + 4 * LANES), bf16),
            pltpu.VMEM((2, halo, width // 2 + 2 * LANES), bf16),
            pltpu.VMEM((RADII, cell_rows, width // 2 + 2 * LANES), bf16),
            pltpu.VMEM((FINE, cell_rows, width // 2 + 2 * LANES), bf16),
            pltpu.VMEM((cell_rows, 2 * LANES), f32),
            pltpu.VMEM((2 * size, width), bf16),
            pltpu.VMEM((slots * rows, width), f32),
            pltpu.VMEM((size - slots * rows, width), f32),
            pltpu.VMEM((size, 2 * size), bf16),
            pltpu.VMEM((RADII, 4 * LANES, 2 * LANES), bf16),
            pltpu.VMEM((2 * LANES, 2 * LANES), bf16),
            pltpu.SemaphoreType.DMA((9,)),
            pltpu.SemaphoreType.DMA((5,)),
        ],
        out_shape=[
            jax.ShapeDtypeStruct((slots * rows, width), bf16),
            jax.ShapeDtypeStruct((size - slots * rows, width), bf16),
        ],
        compiler_params=pltpu.CompilerParams(vmem_limit_bytes=20 * 2**20),
        cost_estimate=pl.CostEstimate(
            flops=2 * 10**9, bytes_accessed=4 * 2**20, transcendentals=0
        ),
        name="residual",
    )(most, own, near, far, inverse, select, box, merge)


def assemble_kernel(rows, pieces, select, share, *refs):
    parts, others = refs[:pieces], refs[pieces:-7]
    prints, partial, flat, scaled, wide, total, sent = refs[-7:]
    width = parts[0].shape[1]
    tall = CAMS * rows
    for place, part in enumerate(parts):
        edges = part[: 2 * rows, :].astype(f32) * share[place].reshape(2 * rows, width)
        scaled[place, : 2 * rows, :] = edges.astype(bf16)
    total[...] = jnp.zeros((tall, LANES), f32)
    copies = []
    for block in range(width // (2 * LANES)):
        cols = slice(block * 2 * LANES, (block + 1) * 2 * LANES)
        sources = []
        for place, part in enumerate(parts):
            sources += [scaled[place, :, cols], part[2 * rows :, cols]]
            if others:
                sources.append(others[place][:, cols])
            else:
                sources.append(jnp.zeros((select.shape[2] - part.shape[0], 2 * LANES), bf16))
        joined = jnp.dot(
            jnp.concatenate([select[place] for place in range(pieces)], axis=1),
            jnp.concatenate(sources, axis=0),
            preferred_element_type=f32,
        )
        flat[:, cols] = joined.astype(bf16)
        total[...] += joined[:, :LANES] + joined[:, LANES:]
        wide[:, :, cols] = joined.reshape(CAMS, rows, 2 * LANES)
        there = pl.ds(block * 2 * LANES, 2 * LANES)
        copies.append(
            pltpu.make_async_copy(wide.at[:, :, there], prints.at[:, :, there], sent.at[block])
        )
        copies[-1].start()
    gram = lax.dot_general(
        flat[...], flat[...], (((1,), (1,)), ((), ())), preferred_element_type=f32
    )
    sub = lax.broadcasted_iota(jnp.int32, (tall, tall), 0)
    lane = lax.broadcasted_iota(jnp.int32, (tall, tall), 1)
    gram = jnp.where((sub & (rows - 1)) == (lane & (rows - 1)), gram, 0.0)
    gram = jnp.sum(gram.reshape(CAMS, rows, tall), axis=1)
    sub = lax.broadcasted_iota(jnp.int32, (tall, LANES), 0)
    lane = lax.broadcasted_iota(jnp.int32, (tall, LANES), 1)
    gather = jnp.where((sub >> log2(rows)) == lane, 1.0, 0.0).astype(f32)
    gram = jnp.dot(gram, gather, precision=lax.Precision.HIGHEST, preferred_element_type=f32)
    sums = jnp.sum(total[...], axis=1, keepdims=True)
    sums = jnp.sum(sums.reshape(CAMS, rows, 1), axis=1)
    lane = lax.broadcasted_iota(jnp.int32, (CAMS, LANES), 1)
    partial[...] = jnp.where(lane == CAMS, sums, gram)
    for copy in copies:
        copy.wait()


def assemble(select, share, parts, others, rows):
    width = parts[0].shape[1]
    tall = CAMS * rows
    vmem = pl.BlockSpec(memory_space=pltpu.VMEM)
    return pl.pallas_call(
        functools.partial(assemble_kernel, rows, len(parts)),
        in_specs=[vmem] * (2 + len(parts) + len(others)),
        out_specs=[pl.BlockSpec(memory_space=pl.ANY), vmem],
        out_shape=[
            jax.ShapeDtypeStruct((CAMS, rows, width), f32),
            jax.ShapeDtypeStruct((CAMS, LANES), f32),
        ],
        scratch_shapes=[
            pltpu.VMEM((tall, width), bf16),
            pltpu.VMEM((len(parts), 2 * rows, width), bf16),
            pltpu.VMEM((CAMS, rows, width), f32),
            pltpu.VMEM((tall, LANES), f32),
            pltpu.SemaphoreType.DMA((width // (2 * LANES),)),
        ],
        compiler_params=pltpu.CompilerParams(vmem_limit_bytes=20 * 2**20),
        cost_estimate=pl.CostEstimate(
            flops=2 * 10**9, bytes_accessed=4 * 2**20, transcendentals=0
        ),
        name="assemble",
    )(select, share, *parts, *others)


def correlate_kernel(pixels, *refs):
    parts, out = refs[:-1], refs[-1]
    whole = parts[0][...]
    for part in parts[1:]:
        whole = whole + part[...]
    gram = whole[:, :CAMS]
    mean = whole[:, CAMS : CAMS + 1] / pixels
    sub = lax.broadcasted_iota(jnp.int32, (CAMS, CAMS), 0)
    lane = lax.broadcasted_iota(jnp.int32, (CAMS, CAMS), 1)
    diagonal = sub == lane
    mean_row = jnp.sum(jnp.where(diagonal, mean, 0.0), axis=0, keepdims=True)
    covar = gram / pixels - mean * mean_row
    only = jnp.where(diagonal, covar, 0.0)
    spread = jnp.sum(only, axis=1, keepdims=True) + var_eps
    spread_row = jnp.sum(only, axis=0, keepdims=True) + var_eps
    out[...] = covar / jnp.sqrt(spread * spread_row)


def correlate(parts, pixels):
    return pl.pallas_call(
        functools.partial(correlate_kernel, pixels),
        out_shape=jax.ShapeDtypeStruct((CAMS, CAMS), f32),
        compiler_params=pltpu.CompilerParams(vmem_limit_bytes=4 * 2**20),
        name="correlate",
    )(*parts)


def exchange(array, axis, distance):
    size = lax.axis_size(axis)
    return lax.ppermute(array, axis, [(i, i ^ distance) for i in range(size)])


def summed(array, axis, distances):
    terms = [array] + [exchange(array, axis, distance) for distance in distances]
    while len(terms) > 1:
        terms = [terms[i] + terms[i + 1] for i in range(0, len(terms), 2)]
    return terms[0]


def on_device(photos, camera_id):
    count, rows, width = photos.shape
    pieces, tiles = lax.axis_size("photo"), lax.axis_size("tile")
    own, near, far, *extras = prepare(camera_id, photos, pieces)
    near = exchange(near, "tile", 1)
    across = [(i, i + 1) for i in range(1, tiles - 1, 2)]
    far = lax.ppermute(far, "tile", across + [(j, i) for i, j in across])
    extras = [
        exchange(extra, "photo", distance) if distance else extra
        for distance, extra in enumerate(extras)
    ]
    inverse, select, box, merge = energies(camera_id, own, rows)

    place, share, most, most_row = blend(extras, rows, count * rows)
    few = max(2, 11 * count // 16)
    parts, others = [None] * pieces, [None] * pieces
    for distance in reversed(range(pieces)):
        part, other = main_part(
            distance, most_row, own, near, far, inverse, select, box, merge,
            rows, pieces, few,
        )
        parts[distance] = exchange(part, "photo", distance) if distance else part
        others[distance] = other

    def finish_few():
        return assemble(place, share, parts, [], rows)

    def finish_all():
        late = [
            exchange(other, "photo", distance) if distance else other
            for distance, other in enumerate(others)
        ]
        return assemble(place, share, parts, late, rows)

    prints, partial = lax.cond(most[0] > few, finish_all, finish_few)

    total = summed(partial, "tile", (1,))
    total = summed(total, "photo", range(1, pieces))
    total = summed(total, "tile", range(2, tiles, 2))
    return prints, correlate([total], float(rows * tiles * width))


def solution(mesh):
    return jax.shard_map(
        on_device,
        mesh=mesh,
        in_specs=(P("photo", "tile", None), P("photo")),
        out_specs=(P(None, "tile", "photo"), P()),
        check_vma=False,
    )
```
